32 devices in a mesh: dp: 8 (over z, x), tensor: 4 (over y, core).
Axes of the slice: x: 2, y: 2, z: 4, core: 2. Of those that a mesh axis runs over, the one named last changes fastest.
Arguments:
- tokens: bfloat16 [32, 1024, 1024], P('dp', 'tensor'), may hold values from -6 to 6
- cotangent: bfloat16 [32, 1024, 1024], P('dp', 'tensor'), may hold values from -6 to 6
- destination: int32 [32], replicated, may hold values from 0 to 31, as said below
- lengths: int32 [32], replicated, may hold values from 128 to 1024, as said below
- adapter_of: int32 [32], replicated, may hold values from 0 to 7
- norm_gain: bfloat16 [1024], replicated, may hold values from 0.5 to 1.5
- w_zx: bfloat16 [1024, 2, 2048], P('dp', None, 'tensor'), may hold values from -0.1875 to 0.1875
- w_bc: bfloat16 [1024, 256], P('dp'), may hold values from -0.1875 to 0.1875
- w_dt: bfloat16 [1024, 32], P('dp', 'tensor'), may hold values from -0.1875 to 0.1875
- w_out: bfloat16 [1024, 2048], P('dp', 'tensor'), may hold values from -0.125 to 0.125
- conv_x: bfloat16 [5, 2048], P(None, 'tensor'), may hold values from -3 to 3
- conv_bc: bfloat16 [5, 256], replicated, may hold values from -3 to 3
- dt_bias: float32 [32], P('tensor'), may hold values from -7 to -2.5
- a_log: float32 [32], P('tensor'), may hold values from 0 to 2.77
- d_skip: float32 [32], P('tensor'), may hold values from 0.5 to 1.5
- out_gain: bfloat16 [2048], P('tensor'), may hold values from 0.5 to 1.5
- in_down: bfloat16 [1024, 128], replicated, may hold values from -0.1875 to 0.1875
- in_up: bfloat16 [128, 2, 2048], P(None, None, 'tensor'), may hold values from -1.5 to 1.5
- out_down: bfloat16 [128, 2048], replicated, may hold values from -0.125 to 0.125
- out_up: bfloat16 [128, 1024], replicated, may hold values from -1.5 to 1.5
Outputs:
- mixed: bfloat16 [32, 1024, 1024], P('dp', 'tensor')
- token_grad: bfloat16 [32, 1024, 1024], P('dp', 'tensor')
- in_down_grad: float32 [1024, 128], replicated
- in_up_grad: float32 [128, 2, 2048], P(None, None, 'tensor')
- out_down_grad: float32 [128, 2048], replicated
- out_up_grad: float32 [128, 1024], replicated
The draws below stay inside these ranges and needn't reach their ends.
Inputs may be any that keep to these rules, and one draw needn't show every extreme that they name: `destination`: input sequence 4 * g + p goes to slot 4 * ((g + o[p]) mod 8) + p, with one offset o[p] for each position p of a group, the same for all groups. `lengths`: of the 4 sequences dealt to the slots of one data-shard group, one has length 1024.
All inputs are finite; a program needn't handle non-finite values.
Results may differ from the reference program's by a relative error of at most 0.0095.
Values may be sent and summed in bfloat16 or wider, within the bound.
No kernel may reach another device: no remote copies, remote signals or barrier semaphores. Data moves between devices by JAX's collectives and lax.ppermute only.
A program may use at most 256 MiB of HBM per device.

```python
import jax
import jax.numpy as jnp
from jax import lax

D = 1024
INNER = 2048
HEADS = 32
NSTATE = 128
CONV = 4
BLOCK = 256
RANK = 16
ADAPTERS = 8
LEN = 1024
SEQ_GRP = 4
SEQS = 32
N_DP = 8


def offsets_from(key):
    return jax.random.randint(key, (SEQ_GRP,), 0, N_DP)


def slots_of(offsets):
    inputs = jnp.arange(SEQS, dtype=jnp.int32)
    group = inputs // SEQ_GRP
    place = inputs % SEQ_GRP
    return ((group + offsets[place]) % N_DP * SEQ_GRP + place).astype(jnp.int32)


def draw_destination(key, part):
    offsets = offsets_from(key)
    return slots_of(offsets)


def draw_lengths(key, part):
    offsets = offsets_from(key)
    key = jax.random.fold_in(key, 23)
    first_key, second_key = jax.random.split(key)
    slot_lengths = jax.random.randint(first_key, (SEQS,), LEN // 8, LEN + 1)
    full_place = jax.random.randint(second_key, (N_DP,), 0, SEQ_GRP)
    slots = jnp.arange(SEQS, dtype=jnp.int32)
    is_full = slots % SEQ_GRP == full_place[slots // SEQ_GRP]
    slot_lengths = jnp.where(is_full, LEN, slot_lengths)
    return slot_lengths[slots_of(offsets)].astype(jnp.int32)


def plant(entries, own_key, low, largest):
    longest = entries.shape.index(max(entries.shape))
    spots = []
    for shift in (0, 1):
        where = [jax.random.randint(jax.random.fold_in(own_key, axis), (), 0, length) for axis, length in enumerate(entries.shape)]
        where[longest] = (where[longest] + shift) % entries.shape[longest]
        spots.append(tuple(where))
    return entries.at[spots[0]].set(low).at[spots[1]].set(largest)


def block_scale(own_key, dims, shards, least, top_value):
    loudness, own = 1.0, jax.random.fold_in(own_key, 6)
    for axis_at, parts in shards:
        draws = jnp.exp(jax.random.uniform(jax.random.fold_in(own, axis_at), (parts,), jnp.float32, least / len(shards), top_value / len(shards)))
        loudness = loudness * jnp.repeat(draws, dims[axis_at] // parts).reshape([-1 if axis == axis_at else 1 for axis in range(len(dims))])
    return loudness


def bell_draw(stream_key, dims, deviation, limit, shards=(), kind=jnp.bfloat16):
    drawn = jax.random.normal(stream_key, dims, jnp.float32) * deviation
    if len(shards) > 0:
        drawn = block_scale(stream_key, dims, shards, -0.22, 0.18) * drawn
    return jnp.clip(drawn, min=-limit, max=limit).astype(kind)


def setup_inputs(seed: int = 0) -> dict:
    splits = jax.random.split(jax.random.key(seed), 21)
    tokens = bell_draw(splits[0], (SEQS, LEN, D), 1.0, 6.0, ((0, 8), (1, 4)))
    cotangent = bell_draw(splits[1], (SEQS, LEN, D), 1.0, 6.0, ((0, 8), (1, 4)))
    destination = draw_destination(jax.random.fold_in(splits[20], 71), 0)
    lengths = draw_lengths(jax.random.fold_in(splits[20], 71), 0)
    adapter_of = plant(jax.random.randint(splits[4], (SEQS,), 0, ADAPTERS), jax.random.fold_in(splits[4], 1), 0, ADAPTERS - 1).astype(jnp.int32)
    norm_gain = jnp.clip(1.0 + 0.1 * jax.random.normal(splits[5], (D,), jnp.float32), 0.5, 1.5).astype(jnp.bfloat16)
    w_zx = bell_draw(splits[6], (D, 2, INNER), D ** -0.5, 0.1875, ((0, 8), (2, 4)))
    w_bc = bell_draw(splits[7], (D, 2 * NSTATE), D ** -0.5, 0.1875, ((0, 8),))
    w_dt = bell_draw(splits[8], (D, HEADS), D ** -0.5, 0.1875, ((0, 8), (1, 4)))
    w_out = bell_draw(splits[9], (D, INNER), INNER ** -0.5, 0.125, ((0, 8), (1, 4)))
    conv_x = bell_draw(splits[10], (CONV + 1, INNER), CONV ** -0.5, 3.0, ((1, 4),))
    conv_bc = bell_draw(splits[11], (CONV + 1, 2 * NSTATE), CONV ** -0.5, 3.0)
    dt_bias = jnp.clip(-7.0 + 4.5 * jax.random.uniform(splits[12], (HEADS,), jnp.float32) ** block_scale(splits[12], (HEADS,), ((0, 4),), -0.2, 0.2), -7.0, -2.5)
    a_log = jnp.clip(2.77 * jax.random.uniform(splits[13], (HEADS,), jnp.float32) ** block_scale(splits[13], (HEADS,), ((0, 4),), -0.2, 0.2), 0.0, 2.77)
    d_skip = jnp.clip(0.5 + 1.0 * jax.random.uniform(splits[14], (HEADS,), jnp.float32) ** block_scale(splits[14], (HEADS,), ((0, 4),), -0.2, 0.2), 0.5, 1.5)
    out_gain = jnp.clip(1.0 + 0.1 * jax.random.normal(splits[15], (INNER,), jnp.float32), 0.5, 1.5).astype(jnp.bfloat16)
    in_down = bell_draw(splits[16], (D, ADAPTERS * RANK), D ** -0.5, 0.1875)
    in_up = bell_draw(splits[17], (ADAPTERS * RANK, 2, INNER), RANK ** -0.5, 1.5, ((2, 4),))
    out_down = bell_draw(splits[18], (ADAPTERS * RANK, INNER), INNER ** -0.5, 0.125)
    out_up = bell_draw(splits[19], (ADAPTERS * RANK, D), RANK ** -0.5, 1.5)
    return dict(tokens=tokens, cotangent=cotangent, destination=destination, lengths=lengths, adapter_of=adapter_of, norm_gain=norm_gain, w_zx=w_zx, w_bc=w_bc, w_dt=w_dt, w_out=w_out, conv_x=conv_x, conv_bc=conv_bc, dt_bias=dt_bias, a_log=a_log, d_skip=d_skip, out_gain=out_gain, in_down=in_down, in_up=in_up, out_down=out_down, out_up=out_up)


@jax.custom_vjp
def low(v):
    return lax.optimization_barrier(v.astype(jnp.bfloat16)).astype(jnp.float32)

@jax.custom_vjp
def low_back(v):
    return v

def low_keep(v):
    return (low(v), None)

def low_pass(kept, grad):
    return (grad,)

def back_keep(v):
    return (v, None)

def back_low(kept, grad):
    return (low(grad),)
low.defvjp(low_keep, low_pass)
low_back.defvjp(back_keep, back_low)
epsilon = 1e-05

def einsum_high(form, *operands):
    return jnp.einsum(form, *operands, precision=lax.Precision.HIGHEST)

def causal_conv(values, kernel):
    taps = kernel.shape[0] - 1
    length = values.shape[1]
    padded = jnp.pad(values, ((0, 0), (taps - 1, 0), (0, 0)))
    result = jnp.zeros_like(values) + kernel[taps]
    for offset in range(taps):
        result = result + padded[:, offset:offset + length, :] * kernel[offset]
    return result

def scan_sequence(values, steps, rate, keys_b, queries_c):
    length, heads, width = values.shape
    blocks = length // BLOCK
    value_blocks = values.reshape(blocks, BLOCK, heads, width)
    step_blocks = steps.reshape(blocks, BLOCK, heads)
    key_blocks = keys_b.reshape(blocks, BLOCK, keys_b.shape[-1])
    query_blocks = queries_c.reshape(blocks, BLOCK, queries_c.shape[-1])
    within = jnp.cumsum(step_blocks * rate, axis=1)
    lower = (jnp.arange(BLOCK)[:, None] >= jnp.arange(BLOCK)[None, :])[None, :, :, None]
    spread = within[:, :, None, :] - within[:, None, :, :]
    decay = jnp.where(lower, jnp.exp(jnp.where(lower, spread, 0.0)), 0.0)
    scores = einsum_high('ctn,csn->cts', query_blocks, key_blocks)
    weighted = value_blocks * step_blocks[..., None]
    diagonal = einsum_high('cts,ctsh,cshp->cthp', scores, decay, weighted)
    tail = jnp.exp(within[:, -1:, :] - within)
    states = einsum_high('csn,csh,cshp->chnp', key_blocks, tail, weighted)
    carry_decay = jnp.exp(within[:, -1, :])

    def advance(carry, item):
        state, factor = item
        return (factor[:, None, None] * carry + state, carry)
    start = jnp.zeros(states.shape[1:], jnp.float32)
    _, before = lax.scan(advance, start, (states, carry_decay))
    offdiag = einsum_high('ctn,chnp,cth->cthp', query_blocks, before, jnp.exp(within))
    return (diagonal + offdiag).reshape(length, heads, width)

def mix(values, steps, keys, a_log, d_skip):
    count, length, inner = values.shape
    heads = a_log.shape[0]
    split_values = values.reshape(count, length, heads, inner // heads)
    rate = -jnp.exp(a_log)

    def one_sequence(item):
        seq_values, seq_steps, seq_b, seq_c = item
        return scan_sequence(seq_values, seq_steps, rate, seq_b, seq_c)
    scanned = lax.map(jax.checkpoint(one_sequence), (split_values, steps, keys[..., :NSTATE], keys[..., NSTATE:]))
    return (scanned + d_skip[:, None] * split_values).reshape(count, length, inner)

def activate(x_part, bc_part, step_raw, conv_x, conv_bc, dt_bias):
    conv_values = jax.nn.silu(causal_conv(x_part, conv_x))
    conv_keys = jax.nn.silu(causal_conv(bc_part, conv_bc))
    steps = jax.nn.softplus(step_raw + dt_bias)
    return (conv_values, conv_keys, steps)

def layer(tokens, adapters, frozen, select, live):
    in_down, in_up, out_down, out_up = adapters
    norm_gain, w_zx, w_bc, w_dt, w_out, conv_x, conv_bc, dt_bias, a_log, d_skip, out_gain = frozen
    rms = lax.rsqrt(lax.optimization_barrier(jnp.mean(tokens * tokens, axis=-1, keepdims=True)) + epsilon)
    normed = low(tokens * rms * norm_gain)
    lowrank = low(einsum_high('bld,dr->blr', normed, in_down) * select[:, None, :])
    both = einsum_high('bld,dkc->blkc', normed, w_zx) + einsum_high('blr,rkc->blkc', lowrank, in_up)
    both = low_back(both)
    bc_part = einsum_high('bld,dn->bln', normed, w_bc)
    step_raw = einsum_high('bld,dh->blh', normed, w_dt)
    conv_values, conv_keys, steps = activate(both[:, :, 1], bc_part, step_raw, conv_x, conv_bc, dt_bias)
    scanned = mix(low(conv_values), steps, low(conv_keys), a_log, d_skip)
    gated_in = scanned * jax.nn.silu(both[:, :, 0])
    scale = lax.rsqrt(lax.optimization_barrier(jnp.mean(gated_in * gated_in, axis=-1, keepdims=True)) + epsilon)
    gated = low_back(low(gated_in * scale * out_gain))
    side = einsum_high('blc,rc->blr', gated, out_down) * select[:, None, :]
    branch = einsum_high('blc,dc->bld', gated, w_out) + einsum_high('blr,rd->bld', side, out_up)
    return live[:, :, None] * (tokens + branch)

def reference(tokens, cotangent, destination, lengths, adapter_of, norm_gain, w_zx, w_bc, w_dt, w_out, conv_x, conv_bc, dt_bias, a_log, d_skip, out_gain, in_down, in_up, out_down, out_up):
    frozen = tuple((item.astype(jnp.float32) for item in (norm_gain, w_zx, w_bc, w_dt, w_out, conv_x, conv_bc, dt_bias, a_log, d_skip, out_gain)))
    adapters = tuple((item.astype(jnp.float32) for item in (in_down, in_up, out_down, out_up)))
    count = tokens.shape[0]
    live = (jnp.arange(LEN, dtype=jnp.int32)[None, :] < lengths[:, None]).astype(jnp.float32)
    columns = jnp.arange(ADAPTERS * RANK, dtype=jnp.int32) // RANK
    select = (columns[None, :] == adapter_of[:, None]).astype(jnp.float32)
    groups = count // SEQ_GRP

    def shaped(array):
        return array.reshape((groups, SEQ_GRP) + array.shape[1:])

    def one_group(totals, item):
        block_tokens, block_cot, block_select, block_live = item

        def forward(values, *trained):
            return layer(values, trained, frozen, block_select, block_live)
        result, pull = jax.vjp(forward, block_tokens, *adapters)
        grads = pull(block_cot)
        return (tuple((total + grad for total, grad in zip(totals, grads[1:]))), (result, grads[0]))
    zeros = tuple((jnp.zeros_like(item) for item in adapters))
    totals, (results, input_grads) = lax.scan(one_group, zeros, (shaped(tokens.astype(jnp.float32)), shaped(cotangent.astype(jnp.float32)), shaped(select), shaped(live)))
    results = results.reshape(tokens.shape)
    input_grads = input_grads.reshape(tokens.shape)
    slots = jnp.zeros((count,), jnp.int32).at[destination].set(jnp.arange(count, dtype=jnp.int32))
    mixed = results[slots].astype(jnp.bfloat16)
    return (mixed, input_grads.astype(jnp.bfloat16), totals[0], totals[1], totals[2], totals[3])
```

```python
import functools

import jax
import jax.numpy as jnp
from jax import lax
from jax.experimental import pallas as pl
from jax.experimental.pallas import tpu as pltpu
from jax.sharding import PartitionSpec as P

RANK = 16
SCAN = 128
ROWS = 256
TILE = 256
HEAD = 64
EPS = 1e-05
LIMIT = 56 * 1024 * 1024

f32 = jnp.float32
bf16 = jnp.bfloat16
ANY = pl.BlockSpec(memory_space=pl.ANY)
SMEM = pl.BlockSpec(memory_space=pltpu.SMEM)


def nn(a, b):
    return lax.dot_general(a, b, (((1,), (0,)), ((), ())), preferred_element_type=f32)


def nt(a, b):
    return lax.dot_general(a, b, (((1,), (1,)), ((), ())), preferred_element_type=f32)


def tn(a, b):
    return lax.dot_general(a, b, (((0,), (0,)), ((), ())), preferred_element_type=f32)


def exact(a, b):
    return lax.dot_general(
        a, b, (((1,), (0,)), ((), ())), preferred_element_type=f32, precision=lax.Precision.HIGHEST
    )


def halves(v, axis):
    high = v.astype(bf16)
    low = (v - high.astype(f32)).astype(bf16)
    return jnp.concatenate([high, low], axis=axis)


def sigmoid(v):
    return 1.0 / (1.0 + jnp.exp(-v))


def softplus(v):
    return jnp.maximum(v, 0.0) + jnp.log1p(jnp.exp(-jnp.abs(v)))


def triangle(n, lower):
    row = lax.broadcasted_iota(jnp.int32, (n, n), 0)
    col = lax.broadcasted_iota(jnp.int32, (n, n), 1)
    return row >= col if lower else row <= col


def head_vectors(vec, parts):
    width = vec.shape[1] // parts
    total = vec[8:16, 0:128]
    for t in range(1, parts):
        total = total + vec[8:16, t * width : t * width + 128]
    return total


def split_lanes(v):
    low_lanes = lax.broadcasted_iota(jnp.int32, v.shape, 1) < HEAD
    return jnp.where(low_lanes, v, 0.0).astype(bf16), jnp.where(low_lanes, 0.0, v).astype(bf16)


class Pieces:
    def __init__(self, arrays, moves):
        self.arrays, self.moves = arrays, moves


def copy_in(info, groups, sems):
    copies = []
    for refs, moves, full in groups:
        for which, index, take, place in moves:
            src = refs[which]
            if index is not None:
                src = src.at[index]
            if take is not None:
                src = src.at[take]
            copies.append(pltpu.make_async_copy(src, place(info, full), sems.at[len(copies)]))
    for copy in copies:
        copy.start()
    for copy in copies:
        copy.wait()


def whole_block(shape):
    return pl.BlockSpec(shape, lambda c: (0,) * len(shape))


def row_block(width, rows=ROWS):
    return pl.BlockSpec((rows, width), lambda c: (c, 0))


def take_refs(refs, counts):
    taken, at = [], 0
    for count in counts:
        taken.append(refs[at : at + count])
        at += count
    return taken, refs[at:]


def scan_kernel(names, moves, counts, parts, heads, *refs):
    info, gain, in_down, convbc, spread_heads = refs[:5]
    groups, rest = take_refs(refs[5:], counts)
    (x_out, w_full, bc_full, dt_full, vec, up, normed_out, low_out, pre_out, values_out, scanned_out) = rest[:11]
    (keys_out, prebc_out, scal_out, states_out, xs, dt_wide, xbuf, bcbuf, state, sems) = rest[11:]
    fulls = dict(x=xs, w=w_full, bc=bc_full, dt=dt_wide, up=up, vec=vec)
    c = pl.program_id(0)
    inner = w_full.shape[1]
    subs = ROWS // SCAN

    @pl.when(c == 0)
    def _():
        copy_in(info, [(groups[g], m, fulls[name]) for name, g, m in zip(names, moves[0], moves[1])], sems)
        state[...] = jnp.zeros_like(state)
        xbuf[0:8, :] = jnp.zeros((8, inner), f32)
        bcbuf[0:8, :] = jnp.zeros((8, bcbuf.shape[1]), f32)
        own = heads // parts
        dt_full[...] = jnp.concatenate(
            [dt_wide[16 * t : 16 * t + 16, :].astype(f32)[:own] for t in range(parts)], axis=0
        ).astype(bf16)

    x_low = xs[pl.ds(pl.multiple_of(c * ROWS, ROWS), ROWS), :]
    x_out[...] = x_low
    x = x_low.astype(f32)
    rms = lax.rsqrt(jnp.mean(x * x, axis=1, keepdims=True) + EPS)
    normed_out[...] = (x * rms * gain[...]).astype(bf16)
    low_out[...] = nn(normed_out[...], in_down[...]).astype(bf16)
    hv = head_vectors(vec, parts)
    bias, rate = hv[0:1, 0:heads], -jnp.exp(hv[1:2, 0:heads])

    bcbuf[8:, :] = nn(normed_out[...], bc_full[...])
    pre = convbc[4:5, :] + sum(convbc[k : k + 1, :] * bcbuf[5 + k : 5 + k + ROWS, :] for k in range(4))
    bcbuf[0:8, :] = bcbuf[ROWS : ROWS + 8, :]
    prebc_out[...] = pre
    keys_out[...] = (pre * sigmoid(pre)).astype(bf16)
    nstate = keys_out.shape[1] // 2

    raw = nt(normed_out[...], dt_full[...]) + bias
    steps = softplus(raw)
    lower = triangle(SCAN, True)
    lower_f = lower.astype(f32)
    cums, cum_rows, grown, scores, key_cols = [], [], [], [], []
    for s in range(subs):
        rows = slice(s * SCAN, (s + 1) * SCAN)
        dt_s = steps[rows]
        cum = exact(lower_f, dt_s * rate)
        cums.append(cum)
        cum_rows.append(cum.T)
        b_part, c_part = keys_out[rows, 0:nstate], keys_out[rows, nstate:]
        scores.append(jnp.where(lower, nt(c_part, b_part), 0.0))
        key_cols.append(b_part.astype(f32).T.astype(bf16))
        tail = jnp.exp(cum[SCAN - 1 : SCAN, :] - cum)
        grown.append((halves(dt_s, 1), halves(jnp.exp(cum), 1), halves(dt_s * tail, 1)))
    scal_out[...] = jnp.concatenate(
        [steps, jnp.concatenate(cums, axis=0), sigmoid(raw), jnp.zeros((ROWS, 128 - 3 * heads), f32)], axis=1
    )

    for j in range(inner // TILE):
        cols = slice(j * TILE, (j + 1) * TILE)
        xbuf[8:, cols] = nn(normed_out[...], w_full[:, cols]) + nn(low_out[...], up[:, cols])
        pre = vec[4:5, cols] + sum(vec[k : k + 1, cols] * xbuf[5 + k : 5 + k + ROWS, cols] for k in range(4))
        xbuf[0:8, cols] = xbuf[ROWS : ROWS + 8, cols]
        pre_out[:, cols] = pre.astype(bf16)
        values_out[:, cols] = (pre * sigmoid(pre)).astype(bf16)
        for s in range(subs):
            rows = slice(s * SCAN, (s + 1) * SCAN)
            dtx, ecx, tlx = (nn(v, spread_heads[:, cols]) for v in grown[s])
            state_low = state[:, cols].astype(bf16)
            states_out[s, :, cols] = state_low
            v = values_out[rows, cols].astype(f32)
            y = ecx * nn(keys_out[rows, nstate:], state_low) + vec[6:7, cols] * v
            vw = v * dtx
            within = []
            for p in range(TILE // 128):
                lhs = []
                for a in range(2):
                    h = (j * TILE + p * 128) // HEAD + a
                    gap = cums[s][:, h : h + 1] - cum_rows[s][h : h + 1, :]
                    lhs.append((jnp.exp(jnp.minimum(gap, 0.0)) * scores[s]).astype(bf16))
                rhs = jnp.concatenate(split_lanes(vw[:, p * 128 : (p + 1) * 128]), axis=0)
                within.append(nn(jnp.concatenate(lhs, axis=1), rhs))
            scanned_out[rows, cols] = y + jnp.concatenate(within, axis=1)
            state[:, cols] = ecx[SCAN - 1 : SCAN, :] * state[:, cols] + nn(key_cols[s], (v * tlx).astype(bf16))


def call_scan(info, gain, in_down, convbc, spread_heads, pieces, parts, heads, length, width, inner):
    names = ("x", "w", "bc", "dt", "up", "vec")
    owners, lists, arrays, counts = [], [], [], []
    for i, name in enumerate(names):
        owners.append(i)
        lists.append(pieces[name].moves)
        arrays += pieces[name].arrays
        counts.append(len(pieces[name].arrays))
    total = sum(len(m) for m in lists)
    two_n = convbc.shape[1]
    steps, subs = length // ROWS, ROWS // SCAN
    shapes = [
        ((length, width), bf16), ((width, inner), bf16), ((width, two_n), bf16), ((heads, width), bf16),
        ((16, inner), f32), ((RANK, inner), bf16), ((length, width), bf16), ((length, RANK), bf16),
        ((length, inner), bf16), ((length, inner), bf16), ((length, inner), f32), ((length, two_n), bf16),
        ((length, two_n), f32), ((length, 128), f32), ((length // SCAN, two_n // 2, inner), bf16),
    ]
    specs = [
        row_block(width), whole_block((width, inner)), whole_block((width, two_n)), whole_block((heads, width)),
        whole_block((16, inner)), whole_block((RANK, inner)), row_block(width), row_block(RANK),
        row_block(inner), row_block(inner), row_block(inner), row_block(two_n),
        row_block(two_n), row_block(128), pl.BlockSpec((subs, two_n // 2, inner), lambda c: (c, 0, 0)),
    ]
    return pl.pallas_call(
        functools.partial(scan_kernel, names, (owners, lists), counts, parts, heads),
        grid=(steps,),
        in_specs=[SMEM, whole_block(gain.shape), whole_block(in_down.shape), whole_block(convbc.shape)]
        + [whole_block(spread_heads.shape)] + [ANY] * len(arrays),
        out_shape=[jax.ShapeDtypeStruct(s, d) for s, d in shapes],
        out_specs=specs,
        scratch_shapes=[
            pltpu.VMEM((length, width), bf16), pltpu.VMEM((parts * 16, width), bf16),
            pltpu.VMEM((ROWS + 8, inner), f32), pltpu.VMEM((ROWS + 8, two_n), f32),
            pltpu.VMEM((two_n // 2, inner), f32), pltpu.SemaphoreType.DMA((total,)),
        ],
        compiler_params=pltpu.CompilerParams(vmem_limit_bytes=LIMIT, dimension_semantics=("arbitrary",)),
    )(info, gain, in_down, convbc, spread_heads, *arrays)


def gate_kernel(names, moves, counts, *refs):
    info, normed, low, scanned, x, vec, head_sum, out_down, out_up = refs[:9]
    groups, rest = take_refs(refs[9:], counts)
    (mixed_out, dlayer_out, dy_out, dot_out, back_out, low_back_out, in_up_out, out_down_out, out_up_out) = rest[:9]
    (wz, wo, upz, cots, z, gi, gated, gg, zg, sems) = rest[9:]
    fulls = dict(z=wz, o=wo, up=upz, cot=cots)
    c = pl.program_id(0)
    inner = wz.shape[1]
    tiles = [slice(j * TILE, (j + 1) * TILE) for j in range(inner // TILE)]

    @pl.when(c == 0)
    def _():
        copy_in(info, [(groups[g], m, fulls[name]) for name, g, m in zip(names, moves[0], moves[1])], sems)
        in_up_out[...] = jnp.zeros_like(in_up_out)
        out_down_out[...] = jnp.zeros_like(out_down_out)
        out_up_out[...] = jnp.zeros_like(out_up_out)

    squares = jnp.zeros((ROWS, TILE), f32)
    for cols in tiles:
        zj = nn(normed[...], wz[:, cols]) + nn(low[...], upz[:, cols])
        z[:, cols] = zj
        g = scanned[:, cols] * (zj * sigmoid(zj))
        gi[:, cols] = g
        squares = squares + g * g
    scale = lax.rsqrt(jnp.sum(squares, axis=1, keepdims=True) / inner + EPS)
    for cols in tiles:
        gated[:, cols] = (gi[:, cols] * scale * vec[5:6, cols]).astype(bf16)
    side = nt(gated[...], out_down[...]).astype(bf16)
    terms = nt(gated[...], wo[...]) + nn(side, out_up[...])
    rows = lax.broadcasted_iota(jnp.int32, (ROWS, 1), 0) + c * ROWS
    live = rows < info[0]
    mixed_out[...] = jnp.where(live, x[...].astype(f32) + terms, 0.0).astype(bf16)
    cot = cots[pl.ds(pl.multiple_of(c * ROWS, ROWS), ROWS), :]
    dlayer_out[...] = jnp.where(live, cot.astype(f32), 0.0).astype(bf16)
    side_grad = nt(dlayer_out[...], out_up[...]).astype(bf16)
    inner_dot = jnp.zeros((ROWS, TILE), f32)
    for cols in tiles:
        grad = (nn(dlayer_out[...], wo[:, cols]) + nn(side_grad, out_down[:, cols])).astype(bf16)
        gg[:, cols] = grad
        inner_dot = inner_dot + grad.astype(f32) * vec[5:6, cols] * gi[:, cols]
    factor = scale * scale * scale * (jnp.sum(inner_dot, axis=1, keepdims=True) / inner)
    dots = jnp.zeros((ROWS, head_sum.shape[1]), f32)
    for cols in tiles:
        grad = scale * (gg[:, cols].astype(f32) * vec[5:6, cols]) - gi[:, cols] * factor
        zj = z[:, cols]
        sig = sigmoid(zj)
        sc = scanned[:, cols]
        dy = (grad * (zj * sig)).astype(bf16)
        dy_out[:, cols] = dy
        zg[:, cols] = (grad * sc * (sig * (1.0 + zj * (1.0 - sig)))).astype(bf16)
        summer = head_sum[cols, :]
        dots = dots + nn(halves(dy.astype(f32) * sc, 1), jnp.concatenate([summer, summer], axis=0))
    dot_out[...] = dots
    back_out[...] = nt(zg[...], wz[...])
    low_back_out[...] = nt(zg[...], upz[...])
    in_up_out[...] += tn(low[...], zg[...])
    out_down_out[...] += tn(side_grad, gated[...])
    out_up_out[...] += tn(side, dlayer_out[...])


def call_gate(info, normed, low, scanned, x, vec, head_sum, out_down, out_up, pieces):
    names = ("z", "o", "up", "cot")
    owners, lists, arrays, counts = [], [], [], []
    for i, name in enumerate(names):
        owners.append(i)
        lists.append(pieces[name].moves)
        arrays += pieces[name].arrays
        counts.append(len(pieces[name].arrays))
    total = sum(len(m) for m in lists)
    length, width = x.shape
    inner, heads = head_sum.shape
    shapes = [
        ((length, width), bf16), ((length, width), bf16), ((length, inner), bf16), ((length, heads), f32),
        ((length, width), f32), ((length, RANK), f32), ((RANK, inner), f32), ((RANK, inner), f32),
        ((RANK, width), f32),
    ]
    specs = [
        row_block(width), row_block(width), row_block(inner), row_block(heads), row_block(width), row_block(RANK),
        whole_block((RANK, inner)), whole_block((RANK, inner)), whole_block((RANK, width)),
    ]
    return pl.pallas_call(
        functools.partial(gate_kernel, names, (owners, lists), counts),
        grid=(length // ROWS,),
        in_specs=[SMEM, row_block(width), row_block(RANK), row_block(inner), row_block(width), whole_block(vec.shape)]
        + [whole_block(head_sum.shape), whole_block(out_down.shape), whole_block(out_up.shape)] + [ANY] * len(arrays),
        out_shape=[jax.ShapeDtypeStruct(s, d) for s, d in shapes],
        out_specs=specs,
        scratch_shapes=[
            pltpu.VMEM((width, inner), bf16), pltpu.VMEM((width, inner), bf16), pltpu.VMEM((RANK, inner), bf16),
            pltpu.VMEM((length, width), bf16), pltpu.VMEM((ROWS, inner), f32), pltpu.VMEM((ROWS, inner), f32),
            pltpu.VMEM((ROWS, inner), bf16), pltpu.VMEM((ROWS, inner), bf16), pltpu.VMEM((ROWS, inner), bf16),
            pltpu.SemaphoreType.DMA((total,)),
        ],
        compiler_params=pltpu.CompilerParams(vmem_limit_bytes=LIMIT, dimension_semantics=("arbitrary",)),
    )(info, normed, low, scanned, x, vec, head_sum, out_down, out_up, *arrays)


def back_kernel(parts, heads, *refs):
    (x, normed, low, dlayer, dy, values, pre, keys, prebc, scal, states, dot, back, low_back) = refs[:14]
    (w_full, bc_full, dt_full, vec, up, gain, in_down, convbc, spread_heads, head_sum) = refs[14:24]
    (grad_out, in_up_out, in_down_out, dstate, xbuf, bcbuf, xg, summed) = refs[24:]
    i = pl.program_id(0)
    inner = w_full.shape[1]
    subs = ROWS // SCAN
    nstate = keys.shape[1] // 2
    tiles = [slice(j * TILE, (j + 1) * TILE) for j in range(inner // TILE)]

    @pl.when(i == 0)
    def _():
        dstate[...] = jnp.zeros_like(dstate)
        xbuf[ROWS:, :] = jnp.zeros((8, inner), f32)
        bcbuf[ROWS:, :] = jnp.zeros((8, bcbuf.shape[1]), f32)
        summed[...] = jnp.zeros_like(summed)
        in_up_out[...] = jnp.zeros_like(in_up_out)
        in_down_out[...] = jnp.zeros_like(in_down_out)

    hv = head_vectors(vec, parts)
    rate = -jnp.exp(hv[1:2, 0:heads])
    upper = triangle(SCAN, False)
    upper_f = upper.astype(f32)
    raw_parts = [None] * subs
    for s in reversed(range(subs)):
        rows = slice(s * SCAN, (s + 1) * SCAN)
        steps, cum = scal[rows, 0:heads], scal[rows, heads : 2 * heads]
        cum_row = cum.T
        last = cum[SCAN - 1 : SCAN, :]
        dt2, ecum2, tail2 = halves(steps, 1), halves(jnp.exp(cum), 1), halves(jnp.exp(last - cum), 1)
        b_part, c_part = keys[rows, 0:nstate], keys[rows, nstate:]
        c_cols = c_part.astype(f32).T.astype(bf16)
        scores = jnp.where(upper, nt(b_part, c_part), 0.0)
        pulled = jnp.zeros((SCAN, SCAN), f32)
        c_grad = jnp.zeros((SCAN, nstate), f32)
        b_grad = jnp.zeros((SCAN, nstate), f32)
        direct = jnp.zeros((SCAN, heads), f32)
        through = jnp.zeros((SCAN, heads), f32)
        for j, cols in enumerate(tiles):
            dtx, ecx, tlx = (nn(v, spread_heads[:, cols]) for v in (dt2, ecum2, tail2))
            g_low = dy[rows, cols]
            g = g_low.astype(f32)
            v = values[rows, cols].astype(f32)
            vw = v * dtx
            dstate_low = dstate[:, cols].astype(bf16)
            within = []
            for p in range(TILE // 128):
                part = slice(p * 128, (p + 1) * 128)
                vw_split = split_lanes(vw[:, part])
                lhs = []
                for a in range(2):
                    h = (j * TILE + p * 128) // HEAD + a
                    gap = cum_row[h : h + 1, :] - cum[:, h : h + 1]
                    decay = jnp.exp(jnp.minimum(gap, 0.0))
                    pulled = pulled + decay * nt(vw_split[a], g_low[:, part])
                    lhs.append((decay * scores).astype(bf16))
                rhs = jnp.concatenate(split_lanes(g[:, part]), axis=0)
                within.append(nn(jnp.concatenate(lhs, axis=1), rhs))
            dvw = jnp.concatenate(within, axis=1) + tlx * nn(b_part, dstate_low)
            vg = dtx * dvw + vec[6:7, cols] * g
            summer = head_sum[cols, :]
            summer = jnp.concatenate([summer, summer], axis=0)
            direct = direct + nn(halves(v * dvw, 1), summer)
            through = through + nn(halves(v * vg, 1), summer)
            ge = (ecx * g).astype(bf16)
            c_grad = c_grad + nt(ge, states[s, :, cols])
            b_grad = b_grad + nt((tlx * vw).astype(bf16), dstate_low)
            dstate[:, cols] = ecx[SCAN - 1 : SCAN, :] * dstate[:, cols] + nn(c_cols, ge)
            pv = pre[rows, cols].astype(f32)
            sig = sigmoid(pv)
            xbuf[rows, cols] = vg * (sig * (1.0 + pv * (1.0 - sig)))
        pulled = jnp.where(upper, pulled, 0.0)
        b_grad = b_grad + nn(pulled.astype(bf16), c_part)
        c_grad = c_grad + nn(pulled.T.astype(bf16), b_part)
        pb = prebc[rows, :]
        sig = sigmoid(pb)
        bcbuf[rows, :] = jnp.concatenate([b_grad, c_grad], axis=1) * (sig * (1.0 + pb * (1.0 - sig)))
        change = dot[rows, :] - through
        later = exact(upper_f, change) + summed[0:1, 0:heads]
        summed[0:1, 0:heads] = later[0:1, :]
        raw_parts[s] = (direct + rate * later) * scal[rows, 2 * heads : 3 * heads]
    raw_grad = jnp.concatenate(raw_parts, axis=0).astype(bf16)

    for cols in tiles:
        xg[:, cols] = sum(vec[k : k + 1, cols] * xbuf[3 - k : 3 - k + ROWS, cols] for k in range(4)).astype(bf16)
    xbuf[ROWS:, :] = xbuf[0:8, :]
    bc_grad = sum(convbc[k : k + 1, :] * bcbuf[3 - k : 3 - k + ROWS, :] for k in range(4)).astype(bf16)
    bcbuf[ROWS:, :] = bcbuf[0:8, :]
    low_grad = (low_back[...] + nt(xg[...], up[...])).astype(bf16)
    in_up_out[...] += tn(low[...], xg[...])
    in_down_out[...] += tn(low_grad, normed[...])
    ng = back[...] + nt(xg[...], w_full[...]) + nt(bc_grad, bc_full[...])
    ng = ng + nn(raw_grad, dt_full[...]) + nt(low_grad, in_down[...])
    xv = x[...].astype(f32)
    rms = lax.rsqrt(jnp.mean(xv * xv, axis=1, keepdims=True) + EPS)
    ng = ng * gain[...]
    inner_norm = jnp.mean(ng * xv, axis=1, keepdims=True)
    grad_out[...] = (dlayer[...].astype(f32) + rms * ng - xv * (rms * rms * rms * inner_norm)).astype(bf16)


def call_back(rows_in, consts, parts, heads):
    x, w_full = rows_in[0], consts[0]
    length, width = x.shape
    inner = w_full.shape[1]
    two_n = rows_in[7].shape[1]
    steps, subs = length // ROWS, ROWS // SCAN

    def spec(a):
        if a.ndim == 3:
            return pl.BlockSpec((subs,) + a.shape[1:], lambda i: (steps - 1 - i, 0, 0))
        return pl.BlockSpec((ROWS, a.shape[1]), lambda i: (steps - 1 - i, 0))

    return pl.pallas_call(
        functools.partial(back_kernel, parts, heads),
        grid=(steps,),
        in_specs=[spec(a) for a in rows_in] + [whole_block(a.shape) for a in consts],
        out_shape=[
            jax.ShapeDtypeStruct((length, width), bf16),
            jax.ShapeDtypeStruct((RANK, inner), f32),
            jax.ShapeDtypeStruct((RANK, width), f32),
        ],
        out_specs=[spec(x), whole_block((RANK, inner)), whole_block((RANK, width))],
        scratch_shapes=[
            pltpu.VMEM((two_n // 2, inner), f32), pltpu.VMEM((ROWS + 8, inner), f32),
            pltpu.VMEM((ROWS + 8, two_n), f32), pltpu.VMEM((ROWS, inner), bf16), pltpu.VMEM((8, 128), f32),
        ],
        compiler_params=pltpu.CompilerParams(vmem_limit_bytes=LIMIT, dimension_semantics=("arbitrary",)),
    )(*rows_in, *consts)


def moved(block, axis, route):
    size = lax.axis_size(axis)
    return lax.ppermute(block, axis, [(i, route(i, size)) for i in range(size)])


def near(axis):
    return [lambda block: moved(block, axis, lambda i, n: i ^ 1)]


def far(axis):
    return [
        functools.partial(lambda k, block: moved(block, axis, lambda i, n: (i + 2 * k) % n), k)
        for k in range(1, lax.axis_size(axis) // 2)
    ]


def spread(block, order):
    stages = dict(z=far("dp"), x=near("dp"), y=far("tensor"), c=near("tensor"))
    held, labels = block[None], [dict(z=0, x=0, y=0, c=0)]
    for at, name in enumerate(order):
        got = [move(held) for move in stages[name]]
        lists = [labels] + [[dict(label, **{name: k + 1}) for label in labels] for k in range(len(got))]
        if at == len(order) - 1:
            return [held] + got, lists
        held = jnp.concatenate([held] + got, axis=0)
        labels = sum(lists, [])
    return None


def index_table(length_of, groups, parts, group, rank):
    dp_from = [((group ^ kx) - 2 * kz) % groups for kz in range(groups // 2) for kx in range(2)]
    part_from = [((rank ^ kc) - 2 * ky) % parts for ky in range(parts // 2) for kc in range(2)]
    partner = [rank ^ k for k in range(parts)]
    return jnp.stack([length_of] + dp_from + part_from + partner).astype(jnp.int32)


def placed(gathered, groups, take, place):
    arrays, lists = gathered
    moves = []
    for which, labels in enumerate(lists):
        for index, label in enumerate(labels):
            g_at = 1 + label["z"] * 2 + label["x"]
            t_at = 1 + groups + label["y"] * 2 + label["c"]
            moves.append((which, index, take, functools.partial(
                lambda g_at, t_at, info, full: place(info[g_at], info[t_at], full), g_at, t_at)))
    return Pieces(list(arrays), moves)


def paired(arrays, groups, parts, index, place):
    moves = [
        (k, index, None, functools.partial(lambda at, info, full: place(info[at], full), 1 + groups + parts + k))
        for k in range(parts)
    ]
    return Pieces(list(arrays), moves)


def single(array):
    return Pieces([array], [(0, None, None, lambda info, full: full)])


def span(index, size):
    return pl.ds(pl.multiple_of(index * size, size), size)


def exchanged(blocks):
    return [
        block if k == 0 else moved(block, "tensor", functools.partial(lambda k, i, n: i ^ k, k))
        for k, block in enumerate(blocks)
    ]


def dealt(block, offset, group):
    groups = lax.axis_size("dp")
    odd = offset % 2 == 1
    block = jnp.where(odd, moved(block, "dp", lambda i, n: i ^ 1), block)
    hops = offset // 2 + jnp.where(odd & (group % 2 == 0), 1, 0)
    for level in range((groups // 2 - 1).bit_length()):
        arrived = moved(block, "dp", functools.partial(lambda step, i, n: (i + step) % n, 2 << level))
        block = jnp.where(hops >> level & 1 == 1, arrived, block)
    return block


def on_device(
    tokens, cotangent, destination, lengths, adapter_of, norm_gain, w_zx, w_bc, w_dt, w_out,
    conv_x, conv_bc, dt_bias, a_log, d_skip, out_gain, in_down, in_up, out_down, out_up,
):
    groups, parts = lax.axis_size("dp"), lax.axis_size("tensor")
    group, rank = lax.axis_index("dp"), lax.axis_index("tensor")
    seq_grp, part_len, width = tokens.shape
    rows, _, cols = w_zx.shape
    own_heads = w_dt.shape[1]
    length, inner, heads = part_len * parts, cols * parts, own_heads * parts
    places = jnp.arange(seq_grp, dtype=jnp.int32)
    offsets = destination[:seq_grp] // seq_grp
    mine = group * seq_grp + rank
    adapter = adapter_of[mine] * RANK
    info = index_table(lengths[mine], groups, parts, group, rank)

    def rows_of(array):
        return exchanged([lax.dynamic_index_in_dim(array, rank ^ k, 0, keepdims=False) for k in range(parts)])

    def row_place(t, full):
        return full.at[span(t, part_len), :]

    x_pieces = paired(rows_of(tokens), groups, parts, None, row_place)

    own_vec = jnp.concatenate(
        [conv_x.astype(f32), out_gain.astype(f32)[None], jnp.repeat(d_skip, cols // own_heads)[None], jnp.zeros((1, cols), f32)]
    )
    own_heads_vec = lax.dynamic_update_slice(
        jnp.zeros((8, cols), f32), jnp.stack([dt_bias, a_log]), (0, rank * own_heads)
    )
    own_vec = jnp.concatenate([own_vec, own_heads_vec])

    def col_place(t, full):
        return full.at[:, span(t, cols)]

    vec_pieces = paired(exchanged([own_vec] * parts), groups, parts, None, col_place)
    ups = []
    for k in range(parts):
        theirs = adapter_of[group * seq_grp + (rank ^ k)] * RANK
        ups.append(lax.dynamic_slice_in_dim(in_up, theirs, RANK, 0).transpose(1, 0, 2))
    ups = exchanged(ups)
    up_x, up_z = (paired(ups, groups, parts, k, col_place) for k in (1, 0))

    order = ("z", "x", "y", "c")

    def block_place(g, t, full):
        return full.at[span(g, rows), span(t, cols)]

    x_weights = placed(spread(w_zx[:, 1], order), groups, None, block_place)
    share = rows // parts
    if share % 16 == 0 and rows % 128 == 0:
        own_bc = lax.dynamic_slice_in_dim(w_bc, rank * share, share, 0)
        own_dt = jnp.zeros((16, w_bc.shape[1]), bf16).at[:own_heads, :rows].set(w_dt.T)
        small = spread(jnp.concatenate([own_bc, own_dt]), order)
        bc_weights = placed(
            small, groups, (pl.ds(0, share),), lambda g, t, full: full.at[span(g * parts + t, share), :]
        )
        dt_weights = placed(
            small, groups, (pl.ds(share, 16), pl.ds(0, rows)), lambda g, t, full: full.at[span(t, 16), span(g, rows)]
        )
        dt_weights.arrays = bc_weights.arrays
    else:
        bc_weights = single(lax.all_gather(w_bc, "dp", axis=0, tiled=True))
        all_dt = lax.all_gather(lax.all_gather(w_dt, "dp", axis=0, tiled=True), "tensor", axis=0)
        all_dt = jnp.pad(all_dt.transpose(0, 2, 1), ((0, 0), (0, 16 - own_heads), (0, 0)))
        dt_weights = single(all_dt.reshape(parts * 16, width))
    rest = spread(jnp.concatenate([w_zx[:, 0], w_out]), order)
    z_weights = placed(rest, groups, (pl.ds(0, rows),), block_place)
    o_weights = placed(rest, groups, (pl.ds(rows, rows),), block_place)

    down_in = lax.dynamic_slice_in_dim(in_down, adapter, RANK, 1)
    down_out = lax.dynamic_slice_in_dim(out_down, adapter, RANK, 0)
    up_out = lax.dynamic_slice_in_dim(out_up, adapter, RANK, 0)
    gain = norm_gain.astype(f32)[None]
    convbc = jnp.pad(conv_bc.astype(f32), ((0, 3), (0, 0)))
    head_of = jnp.arange(inner) // (inner // heads)
    spread_heads = (jnp.arange(2 * heads)[:, None] % heads == head_of[None, :]).astype(bf16)
    head_sum = (head_of[:, None] == jnp.arange(heads)[None, :]).astype(bf16)

    (x, w_full, bc_full, dt_full, vec, up, normed, low, pre, values, scanned, keys, prebc, scal, states) = call_scan(
        info, gain, down_in, convbc, spread_heads,
        dict(x=x_pieces, w=x_weights, bc=bc_weights, dt=dt_weights, up=up_x, vec=vec_pieces),
        parts, heads, length, width, inner,
    )
    cot_pieces = paired(rows_of(cotangent), groups, parts, None, row_place)
    (mixed_rows, dlayer, dy, dot, back, low_back, up_z_grad, out_down_part, out_up_part) = call_gate(
        info, normed, low, scanned, x, vec, head_sum, down_out, up_out,
        dict(z=z_weights, o=o_weights, up=up_z, cot=cot_pieces),
    )

    def returned(array):
        return exchanged([lax.dynamic_slice_in_dim(array, (rank ^ k) * part_len, part_len, 0) for k in range(parts)])

    def stacked(blocks):
        result = jnp.zeros((parts,) + blocks[0].shape, blocks[0].dtype)
        for k, block in enumerate(blocks):
            result = lax.dynamic_update_index_in_dim(result, block, rank ^ k, 0)
        return result

    mixed = stacked([dealt(block, offsets[rank ^ k], group) for k, block in enumerate(returned(mixed_rows))])

    def at_adapter(part):
        return lax.dynamic_update_slice_in_dim(
            jnp.zeros((in_down.shape[1], part.shape[1]), bf16), part.astype(bf16), adapter, 0
        )

    early = lax.psum(at_adapter(jnp.concatenate([out_down_part, out_up_part], axis=1)), ("dp", "tensor"))
    early = early.astype(f32)

    token_rows, up_x_grad, in_down_part = call_back(
        (x, normed, low, dlayer, dy, values, pre, keys, prebc, scal, states, dot, back, low_back),
        (w_full, bc_full, dt_full, vec, up, gain, down_in, convbc, spread_heads, head_sum), parts, heads,
    )
    token_grad = stacked(returned(token_rows))
    in_up_part = at_adapter(jnp.concatenate([up_z_grad, up_x_grad], axis=1)).reshape(-1, 2, inner)
    in_up_grad = lax.psum_scatter(in_up_part, "tensor", scatter_dimension=2, tiled=True)
    in_up_grad = lax.psum(in_up_grad, "dp").astype(f32)
    in_down_grad = lax.psum(at_adapter(in_down_part), ("dp", "tensor")).astype(f32).T
    return (mixed, token_grad, in_down_grad, in_up_grad, early[:, :inner], early[:, inner:])


def solution(mesh):
    return jax.shard_map(
        on_device,
        mesh=mesh,
        in_specs=(
            P("dp", "tensor", None), P("dp", "tensor", None), P(), P(), P(), P(),
            P("dp", None, "tensor"), P("dp", None), P("dp", "tensor"), P("dp", "tensor"),
            P(None, "tensor"), P(), P("tensor"), P("tensor"), P("tensor"), P("tensor"),
            P(), P(None, None, "tensor"), P(), P(),
        ),
        out_specs=(
            P("dp", "tensor", None), P("dp", "tensor", None), P(), P(None, None, "tensor"), P(), P(),
        ),
        check_vma=False,
    )
```

```python
import functools

import jax
import jax.numpy as jnp
from jax import lax
from jax.experimental import pallas as pl
from jax.experimental.pallas import tpu as pltpu
from jax.sharding import PartitionSpec as P

RANK = 16
SCAN = 128
ROWS = 256
TILE = 512
HEAD = 64
EPS = 1e-05
LIMIT = 58 * 1024 * 1024

f32 = jnp.float32
bf16 = jnp.bfloat16
ANY = pl.BlockSpec(memory_space=pl.ANY)
SMEM = pl.BlockSpec(memory_space=pltpu.SMEM)


def nn(a, b):
    return lax.dot_general(a, b, (((1,), (0,)), ((), ())), preferred_element_type=f32)


def nt(a, b):
    return lax.dot_general(a, b, (((1,), (1,)), ((), ())), preferred_element_type=f32)


def tn(a, b):
    return lax.dot_general(a, b, (((0,), (0,)), ((), ())), preferred_element_type=f32)


def exact(a, b):
    return lax.dot_general(
        a, b, (((1,), (0,)), ((), ())), preferred_element_type=f32, precision=lax.Precision.HIGHEST
    )


def halves(v, axis):
    high = v.astype(bf16)
    low = (v - high.astype(f32)).astype(bf16)
    return jnp.concatenate([high, low], axis=axis)


def sigmoid(v):
    return 1.0 / (1.0 + jnp.exp(-v))


def softplus(v):
    return jnp.maximum(v, 0.0) + jnp.log1p(jnp.exp(-jnp.abs(v)))


def triangle(n, lower):
    row = lax.broadcasted_iota(jnp.int32, (n, n), 0)
    col = lax.broadcasted_iota(jnp.int32, (n, n), 1)
    return row >= col if lower else row <= col


def head_vectors(vec, parts):
    width = vec.shape[1] // parts
    total = vec[8:16, 0:128]
    for t in range(1, parts):
        total = total + vec[8:16, t * width : t * width + 128]
    return total


def split_lanes(v):
    low_lanes = lax.broadcasted_iota(jnp.int32, v.shape, 1) < HEAD
    return jnp.where(low_lanes, v, 0.0).astype(bf16), jnp.where(low_lanes, 0.0, v).astype(bf16)


class Pieces:
    def __init__(self, arrays, moves):
        self.arrays, self.moves = arrays, moves


def copy_in(info, groups, sems):
    copies = []
    for refs, moves, full in groups:
        for which, index, take, place in moves:
            src = refs[which]
            if index is not None:
                src = src.at[index]
            if take is not None:
                src = src.at[take]
            copies.append(pltpu.make_async_copy(src, place(info, full), sems.at[len(copies)]))
    for copy in copies:
        copy.start()
    for copy in copies:
        copy.wait()


def whole_block(shape):
    return pl.BlockSpec(shape, lambda c: (0,) * len(shape))


def row_block(width, rows=ROWS):
    return pl.BlockSpec((rows, width), lambda c: (c, 0))


def take_refs(refs, counts):
    taken, at = [], 0
    for count in counts:
        taken.append(refs[at : at + count])
        at += count
    return taken, refs[at:]


def gathered_operands(names, pieces):
    owners, lists, arrays, counts = [], [], [], []
    for i, name in enumerate(names):
        owners.append(i if pieces[name].arrays else owners[-1])
        lists.append(pieces[name].moves)
        arrays += pieces[name].arrays
        counts.append(len(pieces[name].arrays))
    return (owners, lists), arrays, counts, sum(len(m) for m in lists)


def cost(micros):
    return pl.CostEstimate(flops=int(micros * 1.1e9), bytes_accessed=1 << 20, transcendentals=0)


def scan_kernel(names, moves, counts, parts, heads, *refs):
    info, gain, in_down, convbc, spread_heads = refs[:5]
    groups, rest = take_refs(refs[5:], counts)
    (x_out, w_full, bc_full, dt_full, vec, up, normed_out, low_out, pre_out, values_out, scanned_out) = rest[:11]
    (keys_out, prebc_out, scal_out, states_out, xs, dt_wide, xbuf, bcbuf, state, sems) = rest[11:]
    fulls = dict(x=xs, w=w_full, bc=bc_full, dt=dt_wide, vec=vec)
    c = pl.program_id(0)
    inner = w_full.shape[1]
    subs = ROWS // SCAN

    @pl.when(c == 0)
    def _():
        copy_in(info, [(groups[g], m, fulls[name]) for name, g, m in zip(names, moves[0], moves[1])], sems)
        state[...] = jnp.zeros_like(state)
        xbuf[0:8, :] = jnp.zeros((8, inner), f32)
        bcbuf[0:8, :] = jnp.zeros((8, bcbuf.shape[1]), f32)
        up[...] = vec[16 : 16 + RANK, :].astype(bf16)
        own = heads // parts
        dt_full[...] = jnp.concatenate(
            [dt_wide[16 * t : 16 * t + 16, :].astype(f32)[:own] for t in range(parts)], axis=0
        ).astype(bf16)

    x_low = xs[pl.ds(pl.multiple_of(c * ROWS, ROWS), ROWS), :]
    x_out[...] = x_low
    x = x_low.astype(f32)
    rms = lax.rsqrt(jnp.mean(x * x, axis=1, keepdims=True) + EPS)
    normed_out[...] = (x * rms * gain[...]).astype(bf16)
    low_out[...] = nn(normed_out[...], in_down[...]).astype(bf16)
    hv = head_vectors(vec, parts)
    bias, rate = hv[0:1, 0:heads], -jnp.exp(hv[1:2, 0:heads])

    bcbuf[8:, :] = nn(normed_out[...], bc_full[...])
    pre = convbc[4:5, :] + sum(convbc[k : k + 1, :] * bcbuf[5 + k : 5 + k + ROWS, :] for k in range(4))
    bcbuf[0:8, :] = bcbuf[ROWS : ROWS + 8, :]
    prebc_out[...] = pre
    keys_out[...] = (pre * sigmoid(pre)).astype(bf16)
    nstate = keys_out.shape[1] // 2

    raw = nt(normed_out[...], dt_full[...]) + bias
    steps = softplus(raw)
    lower = triangle(SCAN, True)
    lower_f = lower.astype(f32)
    cums, cum_rows, grown, scores, key_cols = [], [], [], [], []
    for s in range(subs):
        rows = slice(s * SCAN, (s + 1) * SCAN)
        dt_s = steps[rows]
        cum = exact(lower_f, dt_s * rate)
        cums.append(cum)
        cum_rows.append(cum.T)
        b_part, c_part = keys_out[rows, 0:nstate], keys_out[rows, nstate:]
        scores.append(jnp.where(lower, nt(c_part, b_part), 0.0))
        key_cols.append(b_part.astype(f32).T.astype(bf16))
        tail = jnp.exp(cum[SCAN - 1 : SCAN, :] - cum)
        grown.append((halves(dt_s, 1), halves(jnp.exp(cum), 1), halves(dt_s * tail, 1)))
    scal_out[...] = jnp.concatenate(
        [steps, jnp.concatenate(cums, axis=0), sigmoid(raw), jnp.zeros((ROWS, 128 - 3 * heads), f32)], axis=1
    )

    for j in range(inner // TILE):
        cols = slice(j * TILE, (j + 1) * TILE)
        xbuf[8:, cols] = nn(normed_out[...], w_full[:, cols]) + nn(low_out[...], up[:, cols])
        pre = vec[4:5, cols] + sum(vec[k : k + 1, cols] * xbuf[5 + k : 5 + k + ROWS, cols] for k in range(4))
        xbuf[0:8, cols] = xbuf[ROWS : ROWS + 8, cols]
        pre_out[:, cols] = pre.astype(bf16)
        values_out[:, cols] = (pre * sigmoid(pre)).astype(bf16)
        for s in range(subs):
            rows = slice(s * SCAN, (s + 1) * SCAN)
            dtx, ecx, tlx = (nn(v, spread_heads[:, cols]) for v in grown[s])
            state_low = state[:, cols].astype(bf16)
            states_out[s, :, cols] = state_low
            v = values_out[rows, cols].astype(f32)
            y = ecx * nn(keys_out[rows, nstate:], state_low) + vec[6:7, cols] * v
            vw = v * dtx
            within = []
            for p in range(TILE // 128):
                lhs = []
                for a in range(2):
                    h = (j * TILE + p * 128) // HEAD + a
                    gap = cums[s][:, h : h + 1] - cum_rows[s][h : h + 1, :]
                    lhs.append((jnp.exp(jnp.minimum(gap, 0.0)) * scores[s]).astype(bf16))
                rhs = jnp.concatenate(split_lanes(vw[:, p * 128 : (p + 1) * 128]), axis=0)
                within.append(nn(jnp.concatenate(lhs, axis=1), rhs))
            scanned_out[rows, cols] = y + jnp.concatenate(within, axis=1)
            state[:, cols] = ecx[SCAN - 1 : SCAN, :] * state[:, cols] + nn(key_cols[s], (v * tlx).astype(bf16))


def call_scan(info, gain, in_down, convbc, spread_heads, pieces, parts, heads, length, width, inner):
    names = ("x", "w", "bc", "dt", "vec")
    moves, arrays, counts, total = gathered_operands(names, pieces)
    two_n = convbc.shape[1]
    steps, subs = length // ROWS, ROWS // SCAN
    shapes = [
        ((length, width), bf16), ((width, inner), bf16), ((width, two_n), bf16), ((heads, width), bf16),
        ((16 + 2 * RANK, inner), f32), ((RANK, inner), bf16), ((length, width), bf16), ((length, RANK), bf16),
        ((length, inner), bf16), ((length, inner), bf16), ((length, inner), f32), ((length, two_n), bf16),
        ((length, two_n), f32), ((length, 128), f32), ((length // SCAN, two_n // 2, inner), bf16),
    ]
    specs = [
        row_block(width), whole_block((width, inner)), whole_block((width, two_n)), whole_block((heads, width)),
        whole_block((16 + 2 * RANK, inner)), whole_block((RANK, inner)), row_block(width), row_block(RANK),
        row_block(inner), row_block(inner), row_block(inner), row_block(two_n),
        row_block(two_n), row_block(128), pl.BlockSpec((subs, two_n // 2, inner), lambda c: (c, 0, 0)),
    ]
    return pl.pallas_call(
        functools.partial(scan_kernel, names, moves, counts, parts, heads),
        grid=(steps,),
        in_specs=[SMEM, whole_block(gain.shape), whole_block(in_down.shape), whole_block(convbc.shape)]
        + [whole_block(spread_heads.shape)] + [ANY] * len(arrays),
        out_shape=[jax.ShapeDtypeStruct(s, d) for s, d in shapes],
        out_specs=specs,
        scratch_shapes=[
            pltpu.VMEM((length, width), bf16), pltpu.VMEM((parts * 16, width), bf16),
            pltpu.VMEM((ROWS + 8, inner), f32), pltpu.VMEM((ROWS + 8, two_n), f32),
            pltpu.VMEM((two_n // 2, inner), f32), pltpu.SemaphoreType.DMA((total,)),
        ],
        compiler_params=pltpu.CompilerParams(vmem_limit_bytes=LIMIT, dimension_semantics=("arbitrary",)),
        cost_estimate=cost(44),
    )(info, gain, in_down, convbc, spread_heads, *arrays)


def gate_kernel(names, moves, counts, *refs):
    info, normed, low, scanned, x, vec, head_sum, out_down, out_up = refs[:9]
    groups, rest = take_refs(refs[9:], counts)
    (mixed_out, dlayer_out, dy_out, dot_out, back_out, low_back_out, in_up_out, out_down_out, out_up_out) = rest[:9]
    (wz, wo, upz, cots, z, gi, gated, gg, zg, sems) = rest[9:]
    fulls = dict(z=wz, o=wo, cot=cots)
    c = pl.program_id(0)
    inner = wz.shape[1]
    tiles = [slice(j * TILE, (j + 1) * TILE) for j in range(inner // TILE)]

    @pl.when(c == 0)
    def _():
        copy_in(info, [(groups[g], m, fulls[name]) for name, g, m in zip(names, moves[0], moves[1])], sems)
        upz[...] = vec[16 + RANK : 16 + 2 * RANK, :].astype(bf16)
        in_up_out[...] = jnp.zeros_like(in_up_out)
        out_down_out[...] = jnp.zeros_like(out_down_out)
        out_up_out[...] = jnp.zeros_like(out_up_out)

    squares = jnp.zeros((ROWS, 128), f32)
    for cols in tiles:
        zj = nn(normed[...], wz[:, cols]) + nn(low[...], upz[:, cols])
        z[:, cols] = zj
        g = scanned[:, cols] * (zj * sigmoid(zj))
        gi[:, cols] = g
        g = g * g
        squares = squares + sum(g[:, k : k + 128] for k in range(0, TILE, 128))
    scale = lax.rsqrt(jnp.sum(squares, axis=1, keepdims=True) / inner + EPS)
    for cols in tiles:
        gated[:, cols] = (gi[:, cols] * scale * vec[5:6, cols]).astype(bf16)
    side = nt(gated[...], out_down[...]).astype(bf16)
    terms = nt(gated[...], wo[...]) + nn(side, out_up[...])
    live = lax.broadcasted_iota(jnp.int32, (ROWS, 1), 0) + c * ROWS < info[0]
    mixed = jnp.where(live, x[...].astype(f32) + terms, 0.0).astype(bf16)
    if len(mixed_out.shape) == 2:
        mixed_out[...] = mixed
    else:
        chunk = mixed_out.shape[2]
        for j in range(mixed_out.shape[0]):
            mixed_out[j, 0, :, :] = mixed[j * chunk : (j + 1) * chunk, :]
    cot = cots[pl.ds(pl.multiple_of(c * ROWS, ROWS), ROWS), :]
    dlayer_out[...] = jnp.where(live, cot.astype(f32), 0.0).astype(bf16)
    side_grad = nt(dlayer_out[...], out_up[...]).astype(bf16)
    products = jnp.zeros((ROWS, 128), f32)
    for cols in tiles:
        grad = (nn(dlayer_out[...], wo[:, cols]) + nn(side_grad, out_down[:, cols])).astype(bf16)
        gg[:, cols] = grad
        g = grad.astype(f32) * vec[5:6, cols] * gi[:, cols]
        products = products + sum(g[:, k : k + 128] for k in range(0, TILE, 128))
    factor = scale * scale * scale * (jnp.sum(products, axis=1, keepdims=True) / inner)
    dots = jnp.zeros((ROWS, head_sum.shape[1]), f32)
    for cols in tiles:
        grad = scale * (gg[:, cols].astype(f32) * vec[5:6, cols]) - gi[:, cols] * factor
        zj = z[:, cols]
        sig = sigmoid(zj)
        sc = scanned[:, cols].astype(f32)
        dy = (grad * (zj * sig)).astype(bf16)
        dy_out[:, cols] = dy
        zg[:, cols] = (grad * sc * (sig * (1.0 + zj * (1.0 - sig)))).astype(bf16)
        summer = head_sum[cols, :]
        dots = dots + nn(halves(dy.astype(f32) * sc, 1), jnp.concatenate([summer, summer], axis=0))
    dot_out[...] = dots
    back_out[...] = nt(zg[...], wz[...])
    low_back_out[...] = nt(zg[...], upz[...])
    in_up_out[...] += tn(low[...], zg[...])
    out_down_out[...] += tn(side_grad, gated[...])
    out_up_out[...] += tn(side, dlayer_out[...])


def call_gate(info, normed, low, scanned, x, vec, head_sum, out_down, out_up, pieces, groups, parts):
    names = ("z", "o", "cot")
    moves, arrays, counts, total = gathered_operands(names, pieces)
    length, width = x.shape
    inner, heads = head_sum.shape
    chunk = length // (groups * parts)
    if chunk % 16 == 0 and length // parts == ROWS:
        leaving = ((groups, parts, chunk, width), pl.BlockSpec((groups, 1, chunk, width), lambda c: (0, c, 0, 0)))
    else:
        leaving = ((length, width), row_block(width))
    shapes = [
        (leaving[0], bf16), ((length, width), bf16), ((length, inner), bf16), ((length, heads), f32),
        ((length, width), f32), ((length, RANK), f32), ((RANK, inner), f32), ((RANK, inner), f32),
        ((RANK, width), f32),
    ]
    specs = [
        leaving[1], row_block(width), row_block(inner), row_block(heads), row_block(width), row_block(RANK),
        whole_block((RANK, inner)), whole_block((RANK, inner)), whole_block((RANK, width)),
    ]
    return pl.pallas_call(
        functools.partial(gate_kernel, names, moves, counts),
        grid=(length // ROWS,),
        in_specs=[SMEM, row_block(width), row_block(RANK), row_block(inner), row_block(width), whole_block(vec.shape)]
        + [whole_block(head_sum.shape), whole_block(out_down.shape), whole_block(out_up.shape)] + [ANY] * len(arrays),
        out_shape=[jax.ShapeDtypeStruct(s, d) for s, d in shapes],
        out_specs=specs,
        scratch_shapes=[
            pltpu.VMEM((width, inner), bf16), pltpu.VMEM((width, inner), bf16), pltpu.VMEM((RANK, inner), bf16),
            pltpu.VMEM((length, width), bf16), pltpu.VMEM((ROWS, inner), f32), pltpu.VMEM((ROWS, inner), f32),
            pltpu.VMEM((ROWS, inner), bf16), pltpu.VMEM((ROWS, inner), bf16), pltpu.VMEM((ROWS, inner), bf16),
            pltpu.SemaphoreType.DMA((total,)),
        ],
        compiler_params=pltpu.CompilerParams(vmem_limit_bytes=LIMIT, dimension_semantics=("arbitrary",)),
        cost_estimate=cost(43),
    )(info, normed, low, scanned, x, vec, head_sum, out_down, out_up, *arrays)


def back_kernel(parts, heads, *refs):
    (x, normed, low, dlayer, dy, values, pre, keys, prebc, scal, states, dot, back, low_back) = refs[:14]
    (w_full, bc_full, dt_full, vec, up, gain, in_down, convbc, spread_heads, head_sum) = refs[14:24]
    (grad_out, in_up_out, in_down_out, dstate, xbuf, bcbuf, xg, summed) = refs[24:]
    i = pl.program_id(0)
    inner = w_full.shape[1]
    subs = ROWS // SCAN
    nstate = keys.shape[1] // 2
    tiles = [slice(j * TILE, (j + 1) * TILE) for j in range(inner // TILE)]

    @pl.when(i == 0)
    def _():
        dstate[...] = jnp.zeros_like(dstate)
        xbuf[ROWS:, :] = jnp.zeros((8, inner), f32)
        bcbuf[ROWS:, :] = jnp.zeros((8, bcbuf.shape[1]), f32)
        summed[...] = jnp.zeros_like(summed)
        in_up_out[...] = jnp.zeros_like(in_up_out)
        in_down_out[...] = jnp.zeros_like(in_down_out)

    hv = head_vectors(vec, parts)
    rate = -jnp.exp(hv[1:2, 0:heads])
    upper = triangle(SCAN, False)
    upper_f = upper.astype(f32)
    raw_parts = [None] * subs
    for s in reversed(range(subs)):
        rows = slice(s * SCAN, (s + 1) * SCAN)
        steps, cum = scal[rows, 0:heads], scal[rows, heads : 2 * heads]
        cum_row = cum.T
        last = cum[SCAN - 1 : SCAN, :]
        dt2, ecum2, tail2 = halves(steps, 1), halves(jnp.exp(cum), 1), halves(jnp.exp(last - cum), 1)
        b_part, c_part = keys[rows, 0:nstate], keys[rows, nstate:]
        c_cols = c_part.astype(f32).T.astype(bf16)
        scores = jnp.where(upper, nt(b_part, c_part), 0.0)
        pulled = jnp.zeros((SCAN, SCAN), f32)
        c_grad = jnp.zeros((SCAN, nstate), f32)
        b_grad = jnp.zeros((SCAN, nstate), f32)
        direct = jnp.zeros((SCAN, heads), f32)
        through = jnp.zeros((SCAN, heads), f32)
        for j, cols in enumerate(tiles):
            dtx, ecx, tlx = (nn(v, spread_heads[:, cols]) for v in (dt2, ecum2, tail2))
            g_low = dy[rows, cols]
            g = g_low.astype(f32)
            v = values[rows, cols].astype(f32)
            vw = v * dtx
            dstate_low = dstate[:, cols].astype(bf16)
            within = []
            for p in range(TILE // 128):
                part = slice(p * 128, (p + 1) * 128)
                vw_split = split_lanes(vw[:, part])
                lhs = []
                for a in range(2):
                    h = (j * TILE + p * 128) // HEAD + a
                    gap = cum_row[h : h + 1, :] - cum[:, h : h + 1]
                    decay = jnp.exp(jnp.minimum(gap, 0.0))
                    pulled = pulled + decay * nt(vw_split[a], g_low[:, part])
                    lhs.append((decay * scores).astype(bf16))
                rhs = jnp.concatenate(split_lanes(g[:, part]), axis=0)
                within.append(nn(jnp.concatenate(lhs, axis=1), rhs))
            dvw = jnp.concatenate(within, axis=1) + tlx * nn(b_part, dstate_low)
            vg = dtx * dvw + vec[6:7, cols] * g
            summer = head_sum[cols, :]
            summer = jnp.concatenate([summer, summer], axis=0)
            direct = direct + nn(halves(v * dvw, 1), summer)
            through = through + nn(halves(v * vg, 1), summer)
            ge = (ecx * g).astype(bf16)
            c_grad = c_grad + nt(ge, states[s, :, cols])
            b_grad = b_grad + nt((tlx * vw).astype(bf16), dstate_low)
            dstate[:, cols] = ecx[SCAN - 1 : SCAN, :] * dstate[:, cols] + nn(c_cols, ge)
            pv = pre[rows, cols].astype(f32)
            sig = sigmoid(pv)
            xbuf[rows, cols] = vg * (sig * (1.0 + pv * (1.0 - sig)))
        pulled = jnp.where(upper, pulled, 0.0)
        b_grad = b_grad + nn(pulled.astype(bf16), c_part)
        c_grad = c_grad + nn(pulled.T.astype(bf16), b_part)
        pb = prebc[rows, :]
        sig = sigmoid(pb)
        bcbuf[rows, :] = jnp.concatenate([b_grad, c_grad], axis=1) * (sig * (1.0 + pb * (1.0 - sig)))
        change = dot[rows, :] - through
        later = exact(upper_f, change) + summed[0:1, 0:heads]
        summed[0:1, 0:heads] = later[0:1, :]
        raw_parts[s] = (direct + rate * later) * scal[rows, 2 * heads : 3 * heads]
    raw_grad = jnp.concatenate(raw_parts, axis=0).astype(bf16)

    for cols in tiles:
        xg[:, cols] = sum(vec[k : k + 1, cols] * xbuf[3 - k : 3 - k + ROWS, cols] for k in range(4)).astype(bf16)
    xbuf[ROWS:, :] = xbuf[0:8, :]
    bc_grad = sum(convbc[k : k + 1, :] * bcbuf[3 - k : 3 - k + ROWS, :] for k in range(4)).astype(bf16)
    bcbuf[ROWS:, :] = bcbuf[0:8, :]
    low_grad = (low_back[...] + nt(xg[...], up[...])).astype(bf16)
    in_up_out[...] += tn(low[...], xg[...])
    in_down_out[...] += tn(low_grad, normed[...])
    ng = back[...] + nt(xg[...], w_full[...]) + nt(bc_grad, bc_full[...])
    ng = ng + nn(raw_grad, dt_full[...]) + nt(low_grad, in_down[...])
    xv = x[...].astype(f32)
    rms = lax.rsqrt(jnp.mean(xv * xv, axis=1, keepdims=True) + EPS)
    ng = ng * gain[...]
    inner_norm = jnp.mean(ng * xv, axis=1, keepdims=True)
    grad_out[...] = (dlayer[...].astype(f32) + rms * ng - xv * (rms * rms * rms * inner_norm)).astype(bf16)


def call_back(rows_in, consts, parts, heads):
    x, w_full = rows_in[0], consts[0]
    length, width = x.shape
    inner = w_full.shape[1]
    two_n = rows_in[7].shape[1]
    steps, subs = length // ROWS, ROWS // SCAN

    def spec(a):
        if a.ndim == 3:
            return pl.BlockSpec((subs,) + a.shape[1:], lambda i: (steps - 1 - i, 0, 0))
        return pl.BlockSpec((ROWS, a.shape[1]), lambda i: (steps - 1 - i, 0))

    return pl.pallas_call(
        functools.partial(back_kernel, parts, heads),
        grid=(steps,),
        in_specs=[spec(a) for a in rows_in] + [whole_block(a.shape) for a in consts],
        out_shape=[
            jax.ShapeDtypeStruct((length, width), bf16), jax.ShapeDtypeStruct((RANK, inner), f32),
            jax.ShapeDtypeStruct((RANK, width), f32),
        ],
        out_specs=[spec(x), whole_block((RANK, inner)), whole_block((RANK, width))],
        scratch_shapes=[
            pltpu.VMEM((two_n // 2, inner), f32), pltpu.VMEM((ROWS + 8, inner), f32),
            pltpu.VMEM((ROWS + 8, two_n), f32), pltpu.VMEM((ROWS, inner), bf16), pltpu.VMEM((8, 128), f32),
        ],
        compiler_params=pltpu.CompilerParams(vmem_limit_bytes=LIMIT, dimension_semantics=("arbitrary",)),
        cost_estimate=cost(50),
    )(*rows_in, *consts)


def turn_kernel(info, came, leave):
    groups, parts = came.shape[:2]
    for p in range(parts):
        for d in range(groups):
            leave[d, p, :, :] = came[lax.rem(d + groups - info[p], groups), p, :, :]


def call_turn(offsets, came):
    return pl.pallas_call(
        turn_kernel,
        in_specs=[SMEM, pl.BlockSpec(memory_space=pltpu.VMEM)],
        out_shape=jax.ShapeDtypeStruct(came.shape, came.dtype),
        out_specs=pl.BlockSpec(memory_space=pltpu.VMEM),
        compiler_params=pltpu.CompilerParams(vmem_limit_bytes=LIMIT),
        cost_estimate=cost(3),
    )(offsets, came)


def arrange_kernel(labels, far_labels, groups, parts, info, sums, *refs):
    far, (in_up, out_down, out_up, in_down) = refs[:-4], refs[-4:]
    cols = in_up.shape[1] // groups
    for i, label in enumerate(labels):
        g = info[1 + label["z"] * 2 + label["x"]]
        in_up[:, lanes(g, cols)] = sums[i, :, 0:cols].astype(f32)
    width = far[0].shape[2]
    first, second = out_down.shape[1] // width, out_up.shape[1] // width
    at = 0
    for part in far:
        for i in range(part.shape[0]):
            label = far_labels[at]
            at += 1
            own = info[1 + label["z"] * 2 + label["x"]] * parts + info[1 + groups + label["y"] * 2 + label["c"]]

            @pl.when(own < first)
            def _():
                out_down[:, lanes(own, width)] = part[i, :, :].astype(f32)

            @pl.when((own >= first) & (own < first + second))
            def _():
                out_up[:, lanes(own - first, width)] = part[i, :, :].astype(f32)

            @pl.when(own >= first + second)
            def _():
                in_down[lanes(own - first - second, width), :] = part[i, :, :].astype(f32).T


def call_arrange(info, sums, far_sums, labels, far_labels, groups, parts, inner, width, cols):
    rows = sums.shape[1]
    vmem = pl.BlockSpec(memory_space=pltpu.VMEM)
    shapes = [(rows, 2 * cols), (rows, inner), (rows, width), (width, rows)]
    return pl.pallas_call(
        functools.partial(arrange_kernel, labels, far_labels, groups, parts),
        in_specs=[SMEM, vmem] + [vmem] * len(far_sums),
        out_shape=[jax.ShapeDtypeStruct(s, f32) for s in shapes],
        out_specs=[vmem] * 4,
        compiler_params=pltpu.CompilerParams(vmem_limit_bytes=LIMIT),
        cost_estimate=cost(3),
    )(info, sums, *far_sums)


def moved(block, axis, route):
    size = lax.axis_size(axis)
    return lax.ppermute(block, axis, [(i, route(i, size)) for i in range(size)])


def hop(name, block):
    axis = "dp" if name in "zx" else "tensor"
    if name in "xc":
        return [moved(block, axis, lambda i, n: i ^ 1)]
    return [
        moved(block, axis, functools.partial(lambda k, i, n: (i + 2 * k) % n, k))
        for k in range(1, lax.axis_size(axis) // 2)
    ]


def widened(name, block, labels):
    got = hop(name, block)
    lists = labels + sum([[dict(label, **{name: k + 1}) for label in labels] for k in range(len(got))], [])
    return [block] + got, lists


HERE = dict(z=0, x=0, y=0, c=0)


def tie(first, *others):
    return lax.optimization_barrier((first,) + others)[0]


def index_table(length_of, groups, parts, group, rank):
    dp_from = [((group ^ kx) - 2 * kz) % groups for kz in range(groups // 2) for kx in range(2)]
    part_from = [((rank ^ kc) - 2 * ky) % parts for ky in range(parts // 2) for kc in range(2)]
    partner = [rank ^ k for k in range(parts)]
    return jnp.stack([length_of] + dp_from + part_from + partner).astype(jnp.int32)


def placed(arrays, labels, groups, take, place):
    moves, at = [], 0
    for which, array in enumerate(arrays):
        for index in range(array.shape[0]):
            label = labels[at]
            at += 1
            if label is None:
                continue
            g_at = 1 + label["z"] * 2 + label["x"]
            t_at = 1 + groups + label["y"] * 2 + label["c"]
            moves.append((which, index, take, functools.partial(
                lambda g_at, t_at, info, full: place(info[g_at], info[t_at], full), g_at, t_at)))
    return Pieces(list(arrays), moves)


def paired(arrays, groups, parts, index, place):
    moves = [
        (k, index, None, functools.partial(lambda at, info, full: place(info[at], full), 1 + groups + parts + k))
        for k in range(parts)
    ]
    return Pieces(list(arrays), moves)


def single(array):
    return Pieces([array], [(0, None, None, lambda info, full: full)])


def span(index, size, offset=0, step=None):
    return pl.ds(pl.multiple_of(index * (size if step is None else step) + offset, 16), size)


def lanes(index, size):
    return pl.ds(pl.multiple_of(index * size, size), size)


def exchanged(blocks):
    return [
        block if k == 0 else moved(block, "tensor", functools.partial(lambda k, i, n: i ^ k, k))
        for k, block in enumerate(blocks)
    ]


def on_device(
    tokens, cotangent, destination, lengths, adapter_of, norm_gain, w_zx, w_bc, w_dt, w_out,
    conv_x, conv_bc, dt_bias, a_log, d_skip, out_gain, in_down, in_up, out_down, out_up,
):
    groups, parts = lax.axis_size("dp"), lax.axis_size("tensor")
    group, rank = lax.axis_index("dp"), lax.axis_index("tensor")
    seq_grp, part_len, width = tokens.shape
    rows, _, cols = w_zx.shape
    own_heads = w_dt.shape[1]
    length, inner, heads = part_len * parts, cols * parts, own_heads * parts
    mine = group * seq_grp + rank
    offset = destination[rank] // seq_grp
    adapter = adapter_of[mine] * RANK
    info = index_table(lengths[mine], groups, parts, group, rank)

    def swapped(array, axes="tensor"):
        return lax.all_to_all(array, axes, split_axis=0, concat_axis=0, tiled=True)

    def col_place(t, full):
        return full.at[:, lanes(t, cols)]

    head_rows = lax.dynamic_update_slice(jnp.zeros((8, cols), f32), jnp.stack([dt_bias, a_log]), (0, rank * own_heads))
    own_vec = jnp.concatenate([
        conv_x.astype(f32), out_gain.astype(f32)[None], jnp.repeat(d_skip, cols // own_heads)[None],
        jnp.zeros((1, cols), f32), head_rows])
    own_vec = lax.optimization_barrier(own_vec)
    vecs = []
    for k in range(parts):
        theirs = lax.dynamic_slice_in_dim(in_up, adapter_of[group * seq_grp + (rank ^ k)] * RANK, RANK, 0)
        vecs.append(jnp.concatenate([own_vec, theirs[:, 1].astype(f32), theirs[:, 0].astype(f32)]))

    half, share, two_n = rows // 2, rows // parts, w_bc.shape[1]
    packed = share % 32 == 0 and rows % 128 == 0 and cols == 2 * two_n
    w_x = w_zx[:, 1]
    if packed:
        own_bc = lax.dynamic_slice_in_dim(w_bc, rank * share, share, 0)
        own_bc = jnp.concatenate([own_bc[: share // 2], own_bc[share // 2 :]], axis=1)
        own_dt = jnp.zeros((16, cols), bf16).at[:own_heads, :rows].set(w_dt.T)
        block = jnp.concatenate([w_x[:half], own_bc, w_x[half:], own_dt])
    else:
        block = w_x
    extra = block.shape[0] // 2
    token_rows = swapped(tokens)
    along_z, labels = widened("z", block[None], [HERE])
    wz_y, wz_labels = widened("y", w_zx[:, 0][None], [HERE])
    along_z, wz_y = lax.optimization_barrier((along_z, wz_y))

    count = len(wz_y)
    later, later_labels = widened("z", jnp.concatenate(wz_y + [w_out[None]]), wz_labels + [HERE])

    first, first_labels = widened("x", jnp.concatenate([a[:, :extra] for a in along_z]), labels)
    second, token_rows = lax.optimization_barrier((jnp.concatenate([a[:, extra:] for a in along_z]), token_rows))
    second, second_labels = widened("y", second, labels)
    first, first_labels = widened("y", jnp.concatenate(first), first_labels)
    second, second_labels = widened("x", jnp.concatenate(second), second_labels)
    first, second, later = lax.optimization_barrier((first, second, later))
    gathered = jnp.concatenate(first + second)
    vec_rows = exchanged(vecs)
    gathered = [gathered] + hop("c", gathered)
    x_pieces = single(token_rows.reshape(length, width))
    vec_pieces = paired(vec_rows, groups, parts, None, col_place)
    crossed = [first_labels, second_labels]
    none = [[None] * len(first_labels), [None] * len(second_labels)]

    def across(lists):
        other = [None if label is None else dict(label, c=1) for label in sum(lists, [])]
        return sum(lists, []) + other

    x_weights = placed(
        gathered, across([crossed[0], none[1]]), groups, (pl.ds(0, half),),
        lambda g, t, full: full.at[span(g, half, 0, rows), lanes(t, cols)],
    )
    x_weights.moves += placed(
        gathered, across([none[0], crossed[1]]), groups, (pl.ds(0, half),),
        lambda g, t, full: full.at[span(g, half, half, rows), lanes(t, cols)],
    ).moves
    if packed:
        bc_weights = placed(
            gathered, across([crossed[0], none[1]]), groups, (pl.ds(half, 16), pl.ds(0, two_n)),
            lambda g, t, full: full.at[span(g * parts + t, 16, 0, share), :],
        )
        bc_weights.moves += placed(
            gathered, across([crossed[0], none[1]]), groups, (pl.ds(half, 16), pl.ds(two_n, two_n)),
            lambda g, t, full: full.at[span(g * parts + t, 16, 16, share), :],
        ).moves
        dt_weights = placed(
            gathered, across([none[0], crossed[1]]), groups, (pl.ds(half, 16), pl.ds(0, rows)),
            lambda g, t, full: full.at[span(t, 16), lanes(g, rows)],
        )
        bc_weights.arrays, dt_weights.arrays = [], []
    else:
        bc_weights = single(lax.all_gather(w_bc, "dp", axis=0, tiled=True))
        all_dt = lax.all_gather(lax.all_gather(w_dt, "dp", axis=0, tiled=True), "tensor", axis=0)
        all_dt = jnp.pad(all_dt.transpose(0, 2, 1), ((0, 0), (0, 16 - own_heads), (0, 0)))
        dt_weights = single(all_dt.reshape(parts * 16, width))

    def piece_labels(chosen):
        return [label for at, label in enumerate(later_labels) if (at % (count + 1) < count) == chosen]

    wz, wz_labels = widened("x", jnp.concatenate([a[:count] for a in later]), piece_labels(True))
    wo, wo_labels = jnp.concatenate([a[count:] for a in later]), piece_labels(False)
    by_chip = [(wo, wo_labels), (hop("x", wo)[0], [dict(label, x=1) for label in wo_labels])]
    for k, got in enumerate(hop("y", wo)):
        by_chip.append((got, [dict(label, y=k + 1) for label in wo_labels]))
    for k in range(1, parts // 2):
        got = lax.ppermute(wo, ("dp", "tensor"), [
            (g * parts + t, (g ^ 1) * parts + (t + 2 * k) % parts) for g in range(groups) for t in range(parts)])
        by_chip.append((got, [dict(label, x=1, y=k) for label in wo_labels]))
    wo, wo_labels = [a for a, _ in by_chip], sum([lab for _, lab in by_chip], [])

    def block_place(g, t, full):
        return full.at[span(g, rows), lanes(t, cols)]

    def across_cores(arrays, labels):
        held = jnp.concatenate(arrays)
        held, labels = widened("c", held, labels)
        return placed(held, labels, groups, None, block_place)

    down_in = lax.dynamic_slice_in_dim(in_down, adapter, RANK, 1)
    down_out = lax.dynamic_slice_in_dim(out_down, adapter, RANK, 0)
    up_out = lax.dynamic_slice_in_dim(out_up, adapter, RANK, 0)
    gain = norm_gain.astype(f32)[None]
    convbc = jnp.pad(conv_bc.astype(f32), ((0, 3), (0, 0)))
    head_of = jnp.arange(inner) // (inner // heads)
    spread_heads = (jnp.arange(2 * heads)[:, None] % heads == head_of[None, :]).astype(bf16)
    head_sum = (head_of[:, None] == jnp.arange(heads)[None, :]).astype(bf16)

    (x, w_full, bc_full, dt_full, vec, up, normed, low, pre, values, scanned, keys, prebc, scal, states) = call_scan(
        info, gain, down_in, convbc, spread_heads,
        dict(x=x_pieces, w=x_weights, bc=bc_weights, dt=dt_weights, vec=vec_pieces),
        parts, heads, length, width, inner,
    )

    cot_rows = swapped(tie(cotangent, gathered[0]))
    (wz, wo, cot_rows), low = lax.optimization_barrier(((wz, wo, cot_rows), low))
    cot_pieces = single(cot_rows.reshape(length, width))
    z_weights, o_weights = across_cores(wz, wz_labels), across_cores(wo, wo_labels)
    out = call_gate(
        info, normed, low, scanned, x, vec, head_sum, down_out, up_out,
        dict(z=z_weights, o=o_weights, cot=cot_pieces), groups, parts,
    )
    mixed, dlayer, dy, dot, back, low_back, up_z_grad, out_down_part, out_up_part = out

    if mixed.ndim == 2:
        mixed = mixed.reshape(parts, groups, -1, width).transpose(1, 0, 2, 3)
    chunk = mixed.shape[2]
    came = swapped(mixed.reshape(groups * parts, chunk, width), ("dp", "tensor"))

    out = call_back(
        (x, normed, low, dlayer, dy, values, pre, keys, prebc, scal, states, dot, back, low_back),
        (w_full, bc_full, dt_full, vec, up, gain, down_in, convbc, spread_heads, head_sum), parts, heads,
    )
    came, out = lax.optimization_barrier((came, out))
    token_rows, up_x_grad, in_down_part = out

    offsets = destination[:seq_grp] // seq_grp
    leave = call_turn(offsets, came.reshape(groups, parts, chunk, width))

    def second_leg(leave):
        return swapped(leave, "dp").transpose(1, 0, 2, 3).reshape(parts, part_len, width)

    token_rows = token_rows.reshape(parts, part_len, width)
    token_grad = exchanged([lax.dynamic_index_in_dim(token_rows, rank ^ k, 0, keepdims=False) for k in range(parts)])

    def stacked(blocks):
        result = jnp.zeros((parts,) + blocks[0].shape, blocks[0].dtype)
        for k, block in enumerate(blocks):
            result = lax.dynamic_update_index_in_dim(result, block, rank ^ k, 0)
        return result

    ups = jnp.stack([up_z_grad, up_x_grad]).astype(bf16)
    others = jnp.concatenate([out_down_part, out_up_part, in_down_part], axis=1).astype(bf16)
    own = groups * parts
    if (2 * cols) % (groups * 128) or others.shape[1] % (own * 128):

        def at_adapter(part):
            zeros = jnp.zeros((in_down.shape[1], part.shape[1]), bf16)
            return lax.dynamic_update_slice_in_dim(zeros, part, adapter, 0)

        in_up_grad = jnp.stack([lax.psum_scatter(at_adapter(a), "tensor", scatter_dimension=1, tiled=True) for a in ups], axis=1)
        in_up_grad = lax.psum(in_up_grad, "dp").astype(f32)
        others = lax.psum(at_adapter(others), ("dp", "tensor")).astype(f32)
        return (
            second_leg(leave), stacked(token_grad), others[:, inner + width :].T, in_up_grad, others[:, :inner], others[:, inner : inner + width]
        )

    ups = ups.reshape(2, RANK, parts, cols // 128, 128).transpose(2, 0, 3, 1, 4).reshape(parts, groups, RANK, -1)
    ups = ups.transpose(1, 0, 2, 3).reshape(own, RANK, -1)
    others = others.reshape(RANK, own, -1).transpose(1, 0, 2)
    pooled = swapped(jnp.concatenate([ups, others], axis=2), ("dp", "tensor"))
    row_of = adapter_of[:, None] * RANK + jnp.arange(RANK)[None, :]
    select = (row_of.reshape(1, -1) == jnp.arange(in_down.shape[1])[:, None]).astype(bf16)
    sums = nn(select, pooled.reshape(own * RANK, -1)).astype(bf16)[None]
    sums, labels = widened("z", sums, [HERE])
    sums, token_grad, leave = lax.optimization_barrier((sums, token_grad, leave))
    mixed = second_leg(leave)
    sums, labels = widened("x", jnp.concatenate(sums), labels)
    sums = jnp.concatenate(sums)
    up_count = ups.shape[2] // 128
    far_sums, far_labels = widened("y", sums[:, :, up_count * 128 :], labels)
    far_sums = jnp.concatenate(far_sums)
    far_sums, far_labels = widened("c", far_sums, far_labels)
    in_up_grad, out_down_grad, out_up_grad, in_down_grad = call_arrange(
        info, sums, far_sums, labels, far_labels, groups, parts, inner, width, cols
    )
    in_up_grad = jnp.stack([in_up_grad[:, :cols], in_up_grad[:, cols:]], axis=1)
    return (mixed, stacked(token_grad), in_down_grad, in_up_grad, out_down_grad, out_up_grad)


def solution(mesh):
    return jax.shard_map(
        on_device,
        mesh=mesh,
        in_specs=(
            P("dp", "tensor", None), P("dp", "tensor", None), P(), P(), P(), P(),
            P("dp", None, "tensor"), P("dp", None), P("dp", "tensor"), P("dp", "tensor"),
            P(None, "tensor"), P(), P("tensor"), P("tensor"), P("tensor"), P("tensor"),
            P(), P(None, None, "tensor"), P(), P(),
        ),
        out_specs=(
            P("dp", "tensor", None), P("dp", "tensor", None), P(), P(None, None, "tensor"), P(), P(),
        ),
        check_vma=False,
    )
```

```python
import functools

import jax
import jax.numpy as jnp
from jax import lax
from jax.experimental import pallas as pl
from jax.experimental.pallas import tpu as pltpu
from jax.sharding import PartitionSpec as P

RANK = 16
SCAN = 128
ROWS = 256
TILE = 512
HEAD = 64
EPS = 1e-05
LIMIT = 58 * 1024 * 1024

f32 = jnp.float32
bf16 = jnp.bfloat16
ANY = pl.BlockSpec(memory_space=pl.ANY)
SMEM = pl.BlockSpec(memory_space=pltpu.SMEM)


def nn(a, b):
    return lax.dot_general(a, b, (((1,), (0,)), ((), ())), preferred_element_type=f32)


def nt(a, b):
    return lax.dot_general(a, b, (((1,), (1,)), ((), ())), preferred_element_type=f32)


def tn(a, b):
    return lax.dot_general(a, b, (((0,), (0,)), ((), ())), preferred_element_type=f32)


def exact(a, b):
    return lax.dot_general(
        a, b, (((1,), (0,)), ((), ())), preferred_element_type=f32, precision=lax.Precision.HIGHEST
    )


def halves(v, axis):
    high = v.astype(bf16)
    low = (v - high.astype(f32)).astype(bf16)
    return jnp.concatenate([high, low], axis=axis)


def sigmoid(v):
    return 1.0 / (1.0 + jnp.exp(-v))


def softplus(v):
    return jnp.maximum(v, 0.0) + jnp.log1p(jnp.exp(-jnp.abs(v)))


def triangle(n, lower):
    row = lax.broadcasted_iota(jnp.int32, (n, n), 0)
    col = lax.broadcasted_iota(jnp.int32, (n, n), 1)
    return row >= col if lower else row <= col


def head_vectors(vec, parts):
    width = vec.shape[1] // parts
    total = vec[8:16, 0:128]
    for t in range(1, parts):
        total = total + vec[8:16, t * width : t * width + 128]
    return total


def split_lanes(v):
    low_lanes = lax.broadcasted_iota(jnp.int32, v.shape, 1) < HEAD
    return jnp.where(low_lanes, v, 0.0).astype(bf16), jnp.where(low_lanes, 0.0, v).astype(bf16)


class Pieces:
    def __init__(self, arrays, moves):
        self.arrays, self.moves = arrays, moves


def copy_in(info, groups, sems):
    copies = []
    for refs, moves, full in groups:
        for which, index, take, place in moves:
            src = refs[which]
            if index is not None:
                src = src.at[index]
            if take is not None:
                src = src.at[take]
            copies.append(pltpu.make_async_copy(src, place(info, full), sems.at[len(copies)]))
    for copy in copies:
        copy.start()
    for copy in copies:
        copy.wait()


def whole_block(shape):
    return pl.BlockSpec(shape, lambda c: (0,) * len(shape))


def row_block(width, rows=ROWS):
    return pl.BlockSpec((rows, width), lambda c: (c, 0))


def take_refs(refs, counts):
    taken, at = [], 0
    for count in counts:
        taken.append(refs[at : at + count])
        at += count
    return taken, refs[at:]


def gathered_operands(names, pieces):
    owners, lists, arrays, counts = [], [], [], []
    for i, name in enumerate(names):
        owners.append(i if pieces[name].arrays else owners[-1])
        lists.append(pieces[name].moves)
        arrays += pieces[name].arrays
        counts.append(len(pieces[name].arrays))
    return (owners, lists), arrays, counts, sum(len(m) for m in lists)


def cost(micros):
    return pl.CostEstimate(flops=int(micros * 1.1e9), bytes_accessed=1 << 20, transcendentals=0)


def scan_kernel(names, moves, counts, parts, heads, *refs):
    info, gain, in_down, convbc, spread_heads = refs[:5]
    groups, rest = take_refs(refs[5:], counts)
    (x_out, w_full, bc_full, dt_full, vec, up, normed_out, low_out, pre_out, values_out, scanned_out) = rest[:11]
    (keys_out, prebc_out, scal_out, states_out, xs, dt_wide, xbuf, bcbuf, state, sems) = rest[11:]
    fulls = dict(x=xs, w=w_full, bc=bc_full, dt=dt_wide, vec=vec)
    c = pl.program_id(0)
    inner = w_full.shape[1]
    subs = ROWS // SCAN

    @pl.when(c == 0)
    def _():
        copy_in(info, [(groups[g], m, fulls[name]) for name, g, m in zip(names, moves[0], moves[1])], sems)
        state[...] = jnp.zeros_like(state)
        xbuf[0:8, :] = jnp.zeros((8, inner), f32)
        bcbuf[0:8, :] = jnp.zeros((8, bcbuf.shape[1]), f32)
        up[...] = vec[16 : 16 + RANK, :].astype(bf16)
        own = heads // parts
        dt_full[...] = jnp.concatenate(
            [dt_wide[16 * t : 16 * t + 16, :].astype(f32)[:own] for t in range(parts)], axis=0
        ).astype(bf16)

    x_low = xs[pl.ds(pl.multiple_of(c * ROWS, ROWS), ROWS), :]
    x_out[...] = x_low
    x = x_low.astype(f32)
    rms = lax.rsqrt(jnp.mean(x * x, axis=1, keepdims=True) + EPS)
    normed_out[...] = (x * rms * gain[...]).astype(bf16)
    low_out[...] = nn(normed_out[...], in_down[...]).astype(bf16)
    hv = head_vectors(vec, parts)
    bias, rate = hv[0:1, 0:heads], -jnp.exp(hv[1:2, 0:heads])

    bcbuf[8:, :] = nn(normed_out[...], bc_full[...])
    pre = convbc[4:5, :] + sum(convbc[k : k + 1, :] * bcbuf[5 + k : 5 + k + ROWS, :] for k in range(4))
    bcbuf[0:8, :] = bcbuf[ROWS : ROWS + 8, :]
    prebc_out[...] = pre
    keys_out[...] = (pre * sigmoid(pre)).astype(bf16)
    nstate = keys_out.shape[1] // 2

    raw = nt(normed_out[...], dt_full[...]) + bias
    steps = softplus(raw)
    lower = triangle(SCAN, True)
    lower_f = lower.astype(f32)
    cums, cum_rows, grown, scores, key_cols = [], [], [], [], []
    for s in range(subs):
        rows = slice(s * SCAN, (s + 1) * SCAN)
        dt_s = steps[rows]
        cum = exact(lower_f, dt_s * rate)
        cums.append(cum)
        cum_rows.append(cum.T)
        b_part, c_part = keys_out[rows, 0:nstate], keys_out[rows, nstate:]
        scores.append(jnp.where(lower, nt(c_part, b_part), 0.0))
        key_cols.append(b_part.astype(f32).T.astype(bf16))
        tail = jnp.exp(cum[SCAN - 1 : SCAN, :] - cum)
        grown.append((halves(dt_s, 1), halves(jnp.exp(cum), 1), halves(dt_s * tail, 1)))
    scal_out[...] = jnp.concatenate(
        [steps, jnp.concatenate(cums, axis=0), sigmoid(raw), jnp.zeros((ROWS, 128 - 3 * heads), f32)], axis=1
    )

    for j in range(inner // TILE):
        cols = slice(j * TILE, (j + 1) * TILE)
        xbuf[8:, cols] = nn(normed_out[...], w_full[:, cols]) + nn(low_out[...], up[:, cols])
        halo = xbuf[:, cols]
        pre = vec[4:5, cols] + vec[3:4, cols] * halo[8:]
        pre = pre + sum(vec[k : k + 1, cols] * pltpu.roll(halo, 3 - k, 0)[8:] for k in range(3))
        xbuf[0:8, cols] = xbuf[ROWS : ROWS + 8, cols]
        pre_out[:, cols] = pre.astype(bf16)
        values_out[:, cols] = (pre * sigmoid(pre)).astype(bf16)
        for s in range(subs):
            rows = slice(s * SCAN, (s + 1) * SCAN)
            dtx, ecx, tlx = (nn(v, spread_heads[:, cols]) for v in grown[s])
            state_low = state[:, cols].astype(bf16)
            states_out[s, :, cols] = state_low
            v = values_out[rows, cols].astype(f32)
            y = ecx * nn(keys_out[rows, nstate:], state_low) + vec[6:7, cols] * v
            vw = v * dtx
            within = []
            for p in range(TILE // 128):
                lhs = []
                for a in range(2):
                    h = (j * TILE + p * 128) // HEAD + a
                    gap = cums[s][:, h : h + 1] - cum_rows[s][h : h + 1, :]
                    lhs.append((jnp.exp(jnp.minimum(gap, 0.0)) * scores[s]).astype(bf16))
                rhs = jnp.concatenate(split_lanes(vw[:, p * 128 : (p + 1) * 128]), axis=0)
                within.append(nn(jnp.concatenate(lhs, axis=1), rhs))
            scanned_out[rows, cols] = y + jnp.concatenate(within, axis=1)
            state[:, cols] = ecx[SCAN - 1 : SCAN, :] * state[:, cols] + nn(key_cols[s], (v * tlx).astype(bf16))


def call_scan(info, gain, in_down, convbc, spread_heads, pieces, parts, heads, length, width, inner):
    names = ("x", "w", "bc", "dt", "vec")
    moves, arrays, counts, total = gathered_operands(names, pieces)
    two_n = convbc.shape[1]
    steps, subs = length // ROWS, ROWS // SCAN
    shapes = [
        ((length, width), bf16), ((width, inner), bf16), ((width, two_n), bf16), ((heads, width), bf16),
        ((16 + 2 * RANK, inner), f32), ((RANK, inner), bf16), ((length, width), bf16), ((length, RANK), bf16),
        ((length, inner), bf16), ((length, inner), bf16), ((length, inner), f32), ((length, two_n), bf16),
        ((length, two_n), f32), ((length, 128), f32), ((length // SCAN, two_n // 2, inner), bf16),
    ]
    specs = [
        row_block(width), whole_block((width, inner)), whole_block((width, two_n)), whole_block((heads, width)),
        whole_block((16 + 2 * RANK, inner)), whole_block((RANK, inner)), row_block(width), row_block(RANK),
        row_block(inner), row_block(inner), row_block(inner), row_block(two_n),
        row_block(two_n), row_block(128), pl.BlockSpec((subs, two_n // 2, inner), lambda c: (c, 0, 0)),
    ]
    return pl.pallas_call(
        functools.partial(scan_kernel, names, moves, counts, parts, heads),
        grid=(steps,),
        in_specs=[SMEM, whole_block(gain.shape), whole_block(in_down.shape), whole_block(convbc.shape)]
        + [whole_block(spread_heads.shape)] + [ANY] * len(arrays),
        out_shape=[jax.ShapeDtypeStruct(s, d) for s, d in shapes],
        out_specs=specs,
        scratch_shapes=[
            pltpu.VMEM((length, width), bf16), pltpu.VMEM((parts * 16, width), bf16),
            pltpu.VMEM((ROWS + 8, inner), f32), pltpu.VMEM((ROWS + 8, two_n), f32),
            pltpu.VMEM((two_n // 2, inner), f32), pltpu.SemaphoreType.DMA((total,)),
        ],
        compiler_params=pltpu.CompilerParams(vmem_limit_bytes=LIMIT, dimension_semantics=("arbitrary",)),
        cost_estimate=cost(44),
    )(info, gain, in_down, convbc, spread_heads, *arrays)


def gate_kernel(names, moves, counts, *refs):
    info, normed, low, scanned, x, vec, out_down, out_up = refs[:8]
    groups, rest = take_refs(refs[8:], counts)
    (mixed_out, dlayer_out, dy_out, side_out, back_out, low_back_out, in_up_out, out_down_out) = rest[:8]
    (wz, wo, upz, cots, z, gi, gated, gg, zg, sems) = rest[8:]
    fulls = dict(z=wz, o=wo, cot=cots)
    c = pl.program_id(0)
    inner = wz.shape[1]
    tiles = [slice(j * TILE, (j + 1) * TILE) for j in range(inner // TILE)]

    @pl.when(c == 0)
    def _():
        copy_in(info, [(groups[g], m, fulls[name]) for name, g, m in zip(names, moves[0], moves[1])], sems)
        upz[...] = vec[16 + RANK : 16 + 2 * RANK, :].astype(bf16)
        in_up_out[...] = jnp.zeros_like(in_up_out)
        out_down_out[...] = jnp.zeros_like(out_down_out)

    squares = jnp.zeros((ROWS, 128), f32)
    for cols in tiles:
        zj = nn(normed[...], wz[:, cols]) + nn(low[...], upz[:, cols])
        z[:, cols] = zj
        g = scanned[:, cols] * (zj * sigmoid(zj))
        gi[:, cols] = g
        g = g * g
        squares = squares + sum(g[:, k : k + 128] for k in range(0, TILE, 128))
    scale = lax.rsqrt(jnp.sum(squares, axis=1, keepdims=True) / inner + EPS)
    for cols in tiles:
        gated[:, cols] = (gi[:, cols] * scale * vec[5:6, cols]).astype(bf16)
    side = nt(gated[...], out_down[...]).astype(bf16)
    side_out[...] = side
    terms = nt(gated[...], wo[...]) + nn(side, out_up[...])
    live = lax.broadcasted_iota(jnp.int32, (ROWS, 1), 0) + c * ROWS < info[0]
    mixed = jnp.where(live, x[...].astype(f32) + terms, 0.0).astype(bf16)
    if len(mixed_out.shape) == 2:
        mixed_out[...] = mixed
    else:
        chunk = mixed_out.shape[2]
        for j in range(mixed_out.shape[0]):
            mixed_out[j, 0, :, :] = mixed[j * chunk : (j + 1) * chunk, :]
    cot = cots[pl.ds(pl.multiple_of(c * ROWS, ROWS), ROWS), :]
    dlayer_out[...] = jnp.where(live, cot.astype(f32), 0.0).astype(bf16)
    side_grad = nt(dlayer_out[...], out_up[...]).astype(bf16)
    products = jnp.zeros((ROWS, 128), f32)
    for cols in tiles:
        grad = (nn(dlayer_out[...], wo[:, cols]) + nn(side_grad, out_down[:, cols])).astype(bf16)
        gg[:, cols] = grad
        g = grad.astype(f32) * vec[5:6, cols] * gi[:, cols]
        products = products + sum(g[:, k : k + 128] for k in range(0, TILE, 128))
    factor = scale * scale * scale * (jnp.sum(products, axis=1, keepdims=True) / inner)
    for cols in tiles:
        grad = scale * (gg[:, cols].astype(f32) * vec[5:6, cols]) - gi[:, cols] * factor
        zj = z[:, cols]
        sig = sigmoid(zj)
        sc = scanned[:, cols].astype(f32)
        dy = (grad * (zj * sig)).astype(bf16)
        dy_out[:, cols] = dy
        zg[:, cols] = (grad * sc * (sig * (1.0 + zj * (1.0 - sig)))).astype(bf16)
    back_out[...] = nt(zg[...], wz[...])
    low_back_out[...] = nt(zg[...], upz[...])
    in_up_out[...] += tn(low[...], zg[...])
    out_down_out[...] += tn(side_grad, gated[...])


def call_gate(info, normed, low, scanned, x, vec, out_down, out_up, pieces, groups, parts):
    names = ("z", "o", "cot")
    moves, arrays, counts, total = gathered_operands(names, pieces)
    length, width = x.shape
    inner = scanned.shape[1]
    chunk = length // (groups * parts)
    if chunk % 16 == 0 and length // parts == ROWS:
        leaving = ((groups, parts, chunk, width), pl.BlockSpec((groups, 1, chunk, width), lambda c: (0, c, 0, 0)))
    else:
        leaving = ((length, width), row_block(width))
    shapes = [
        (leaving[0], bf16), ((length, width), bf16), ((length, inner), bf16), ((length, RANK), bf16),
        ((length, width), f32), ((length, RANK), f32), ((RANK, inner), f32), ((RANK, inner), f32),
    ]
    specs = [
        leaving[1], row_block(width), row_block(inner), row_block(RANK), row_block(width), row_block(RANK),
        whole_block((RANK, inner)), whole_block((RANK, inner)),
    ]
    return pl.pallas_call(
        functools.partial(gate_kernel, names, moves, counts),
        grid=(length // ROWS,),
        in_specs=[SMEM, row_block(width), row_block(RANK), row_block(inner), row_block(width), whole_block(vec.shape)]
        + [whole_block(out_down.shape), whole_block(out_up.shape)] + [ANY] * len(arrays),
        out_shape=[jax.ShapeDtypeStruct(s, d) for s, d in shapes],
        out_specs=specs,
        scratch_shapes=[
            pltpu.VMEM((width, inner), bf16), pltpu.VMEM((width, inner), bf16), pltpu.VMEM((RANK, inner), bf16),
            pltpu.VMEM((length, width), bf16), pltpu.VMEM((ROWS, inner), f32), pltpu.VMEM((ROWS, inner), f32),
            pltpu.VMEM((ROWS, inner), bf16), pltpu.VMEM((ROWS, inner), bf16), pltpu.VMEM((ROWS, inner), bf16),
            pltpu.SemaphoreType.DMA((total,)),
        ],
        compiler_params=pltpu.CompilerParams(vmem_limit_bytes=LIMIT, dimension_semantics=("arbitrary",)),
        cost_estimate=cost(43),
    )(info, normed, low, scanned, x, vec, out_down, out_up, *arrays)


def back_kernel(groups, parts, heads, *refs):
    (x, normed, low, dlayer, dy, values, pre, keys, prebc, scal, states, scanned, side, back, low_back) = refs[:15]
    (w_full, bc_full, dt_full, vec, up, gain, in_down, convbc, spread_heads, head_sum) = refs[15:25]
    (in_up_z, out_down, grad_out) = refs[25:28]
    outs, (in_up_x, out_up, in_down_sum, dstate, xbuf, bcbuf, xg, summed) = refs[28:-8], refs[-8:]
    i = pl.program_id(0)
    inner = w_full.shape[1]
    subs = ROWS // SCAN
    nstate = keys.shape[1] // 2
    tiles = [slice(j * TILE, (j + 1) * TILE) for j in range(inner // TILE)]

    @pl.when(i == 0)
    def _():
        dstate[...] = jnp.zeros_like(dstate)
        xbuf[ROWS:, :] = jnp.zeros((8, inner), f32)
        bcbuf[ROWS:, :] = jnp.zeros((8, bcbuf.shape[1]), f32)
        summed[...] = jnp.zeros_like(summed)
        for total in (in_up_x, out_up, in_down_sum):
            total[...] = jnp.zeros_like(total)

    hv = head_vectors(vec, parts)
    rate = -jnp.exp(hv[1:2, 0:heads])
    upper = triangle(SCAN, False)
    upper_f = upper.astype(f32)
    raw_parts = [None] * subs
    for s in reversed(range(subs)):
        rows = slice(s * SCAN, (s + 1) * SCAN)
        steps, cum = scal[rows, 0:heads], scal[rows, heads : 2 * heads]
        cum_row = cum.T
        last = cum[SCAN - 1 : SCAN, :]
        dt2, ecum2, tail2 = halves(steps, 1), halves(jnp.exp(cum), 1), halves(jnp.exp(last - cum), 1)
        b_part, c_part = keys[rows, 0:nstate], keys[rows, nstate:]
        c_cols = c_part.astype(f32).T.astype(bf16)
        scores = jnp.where(upper, nt(b_part, c_part), 0.0)
        pulled = jnp.zeros((SCAN, SCAN), f32)
        c_grad = jnp.zeros((SCAN, nstate), f32)
        b_grad = jnp.zeros((SCAN, nstate), f32)
        direct = jnp.zeros((SCAN, heads), f32)
        change = jnp.zeros((SCAN, heads), f32)
        for j, cols in enumerate(tiles):
            dtx, ecx, tlx = (nn(v, spread_heads[:, cols]) for v in (dt2, ecum2, tail2))
            g_low = dy[rows, cols]
            g = g_low.astype(f32)
            v = values[rows, cols].astype(f32)
            vw = v * dtx
            dstate_low = dstate[:, cols].astype(bf16)
            within = []
            for p in range(TILE // 128):
                part = slice(p * 128, (p + 1) * 128)
                vw_split = split_lanes(vw[:, part])
                lhs = []
                for a in range(2):
                    h = (j * TILE + p * 128) // HEAD + a
                    gap = cum_row[h : h + 1, :] - cum[:, h : h + 1]
                    decay = jnp.exp(jnp.minimum(gap, 0.0))
                    pulled = pulled + decay * nt(vw_split[a], g_low[:, part])
                    lhs.append((decay * scores).astype(bf16))
                rhs = jnp.concatenate(split_lanes(g[:, part]), axis=0)
                within.append(nn(jnp.concatenate(lhs, axis=1), rhs))
            dvw = jnp.concatenate(within, axis=1) + tlx * nn(b_part, dstate_low)
            vg = dtx * dvw + vec[6:7, cols] * g
            summer = head_sum[cols, :]
            direct = direct + nn((v * dvw).astype(bf16), summer)
            summer = jnp.concatenate([summer, summer], axis=0)
            change = change + nn(halves(g * scanned[rows, cols] - v * vg, 1), summer)
            ge = (ecx * g).astype(bf16)
            c_grad = c_grad + nt(ge, states[s, :, cols])
            b_grad = b_grad + nt((tlx * vw).astype(bf16), dstate_low)
            dstate[:, cols] = ecx[SCAN - 1 : SCAN, :] * dstate[:, cols] + nn(c_cols, ge)
            pv = pre[rows, cols].astype(f32)
            sig = sigmoid(pv)
            xbuf[rows, cols] = vg * (sig * (1.0 + pv * (1.0 - sig)))
        pulled = jnp.where(upper, pulled, 0.0)
        b_grad = b_grad + nn(pulled.astype(bf16), c_part)
        c_grad = c_grad + nn(pulled.T.astype(bf16), b_part)
        pb = prebc[rows, :]
        sig = sigmoid(pb)
        bcbuf[rows, :] = jnp.concatenate([b_grad, c_grad], axis=1) * (sig * (1.0 + pb * (1.0 - sig)))
        later = exact(upper_f, change) + summed[0:1, 0:heads]
        summed[0:1, 0:heads] = later[0:1, :]
        raw_parts[s] = (direct + rate * later) * scal[rows, 2 * heads : 3 * heads]
    raw_grad = jnp.concatenate(raw_parts, axis=0).astype(bf16)

    for cols in tiles:
        halo = xbuf[:, cols]
        total = vec[3:4, cols] * halo[:ROWS]
        total = total + sum(vec[k : k + 1, cols] * pltpu.roll(halo, ROWS + 5 + k, 0)[:ROWS] for k in range(3))
        xg[:, cols] = total.astype(bf16)
    xbuf[ROWS:, :] = xbuf[0:8, :]
    bc_grad = sum(convbc[k : k + 1, :] * bcbuf[3 - k : 3 - k + ROWS, :] for k in range(4)).astype(bf16)
    bcbuf[ROWS:, :] = bcbuf[0:8, :]
    low_grad = (low_back[...] + nt(xg[...], up[...])).astype(bf16)
    in_up_x[...] += tn(low[...], xg[...])
    out_up[...] += tn(side[...], dlayer[...])
    in_down_sum[...] += tn(low_grad, normed[...])
    ng = back[...] + nt(xg[...], w_full[...]) + nt(bc_grad, bc_full[...])
    ng = ng + nn(raw_grad, dt_full[...]) + nt(low_grad, in_down[...])
    xv = x[...].astype(f32)
    rms = lax.rsqrt(jnp.mean(xv * xv, axis=1, keepdims=True) + EPS)
    ng = ng * gain[...]
    inner_norm = jnp.mean(ng * xv, axis=1, keepdims=True)
    grad_out[...] = (dlayer[...].astype(f32) + rms * ng - xv * (rms * rms * rms * inner_norm)).astype(bf16)


    @pl.when(i == pl.num_programs(0) - 1)
    def _():
        if len(outs) > 1:
            for out, total in zip(outs, (in_up_z, in_up_x, out_up, in_down_sum)):
                out[...] = total[...].astype(bf16)
            return
        (shares,) = outs
        cols = inner // parts
        for g in range(groups):
            for t in range(parts):
                own = g * parts + t
                at = g * 2 * cols // groups
                total = in_up_z if at < cols else in_up_x
                at = at % cols + t * cols
                wide = 2 * cols // groups
                shares[own, :, 0:wide] = total[:, at : at + wide].astype(bf16)
                other = shares.shape[2] - wide
                at = own * other
                for total in (out_down, out_up, in_down_sum):
                    if 0 <= at < total.shape[1]:
                        shares[own, :, wide:] = total[:, at : at + other].astype(bf16)
                    at = at - total.shape[1]


def shares_of(groups, parts, inner, width):
    ups, others = 2 * inner // (groups * parts), (inner + 2 * width) // (groups * parts)
    return None if ups % 128 or others % 128 or width % others or inner % others else ups + others


def call_back(rows_in, consts, groups, parts, heads):
    x = rows_in[0]
    length, width = x.shape
    inner = rows_in[4].shape[1]
    two_n = rows_in[7].shape[1]
    steps, subs = length // ROWS, ROWS // SCAN
    shares = shares_of(groups, parts, inner, width)
    if shares is None:
        sums = [(RANK, inner), (RANK, inner), (RANK, width), (RANK, width)]
    else:
        sums = [(groups * parts, RANK, shares)]

    def spec(a):
        if a.ndim == 3:
            return pl.BlockSpec((subs,) + a.shape[1:], lambda i: (steps - 1 - i, 0, 0))
        return pl.BlockSpec((ROWS, a.shape[1]), lambda i: (steps - 1 - i, 0))

    return pl.pallas_call(
        functools.partial(back_kernel, groups, parts, heads),
        grid=(steps,),
        in_specs=[spec(a) for a in rows_in] + [whole_block(a.shape) for a in consts],
        out_shape=[jax.ShapeDtypeStruct((length, width), bf16)] + [jax.ShapeDtypeStruct(s, bf16) for s in sums],
        out_specs=[spec(x)] + [whole_block(s) for s in sums],
        scratch_shapes=[
            pltpu.VMEM((RANK, inner), f32), pltpu.VMEM((RANK, width), f32), pltpu.VMEM((RANK, width), f32),
            pltpu.VMEM((two_n // 2, inner), f32),
            pltpu.VMEM((ROWS + 8, inner), f32), pltpu.VMEM((ROWS + 8, two_n), f32), pltpu.VMEM((ROWS, inner), bf16),
            pltpu.VMEM((8, 128), f32),
        ],
        compiler_params=pltpu.CompilerParams(vmem_limit_bytes=LIMIT, dimension_semantics=("arbitrary",)),
        cost_estimate=cost(50),
    )(*rows_in, *consts)


def turn_kernel(info, came, leave):
    groups, parts = came.shape[:2]
    for p in range(parts):
        for d in range(groups):
            leave[d, p, :, :] = came[lax.rem(d + groups - info[p], groups), p, :, :]


def call_turn(offsets, came):
    return pl.pallas_call(
        turn_kernel,
        in_specs=[SMEM, pl.BlockSpec(memory_space=pltpu.VMEM)],
        out_shape=jax.ShapeDtypeStruct(came.shape, came.dtype),
        out_specs=pl.BlockSpec(memory_space=pltpu.VMEM),
        compiler_params=pltpu.CompilerParams(vmem_limit_bytes=LIMIT),
        cost_estimate=cost(3),
    )(offsets, came)


def arrange_kernel(labels, far_labels, groups, parts, info, sums, *refs):
    far, (in_up, out_down, out_up, in_down) = refs[:-4], refs[-4:]
    cols = in_up.shape[1] // groups
    for i, label in enumerate(labels):
        g = info[1 + label["z"] * 2 + label["x"]]
        in_up[:, lanes(g, cols)] = sums[i, :, 0:cols].astype(f32)
    width = far[0].shape[2]
    first, second = out_down.shape[1] // width, out_up.shape[1] // width
    at = 0
    for part in far:
        for i in range(part.shape[0]):
            label = far_labels[at]
            at += 1
            own = info[1 + label["z"] * 2 + label["x"]] * parts + info[1 + groups + label["y"] * 2 + label["c"]]

            @pl.when(own < first)
            def _():
                out_down[:, lanes(own, width)] = part[i, :, :].astype(f32)

            @pl.when((own >= first) & (own < first + second))
            def _():
                out_up[:, lanes(own - first, width)] = part[i, :, :].astype(f32)

            @pl.when(own >= first + second)
            def _():
                in_down[lanes(own - first - second, width), :] = part[i, :, :].astype(f32).T


def call_arrange(info, sums, far_sums, labels, far_labels, groups, parts, inner, width, cols):
    rows = sums.shape[1]
    vmem = pl.BlockSpec(memory_space=pltpu.VMEM)
    shapes = [(rows, 2 * cols), (rows, inner), (rows, width), (width, rows)]
    return pl.pallas_call(
        functools.partial(arrange_kernel, labels, far_labels, groups, parts),
        in_specs=[SMEM, vmem] + [vmem] * len(far_sums),
        out_shape=[jax.ShapeDtypeStruct(s, f32) for s in shapes],
        out_specs=[vmem] * 4,
        compiler_params=pltpu.CompilerParams(vmem_limit_bytes=LIMIT),
        cost_estimate=cost(3),
    )(info, sums, *far_sums)


def moved(block, axis, route):
    size = lax.axis_size(axis)
    return lax.ppermute(block, axis, [(i, route(i, size)) for i in range(size)])


def hop(name, block):
    axis = "dp" if name in "zx" else "tensor"
    if name in "xc":
        return [moved(block, axis, lambda i, n: i ^ 1)]
    return [
        moved(block, axis, functools.partial(lambda k, i, n: (i + 2 * k) % n, k))
        for k in range(1, lax.axis_size(axis) // 2)
    ]


def widened(name, block, labels):
    got = hop(name, block)
    lists = labels + sum([[dict(label, **{name: k + 1}) for label in labels] for k in range(len(got))], [])
    return [block] + got, lists


HERE = dict(z=0, x=0, y=0, c=0)


def tie(first, *others):
    return lax.optimization_barrier((first,) + others)[0]


def index_table(length_of, groups, parts, group, rank):
    dp_from = [((group ^ kx) - 2 * kz) % groups for kz in range(groups // 2) for kx in range(2)]
    part_from = [((rank ^ kc) - 2 * ky) % parts for ky in range(parts // 2) for kc in range(2)]
    partner = [rank ^ k for k in range(parts)]
    return jnp.stack([length_of] + dp_from + part_from + partner).astype(jnp.int32)


def placed(arrays, labels, groups, take, place):
    moves, at = [], 0
    for which, array in enumerate(arrays):
        for index in range(array.shape[0]):
            label = labels[at]
            at += 1
            if label is None:
                continue
            g_at = 1 + label["z"] * 2 + label["x"]
            t_at = 1 + groups + label["y"] * 2 + label["c"]
            moves.append((which, index, take, functools.partial(
                lambda g_at, t_at, info, full: place(info[g_at], info[t_at], full), g_at, t_at)))
    return Pieces(list(arrays), moves)


def paired(arrays, groups, parts, index, place):
    moves = [
        (k, index, None, functools.partial(lambda at, info, full: place(info[at], full), 1 + groups + parts + k))
        for k in range(parts)
    ]
    return Pieces(list(arrays), moves)


def single(array):
    return Pieces([array], [(0, None, None, lambda info, full: full)])


def span(index, size, offset=0, step=None):
    return pl.ds(pl.multiple_of(index * (size if step is None else step) + offset, 16), size)


def lanes(index, size):
    return pl.ds(pl.multiple_of(index * size, size), size)


def exchanged(blocks):
    return [
        block if k == 0 else moved(block, "tensor", functools.partial(lambda k, i, n: i ^ k, k))
        for k, block in enumerate(blocks)
    ]


def on_device(
    tokens, cotangent, destination, lengths, adapter_of, norm_gain, w_zx, w_bc, w_dt, w_out,
    conv_x, conv_bc, dt_bias, a_log, d_skip, out_gain, in_down, in_up, out_down, out_up,
):
    groups, parts = lax.axis_size("dp"), lax.axis_size("tensor")
    group, rank = lax.axis_index("dp"), lax.axis_index("tensor")
    seq_grp, part_len, width = tokens.shape
    rows, _, cols = w_zx.shape
    own_heads = w_dt.shape[1]
    length, inner, heads = part_len * parts, cols * parts, own_heads * parts
    mine = group * seq_grp + rank
    offset = destination[rank] // seq_grp
    adapter = adapter_of[mine] * RANK
    info = index_table(lengths[mine], groups, parts, group, rank)

    def swapped(array, axes="tensor"):
        return lax.all_to_all(array, axes, split_axis=0, concat_axis=0, tiled=True)

    def col_place(t, full):
        return full.at[:, lanes(t, cols)]

    down_in = lax.dynamic_slice_in_dim(in_down, adapter, RANK, 1)
    down_out = lax.dynamic_slice_in_dim(out_down, adapter, RANK, 0)
    up_out = lax.dynamic_slice_in_dim(out_up, adapter, RANK, 0)
    gain = norm_gain.astype(f32)[None]
    convbc = jnp.pad(conv_bc.astype(f32), ((0, 3), (0, 0)))
    head_of = jnp.arange(inner) // (inner // heads)
    spread_heads = (jnp.arange(2 * heads)[:, None] % heads == head_of[None, :]).astype(bf16)
    small_inputs = (info, down_in, gain, convbc, spread_heads)

    head_rows = lax.dynamic_update_slice(jnp.zeros((8, cols), f32), jnp.stack([dt_bias, a_log]), (0, rank * own_heads))
    own_vec = jnp.concatenate([
        conv_x.astype(f32), out_gain.astype(f32)[None], jnp.repeat(d_skip, cols // own_heads)[None],
        jnp.zeros((1, cols), f32), head_rows])

    half, share, two_n = rows // 2, rows // parts, w_bc.shape[1]
    packed = share % 32 == 0 and rows % 128 == 0 and cols == 2 * two_n
    w_x = w_zx[:, 1]
    if packed:
        own_bc = lax.dynamic_slice_in_dim(w_bc, rank * share, share, 0)
        own_bc = jnp.concatenate([own_bc[: share // 2], own_bc[share // 2 :]], axis=1)
        own_dt = jnp.zeros((16, cols), bf16).at[:own_heads, :rows].set(w_dt.T)
        block = jnp.concatenate([w_x[:half], own_bc, w_x[half:], own_dt])
    else:
        block = w_x
    extra = block.shape[0] // 2
    along_z, labels = widened("z", jnp.concatenate([block, w_out])[None], [HERE])
    wz, wz_labels = widened("y", w_zx[:, 0][None], [HERE])
    along_z, wz, token_rows = lax.optimization_barrier((along_z, wz, swapped(tokens)))

    own_vec, in_up = lax.optimization_barrier((own_vec, in_up, along_z))[:2]
    vecs = []
    for k in range(parts):
        theirs = lax.dynamic_slice_in_dim(in_up, adapter_of[group * seq_grp + k] * RANK, RANK, 0)
        vecs.append(jnp.concatenate([own_vec, theirs[:, 1].astype(f32), theirs[:, 0].astype(f32)]))

    first, first_labels = widened("x", jnp.concatenate([a[:, :extra] for a in along_z]), labels)
    second, second_labels = widened("y", jnp.concatenate([a[:, extra : 2 * extra] for a in along_z]), labels)
    wo, wo_labels = jnp.concatenate([a[:, 2 * extra :] for a in along_z]), labels
    wz, wz_labels = widened("z", jnp.concatenate(wz), wz_labels)
    first, second, wz[1], wz[-1], wo, vecs = lax.optimization_barrier((first, second, wz[1], wz[-1], wo, jnp.stack(vecs)))

    vec_rows = swapped(vecs)
    near = len(wz_labels) // len(wz)
    wz_near = jnp.concatenate([wz[0], wz[1], wz[-1]]) if len(wz) > 2 else jnp.concatenate(wz)
    near_labels = wz_labels[: 2 * near] + (wz_labels[-near:] if len(wz) > 2 else [])
    first = jnp.concatenate(first)
    second = jnp.concatenate(second)
    gathered = [first, second] + hop("c", first) + hop("c", second)
    first, far_first_labels = widened("y", first, first_labels)
    second, far_second_labels = widened("x", second, second_labels)
    wz_far, far_labels = wz[2:-1], wz_labels[2 * near : -near]
    first, second, wz_far, wz_near, vec_rows, gathered, small_inputs = lax.optimization_barrier(
        (first[1:], second[1:], wz_far, wz_near, vec_rows, gathered, small_inputs)
    )
    info, down_in, gain, convbc, spread_heads = small_inputs

    both_labels = [first_labels, second_labels]
    both_labels += [[dict(label, c=1) for label in labels] for labels in both_labels]
    halves_of = [0, 1, 0, 1]
    for which, arrays, labels, own in ((0, first, far_first_labels, first_labels), (1, second, far_second_labels, second_labels)):
        labels = labels[len(own) :]
        for at, array in enumerate(arrays):
            part = labels[at * len(own) : (at + 1) * len(own)]
            gathered += [array] + hop("c", array)
            both_labels += [part, [dict(label, c=1) for label in part]]
            halves_of += [which, which]
    x_pieces = single(token_rows.reshape(length, width))
    vec_pieces = Pieces([vec_rows], [
        (0, k, None, functools.partial(lambda k, info, full: full.at[:, pl.ds(k * cols, cols)], k)) for k in range(parts)])

    def of_half(which):
        return sum([labels if which == h else [None] * len(labels) for labels, h in zip(both_labels, halves_of)], [])

    x_weights = placed(
        gathered, of_half(0), groups, (pl.ds(0, half),),
        lambda g, t, full: full.at[span(g, half, 0, rows), lanes(t, cols)],
    )
    x_weights.moves += placed(
        gathered, of_half(1), groups, (pl.ds(0, half),),
        lambda g, t, full: full.at[span(g, half, half, rows), lanes(t, cols)],
    ).moves
    if packed:
        bc_weights = placed(
            gathered, of_half(0), groups, (pl.ds(half, 16), pl.ds(0, two_n)),
            lambda g, t, full: full.at[span(g * parts + t, 16, 0, share), :],
        )
        bc_weights.moves += placed(
            gathered, of_half(0), groups, (pl.ds(half, 16), pl.ds(two_n, two_n)),
            lambda g, t, full: full.at[span(g * parts + t, 16, 16, share), :],
        ).moves
        dt_weights = placed(
            gathered, of_half(1), groups, (pl.ds(half, 16), pl.ds(0, rows)),
            lambda g, t, full: full.at[span(t, 16), lanes(g, rows)],
        )
        bc_weights.arrays, dt_weights.arrays = [], []
    else:
        bc_weights = single(lax.all_gather(w_bc, "dp", axis=0, tiled=True))
        all_dt = lax.all_gather(lax.all_gather(w_dt, "dp", axis=0, tiled=True), "tensor", axis=0)
        all_dt = jnp.pad(all_dt.transpose(0, 2, 1), ((0, 0), (0, 16 - own_heads), (0, 0)))
        dt_weights = single(all_dt.reshape(parts * 16, width))

    wz, wz_labels = widened("x", wz_near, near_labels)
    for at, array in enumerate(wz_far):
        got, labels = widened("x", array, far_labels[at * near : (at + 1) * near])
        wz, wz_labels = wz + got, wz_labels + labels
    by_chip = [(wo, wo_labels), (hop("x", wo)[0], [dict(label, x=1) for label in wo_labels])]
    for k, got in enumerate(hop("y", wo)):
        by_chip.append((got, [dict(label, y=k + 1) for label in wo_labels]))
    for k in range(1, parts // 2):
        got = lax.ppermute(wo, ("dp", "tensor"), [
            (g * parts + t, (g ^ 1) * parts + (t + 2 * k) % parts) for g in range(groups) for t in range(parts)])
        by_chip.append((got, [dict(label, x=1, y=k) for label in wo_labels]))
    wo, wo_labels = [a for a, _ in by_chip], sum([lab for _, lab in by_chip], [])

    def block_place(g, t, full):
        return full.at[span(g, rows), lanes(t, cols)]

    def across_cores(arrays, labels):
        arrays = arrays + [hop("c", a)[0] for a in arrays]
        return placed(arrays, labels + [dict(label, c=1) for label in labels], groups, None, block_place)

    head_sum = (head_of[:, None] == jnp.arange(heads)[None, :]).astype(bf16)

    (x, w_full, bc_full, dt_full, vec, up, normed, low, pre, values, scanned, keys, prebc, scal, states) = call_scan(
        info, gain, down_in, convbc, spread_heads,
        dict(x=x_pieces, w=x_weights, bc=bc_weights, dt=dt_weights, vec=vec_pieces),
        parts, heads, length, width, inner,
    )

    cot_rows = swapped(tie(cotangent, gathered[0]))
    wz, wo, cot_rows, low = lax.optimization_barrier((wz, wo, cot_rows, low))
    cot_pieces = single(cot_rows.reshape(length, width))
    z_weights, o_weights = across_cores(wz, wz_labels), across_cores(wo, wo_labels)
    out = call_gate(
        info, normed, low, scanned, x, vec, down_out, up_out,
        dict(z=z_weights, o=o_weights, cot=cot_pieces), groups, parts,
    )
    mixed, dlayer, dy, side, back, low_back, up_z_part, out_down_part = out

    if mixed.ndim == 2:
        mixed = mixed.reshape(parts, groups, -1, width).transpose(1, 0, 2, 3)
    chunk = mixed.shape[2]
    came = swapped(mixed.reshape(groups * parts, chunk, width), ("dp", "tensor"))

    out = call_back(
        (x, normed, low, dlayer, dy, values, pre, keys, prebc, scal, states, scanned, side, back, low_back),
        (w_full, bc_full, dt_full, vec, up, gain, down_in, convbc, spread_heads, head_sum)
        + (up_z_part, out_down_part), groups, parts, heads,
    )
    came, out = lax.optimization_barrier((came, out))
    token_rows, sums = out[0], out[1:]

    offsets = destination[:seq_grp] // seq_grp
    leave = call_turn(offsets, came.reshape(groups, parts, chunk, width))

    def second_leg(leave):
        return swapped(leave, "dp").transpose(1, 0, 2, 3).reshape(parts, part_len, width)

    token_rows = token_rows.reshape(parts, part_len, width)
    token_grad = exchanged([lax.dynamic_index_in_dim(token_rows, rank ^ k, 0, keepdims=False) for k in range(parts)])

    def stacked(blocks):
        result = jnp.zeros((parts,) + blocks[0].shape, blocks[0].dtype)
        for k, block in enumerate(blocks):
            result = lax.dynamic_update_index_in_dim(result, block, rank ^ k, 0)
        return result

    own = groups * parts
    if len(sums) > 1:

        def at_adapter(part):
            zeros = jnp.zeros((in_down.shape[1], part.shape[1]), bf16)
            return lax.dynamic_update_slice_in_dim(zeros, part.astype(bf16), adapter, 0)

        in_up_grad = [lax.psum_scatter(at_adapter(a), "tensor", scatter_dimension=1, tiled=True) for a in sums[:2]]
        in_up_grad = lax.psum(jnp.stack(in_up_grad, axis=1), "dp").astype(f32)
        others = [at_adapter(a) for a in (out_down_part, sums[2], sums[3])]
        out_down_grad, out_up_grad, in_down_grad = (a.astype(f32) for a in lax.psum(others, ("dp", "tensor")))
        return second_leg(leave), stacked(token_grad), in_down_grad.T, in_up_grad, out_down_grad, out_up_grad

    pooled = swapped(sums[0], ("dp", "tensor"))
    row_of = adapter_of[:, None] * RANK + jnp.arange(RANK)[None, :]
    select = (row_of.reshape(1, -1) == jnp.arange(in_down.shape[1])[:, None]).astype(bf16)
    sums = nn(select, pooled.reshape(own * RANK, -1)).astype(bf16)[None]
    sums, labels = widened("z", sums, [HERE])
    sums, leave = lax.optimization_barrier((sums, leave))
    mixed = second_leg(leave)
    sums, labels = widened("x", jnp.concatenate(sums), labels)
    sums = jnp.concatenate(sums)
    far_sums, far_labels = widened("y", sums[:, :, 2 * cols // groups :], labels)
    far_sums, token_grad = lax.optimization_barrier((jnp.concatenate(far_sums), token_grad))
    far_sums, far_labels = widened("c", far_sums, far_labels)
    in_up_grad, out_down_grad, out_up_grad, in_down_grad = call_arrange(
        info, sums, far_sums, labels, far_labels, groups, parts, inner, width, cols
    )
    in_up_grad = jnp.stack([in_up_grad[:, :cols], in_up_grad[:, cols:]], axis=1)
    return (mixed, stacked(token_grad), in_down_grad, in_up_grad, out_down_grad, out_up_grad)


def solution(mesh):
    return jax.shard_map(
        on_device,
        mesh=mesh,
        in_specs=(
            P("dp", "tensor", None), P("dp", "tensor", None), P(), P(), P(), P(),
            P("dp", None, "tensor"), P("dp", None), P("dp", "tensor"), P("dp", "tensor"),
            P(None, "tensor"), P(), P("tensor"), P("tensor"), P("tensor"), P("tensor"),
            P(), P(None, None, "tensor"), P(), P(),
        ),
        out_specs=(
            P("dp", "tensor", None), P("dp", "tensor", None), P(), P(None, None, "tensor"), P(), P(),
        ),
        check_vma=False,
    )
```

```python
import functools

import jax
import jax.numpy as jnp
from jax import lax
from jax.experimental import pallas as pl
from jax.experimental.pallas import tpu as pltpu
from jax.sharding import PartitionSpec as P

RANK = 16
SCAN = 128
ROWS = 256
TILE = 512
HEAD = 64
EPS = 1e-05
LIMIT = 58 * 1024 * 1024

f32 = jnp.float32
bf16 = jnp.bfloat16
ANY = pl.BlockSpec(memory_space=pl.ANY)
SMEM = pl.BlockSpec(memory_space=pltpu.SMEM)


def nn(a, b):
    return lax.dot_general(a, b, (((1,), (0,)), ((), ())), preferred_element_type=f32)


def nt(a, b):
    return lax.dot_general(a, b, (((1,), (1,)), ((), ())), preferred_element_type=f32)


def tn(a, b):
    return lax.dot_general(a, b, (((0,), (0,)), ((), ())), preferred_element_type=f32)


def exact(a, b):
    return lax.dot_general(
        a, b, (((1,), (0,)), ((), ())), preferred_element_type=f32, precision=lax.Precision.HIGHEST
    )


def halves(v, axis):
    high = v.astype(bf16)
    low = (v - high.astype(f32)).astype(bf16)
    return jnp.concatenate([high, low], axis=axis)


def sigmoid(v):
    return 1.0 / (1.0 + jnp.exp(-v))


def softplus(v):
    return jnp.maximum(v, 0.0) + jnp.log1p(jnp.exp(-jnp.abs(v)))


def triangle(n, lower):
    row = lax.broadcasted_iota(jnp.int32, (n, n), 0)
    col = lax.broadcasted_iota(jnp.int32, (n, n), 1)
    return row >= col if lower else row <= col


def head_vectors(vec, parts):
    width = vec.shape[1] // parts
    total = vec[8:16, 0:128]
    for t in range(1, parts):
        total = total + vec[8:16, t * width : t * width + 128]
    return total


def split_lanes(v):
    low_lanes = lax.broadcasted_iota(jnp.int32, v.shape, 1) < HEAD
    return jnp.where(low_lanes, v, 0.0).astype(bf16), jnp.where(low_lanes, 0.0, v).astype(bf16)


class Pieces:
    def __init__(self, arrays, moves):
        self.arrays, self.moves = arrays, moves


def copy_in(info, groups, sems):
    copies = []
    for refs, moves, full in groups:
        for which, index, take, place in moves:
            src = refs[which]
            if index is not None:
                src = src.at[index]
            if take is not None:
                src = src.at[take]
            copies.append(pltpu.make_async_copy(src, place(info, full), sems.at[len(copies)]))
    for copy in copies:
        copy.start()
    for copy in copies:
        copy.wait()


def whole_block(shape):
    return pl.BlockSpec(shape, lambda c: (0,) * len(shape))


def row_block(width, rows=ROWS):
    return pl.BlockSpec((rows, width), lambda c: (c, 0))


def take_refs(refs, counts):
    taken, at = [], 0
    for count in counts:
        taken.append(refs[at : at + count])
        at += count
    return taken, refs[at:]


def gathered_operands(names, pieces):
    owners, lists, arrays, counts = [], [], [], []
    for i, name in enumerate(names):
        owners.append(i if pieces[name].arrays else owners[-1])
        lists.append(pieces[name].moves)
        arrays += pieces[name].arrays
        counts.append(len(pieces[name].arrays))
    return (owners, lists), arrays, counts, sum(len(m) for m in lists)


def cost(micros):
    return pl.CostEstimate(flops=int(micros * 1.1e9), bytes_accessed=1 << 20, transcendentals=0)


def scan_kernel(names, moves, counts, parts, heads, *refs):
    info, gain, in_down, convbc, spread_heads = refs[:5]
    groups, rest = take_refs(refs[5:], counts)
    (x_out, w_full, bc_full, dt_full, vec, up, normed_out, low_out, slope_out, values_out, scanned_out) = rest[:11]
    (keys_out, prebc_out, scal_out, states_out, vec_low, xs, dt_wide, xbuf, bcbuf, state, sems) = rest[11:]
    fulls = dict(x=xs, w=w_full, bc=bc_full, dt=dt_wide, vec=vec_low)
    c = pl.program_id(0)
    inner = w_full.shape[1]
    subs = ROWS // SCAN

    @pl.when(c == 0)
    def _():
        copy_in(info, [(groups[g], m, fulls[name]) for name, g, m in zip(names, moves[0], moves[1])], sems)
        state[...] = jnp.zeros_like(state)
        xbuf[0:8, :] = jnp.zeros((8, inner), f32)
        bcbuf[0:8, :] = jnp.zeros((8, bcbuf.shape[1]), f32)
        vec[16:, :] = vec_low[16:, :].astype(f32)
        top = vec_low[0:16, :].astype(f32)
        skip, bias, decay = (top[n : n + 1] + top[n + 1 : n + 2] + top[n + 2 : n + 3] for n in (6, 9, 12))
        vec[0:16, :] = jnp.concatenate([top[0:6], skip, jnp.zeros_like(skip), bias, decay, jnp.zeros((6, inner), f32)], axis=0)
        up[...] = vec_low[16 : 16 + RANK, :]
        own = heads // parts
        dt_full[...] = jnp.concatenate(
            [dt_wide[16 * t : 16 * t + 16, :].astype(f32)[:own] for t in range(parts)], axis=0
        ).astype(bf16)

    x_low = xs[pl.ds(pl.multiple_of(c * ROWS, ROWS), ROWS), :]
    x_out[...] = x_low
    x = x_low.astype(f32)
    rms = lax.rsqrt(jnp.mean(x * x, axis=1, keepdims=True) + EPS)
    normed_out[...] = (x * rms * gain[...]).astype(bf16)
    low_out[...] = nn(normed_out[...], in_down[...]).astype(bf16)
    hv = head_vectors(vec, parts)
    bias, rate = hv[0:1, 0:heads], -jnp.exp(hv[1:2, 0:heads])

    bcbuf[8:, :] = nn(normed_out[...], bc_full[...])
    pre = convbc[4:5, :] + sum(convbc[k : k + 1, :] * bcbuf[5 + k : 5 + k + ROWS, :] for k in range(4))
    bcbuf[0:8, :] = bcbuf[ROWS : ROWS + 8, :]
    prebc_out[...] = pre
    keys_out[...] = (pre * sigmoid(pre)).astype(bf16)
    nstate = keys_out.shape[1] // 2

    raw = nt(normed_out[...], dt_full[...]) + bias
    steps = softplus(raw)
    lower = triangle(SCAN, True)
    lower_f = lower.astype(f32)
    cums, cum_rows, grown, scores, key_cols = [], [], [], [], []
    for s in range(subs):
        rows = slice(s * SCAN, (s + 1) * SCAN)
        dt_s = steps[rows]
        cum = exact(lower_f, dt_s * rate)
        cums.append(cum)
        cum_rows.append(cum.T)
        b_part, c_part = keys_out[rows, 0:nstate], keys_out[rows, nstate:]
        scores.append(jnp.where(lower, nt(c_part, b_part), 0.0))
        key_cols.append(b_part.astype(f32).T.astype(bf16))
        tail = jnp.exp(cum[SCAN - 1 : SCAN, :] - cum)
        grown.append((halves(dt_s, 1), halves(jnp.exp(cum), 1), halves(dt_s * tail, 1)))
    scal_out[...] = jnp.concatenate(
        [steps, jnp.concatenate(cums, axis=0), sigmoid(raw), jnp.zeros((ROWS, 128 - 3 * heads), f32)], axis=1
    )

    for j in range(inner // TILE):
        cols = slice(j * TILE, (j + 1) * TILE)
        xbuf[8:, cols] = nn(normed_out[...], w_full[:, cols]) + nn(low_out[...], up[:, cols])
        halo = xbuf[:, cols]
        pre = vec[4:5, cols] + vec[3:4, cols] * halo[8:]
        pre = pre + sum(vec[k : k + 1, cols] * pltpu.roll(halo, 3 - k, 0)[8:] for k in range(3))
        xbuf[0:8, cols] = xbuf[ROWS : ROWS + 8, cols]
        sig = sigmoid(pre)
        values_out[:, cols] = (pre * sig).astype(bf16)
        slope_out[:, cols] = (sig * (1.0 + pre * (1.0 - sig))).astype(bf16)
        for s in range(subs):
            rows = slice(s * SCAN, (s + 1) * SCAN)
            dtx, ecx, tlx = (nn(v, spread_heads[:, cols]) for v in grown[s])
            state_low = state[:, cols].astype(bf16)
            states_out[s, :, cols] = state_low
            v = values_out[rows, cols].astype(f32)
            y = ecx * nn(keys_out[rows, nstate:], state_low) + vec[6:7, cols] * v
            vw = v * dtx
            within = []
            for p in range(TILE // 128):
                lhs = []
                for a in range(2):
                    h = (j * TILE + p * 128) // HEAD + a
                    gap = cums[s][:, h : h + 1] - cum_rows[s][h : h + 1, :]
                    lhs.append((jnp.exp(jnp.minimum(gap, 0.0)) * scores[s]).astype(bf16))
                rhs = jnp.concatenate(split_lanes(vw[:, p * 128 : (p + 1) * 128]), axis=0)
                within.append(nn(jnp.concatenate(lhs, axis=1), rhs))
            scanned_out[rows, cols] = y + jnp.concatenate(within, axis=1)
            state[:, cols] = ecx[SCAN - 1 : SCAN, :] * state[:, cols] + nn(key_cols[s], (v * tlx).astype(bf16))


def call_scan(info, gain, in_down, convbc, spread_heads, pieces, parts, heads, length, width, inner):
    names = ("x", "w", "bc", "dt", "vec")
    moves, arrays, counts, total = gathered_operands(names, pieces)
    two_n = convbc.shape[1]
    steps, subs = length // ROWS, ROWS // SCAN
    shapes = [
        ((length, width), bf16), ((width, inner), bf16), ((width, two_n), bf16), ((heads, width), bf16),
        ((16 + 2 * RANK, inner), f32), ((RANK, inner), bf16), ((length, width), bf16), ((length, RANK), bf16),
        ((length, inner), bf16), ((length, inner), bf16), ((length, inner), f32), ((length, two_n), bf16),
        ((length, two_n), f32), ((length, 128), f32), ((length // SCAN, two_n // 2, inner), bf16),
    ]
    specs = [
        row_block(width), whole_block((width, inner)), whole_block((width, two_n)), whole_block((heads, width)),
        whole_block((16 + 2 * RANK, inner)), whole_block((RANK, inner)), row_block(width), row_block(RANK),
        row_block(inner), row_block(inner), row_block(inner), row_block(two_n),
        row_block(two_n), row_block(128), pl.BlockSpec((subs, two_n // 2, inner), lambda c: (c, 0, 0)),
    ]
    return pl.pallas_call(
        functools.partial(scan_kernel, names, moves, counts, parts, heads),
        grid=(steps,),
        in_specs=[SMEM, whole_block(gain.shape), whole_block(in_down.shape), whole_block(convbc.shape)]
        + [whole_block(spread_heads.shape)] + [ANY] * len(arrays),
        out_shape=[jax.ShapeDtypeStruct(s, d) for s, d in shapes],
        out_specs=specs,
        scratch_shapes=[
            pltpu.VMEM((16 + 2 * RANK, inner), bf16),
            pltpu.VMEM((length, width), bf16), pltpu.VMEM((parts * 16, width), bf16),
            pltpu.VMEM((ROWS + 8, inner), f32), pltpu.VMEM((ROWS + 8, two_n), f32),
            pltpu.VMEM((two_n // 2, inner), f32), pltpu.SemaphoreType.DMA((total,)),
        ],
        compiler_params=pltpu.CompilerParams(vmem_limit_bytes=LIMIT, dimension_semantics=("arbitrary",)),
        cost_estimate=cost(44),
    )(info, gain, in_down, convbc, spread_heads, *arrays)


def gate_kernel(names, moves, counts, *refs):
    info, normed, low, scanned, x, vec, out_down, out_up = refs[:8]
    groups, rest = take_refs(refs[8:], counts)
    (mixed_out, dlayer_out, dy_out, side_out, zg, low_back_out, in_up_out, out_down_out, wz) = rest[:9]
    (wo, upz, cots, z, gi, gated, gg, sems) = rest[9:]
    fulls = dict(z=wz, o=wo, cot=cots)
    c = pl.program_id(0)
    inner = wz.shape[1]
    tiles = [slice(j * TILE, (j + 1) * TILE) for j in range(inner // TILE)]

    @pl.when(c == 0)
    def _():
        copy_in(info, [(groups[g], m, fulls[name]) for name, g, m in zip(names, moves[0], moves[1])], sems)
        upz[...] = vec[16 + RANK : 16 + 2 * RANK, :].astype(bf16)
        in_up_out[...] = jnp.zeros_like(in_up_out)
        out_down_out[...] = jnp.zeros_like(out_down_out)

    squares = jnp.zeros((ROWS, 128), f32)
    for cols in tiles:
        zj = nn(normed[...], wz[:, cols]) + nn(low[...], upz[:, cols])
        z[:, cols] = zj
        g = scanned[:, cols] * (zj * sigmoid(zj))
        gi[:, cols] = g
        g = g * g
        squares = squares + sum(g[:, k : k + 128] for k in range(0, TILE, 128))
    scale = lax.rsqrt(jnp.sum(squares, axis=1, keepdims=True) / inner + EPS)
    for cols in tiles:
        gated[:, cols] = (gi[:, cols] * scale * vec[5:6, cols]).astype(bf16)
    side = nt(gated[...], out_down[...]).astype(bf16)
    side_out[...] = side
    terms = nt(gated[...], wo[...]) + nn(side, out_up[...])
    live = lax.broadcasted_iota(jnp.int32, (ROWS, 1), 0) + c * ROWS < info[0]
    mixed = jnp.where(live, x[...].astype(f32) + terms, 0.0).astype(bf16)
    if len(mixed_out.shape) == 2:
        mixed_out[...] = mixed
    else:
        chunk = mixed_out.shape[2]
        for j in range(mixed_out.shape[0]):
            mixed_out[j, 0, :, :] = mixed[j * chunk : (j + 1) * chunk, :]
    cot = cots[pl.ds(pl.multiple_of(c * ROWS, ROWS), ROWS), :]
    dlayer_out[...] = jnp.where(live, cot.astype(f32), 0.0).astype(bf16)
    side_grad = nt(dlayer_out[...], out_up[...]).astype(bf16)
    products = jnp.zeros((ROWS, 128), f32)
    for cols in tiles:
        grad = (nn(dlayer_out[...], wo[:, cols]) + nn(side_grad, out_down[:, cols])).astype(bf16)
        gg[:, cols] = grad
        g = grad.astype(f32) * vec[5:6, cols] * gi[:, cols]
        products = products + sum(g[:, k : k + 128] for k in range(0, TILE, 128))
    factor = scale * scale * scale * (jnp.sum(products, axis=1, keepdims=True) / inner)
    for cols in tiles:
        grad = scale * (gg[:, cols].astype(f32) * vec[5:6, cols]) - gi[:, cols] * factor
        zj = z[:, cols]
        sig = sigmoid(zj)
        sc = scanned[:, cols].astype(f32)
        dy = (grad * (zj * sig)).astype(bf16)
        dy_out[:, cols] = dy
        zg[:, cols] = (grad * sc * (sig * (1.0 + zj * (1.0 - sig)))).astype(bf16)
    low_back_out[...] = nt(zg[...], upz[...])
    in_up_out[...] += tn(low[...], zg[...])
    out_down_out[...] += tn(side_grad, gated[...])


def call_gate(info, normed, low, scanned, x, vec, out_down, out_up, pieces, groups, parts):
    names = ("z", "o", "cot")
    moves, arrays, counts, total = gathered_operands(names, pieces)
    length, width = x.shape
    inner = scanned.shape[1]
    chunk = length // (groups * parts)
    if chunk % 16 == 0 and length // parts == ROWS:
        leaving = ((groups, parts, chunk, width), pl.BlockSpec((groups, 1, chunk, width), lambda c: (0, c, 0, 0)))
    else:
        leaving = ((length, width), row_block(width))
    shapes = [
        (leaving[0], bf16), ((length, width), bf16), ((length, inner), bf16), ((length, RANK), bf16),
        ((length, inner), bf16), ((length, RANK), f32), ((RANK, inner), f32), ((RANK, inner), f32),
        ((width, inner), bf16),
    ]
    specs = [
        leaving[1], row_block(width), row_block(inner), row_block(RANK), row_block(inner), row_block(RANK),
        whole_block((RANK, inner)), whole_block((RANK, inner)), whole_block((width, inner)),
    ]
    return pl.pallas_call(
        functools.partial(gate_kernel, names, moves, counts),
        grid=(length // ROWS,),
        in_specs=[SMEM, row_block(width), row_block(RANK), row_block(inner), row_block(width), whole_block(vec.shape)]
        + [whole_block(out_down.shape), whole_block(out_up.shape)] + [ANY] * len(arrays),
        out_shape=[jax.ShapeDtypeStruct(s, d) for s, d in shapes],
        out_specs=specs,
        scratch_shapes=[
            pltpu.VMEM((width, inner), bf16), pltpu.VMEM((RANK, inner), bf16), pltpu.VMEM((length, width), bf16),
            pltpu.VMEM((ROWS, inner), f32), pltpu.VMEM((ROWS, inner), f32), pltpu.VMEM((ROWS, inner), bf16),
            pltpu.VMEM((ROWS, inner), bf16), pltpu.SemaphoreType.DMA((total,)),
        ],
        compiler_params=pltpu.CompilerParams(vmem_limit_bytes=LIMIT, dimension_semantics=("arbitrary",)),
        cost_estimate=cost(43),
    )(info, normed, low, scanned, x, vec, out_down, out_up, *arrays)


def back_kernel(groups, parts, heads, *refs):
    (x, normed, low, dlayer, dy, values, slope, keys, prebc, scal, states, scanned, side, zg, low_back) = refs[:15]
    (w_full, wz, bc_full, dt_full, vec, up, gain, in_down, convbc, spread_heads, head_sum) = refs[15:26]
    (in_up_z, out_down, grad_out) = refs[26:29]
    outs, (in_up_x, out_up, in_down_sum, dstate, xbuf, bcbuf, xg, summed) = refs[29:-8], refs[-8:]
    i = pl.program_id(0)
    inner = w_full.shape[1]
    subs = ROWS // SCAN
    nstate = keys.shape[1] // 2
    tiles = [slice(j * TILE, (j + 1) * TILE) for j in range(inner // TILE)]

    @pl.when(i == 0)
    def _():
        dstate[...] = jnp.zeros_like(dstate)
        xbuf[ROWS:, :] = jnp.zeros((8, inner), f32)
        bcbuf[ROWS:, :] = jnp.zeros((8, bcbuf.shape[1]), f32)
        summed[...] = jnp.zeros_like(summed)
        for total in (in_up_x, out_up, in_down_sum):
            total[...] = jnp.zeros_like(total)

    hv = head_vectors(vec, parts)
    rate = -jnp.exp(hv[1:2, 0:heads])
    upper = triangle(SCAN, False)
    upper_f = upper.astype(f32)
    raw_parts = [None] * subs
    for s in reversed(range(subs)):
        rows = slice(s * SCAN, (s + 1) * SCAN)
        steps, cum = scal[rows, 0:heads], scal[rows, heads : 2 * heads]
        cum_row = cum.T
        last = cum[SCAN - 1 : SCAN, :]
        dt2, ecum2, tail2 = halves(steps, 1), halves(jnp.exp(cum), 1), halves(jnp.exp(last - cum), 1)
        b_part, c_part = keys[rows, 0:nstate], keys[rows, nstate:]
        c_cols = c_part.astype(f32).T.astype(bf16)
        scores = jnp.where(upper, nt(b_part, c_part), 0.0)
        pulled = jnp.zeros((SCAN, SCAN), f32)
        c_grad = jnp.zeros((SCAN, nstate), f32)
        b_grad = jnp.zeros((SCAN, nstate), f32)
        direct = jnp.zeros((SCAN, heads), f32)
        change = jnp.zeros((SCAN, heads), f32)
        for j, cols in enumerate(tiles):
            dtx, ecx, tlx = (nn(v, spread_heads[:, cols]) for v in (dt2, ecum2, tail2))
            g_low = dy[rows, cols]
            g = g_low.astype(f32)
            v = values[rows, cols].astype(f32)
            vw = v * dtx
            dstate_low = dstate[:, cols].astype(bf16)
            within = []
            for p in range(TILE // 128):
                part = slice(p * 128, (p + 1) * 128)
                vw_split = split_lanes(vw[:, part])
                lhs = []
                for a in range(2):
                    h = (j * TILE + p * 128) // HEAD + a
                    gap = cum_row[h : h + 1, :] - cum[:, h : h + 1]
                    decay = jnp.exp(jnp.minimum(gap, 0.0))
                    pulled = pulled + decay * nt(vw_split[a], g_low[:, part])
                    lhs.append((decay * scores).astype(bf16))
                rhs = jnp.concatenate(split_lanes(g[:, part]), axis=0)
                within.append(nn(jnp.concatenate(lhs, axis=1), rhs))
            dvw = jnp.concatenate(within, axis=1) + tlx * nn(b_part, dstate_low)
            vg = dtx * dvw + vec[6:7, cols] * g
            summer = head_sum[cols, :]
            direct = direct + nn((v * dvw).astype(bf16), summer)
            summer = jnp.concatenate([summer, summer], axis=0)
            change = change + nn(halves(g * scanned[rows, cols] - v * vg, 1), summer)
            ge = (ecx * g).astype(bf16)
            c_grad = c_grad + nt(ge, states[s, :, cols])
            b_grad = b_grad + nt((tlx * vw).astype(bf16), dstate_low)
            dstate[:, cols] = ecx[SCAN - 1 : SCAN, :] * dstate[:, cols] + nn(c_cols, ge)
            xbuf[rows, cols] = vg * slope[rows, cols].astype(f32)
        pulled = jnp.where(upper, pulled, 0.0)
        b_grad = b_grad + nn(pulled.astype(bf16), c_part)
        c_grad = c_grad + nn(pulled.T.astype(bf16), b_part)
        pb = prebc[rows, :]
        sig = sigmoid(pb)
        bcbuf[rows, :] = jnp.concatenate([b_grad, c_grad], axis=1) * (sig * (1.0 + pb * (1.0 - sig)))
        later = exact(upper_f, change) + summed[0:1, 0:heads]
        summed[0:1, 0:heads] = later[0:1, :]
        raw_parts[s] = (direct + rate * later) * scal[rows, 2 * heads : 3 * heads]
    raw_grad = jnp.concatenate(raw_parts, axis=0).astype(bf16)

    for cols in tiles:
        halo = xbuf[:, cols]
        total = vec[3:4, cols] * halo[:ROWS]
        total = total + sum(vec[k : k + 1, cols] * pltpu.roll(halo, ROWS + 5 + k, 0)[:ROWS] for k in range(3))
        xg[:, cols] = total.astype(bf16)
    xbuf[ROWS:, :] = xbuf[0:8, :]
    bc_grad = sum(convbc[k : k + 1, :] * bcbuf[3 - k : 3 - k + ROWS, :] for k in range(4)).astype(bf16)
    bcbuf[ROWS:, :] = bcbuf[0:8, :]
    low_grad = (low_back[...] + nt(xg[...], up[...])).astype(bf16)
    in_up_x[...] += tn(low[...], xg[...])
    out_up[...] += tn(side[...], dlayer[...])
    in_down_sum[...] += tn(low_grad, normed[...])
    ng = nt(zg[...], wz[...]) + nt(xg[...], w_full[...]) + nt(bc_grad, bc_full[...])
    ng = ng + nn(raw_grad, dt_full[...]) + nt(low_grad, in_down[...])
    xv = x[...].astype(f32)
    rms = lax.rsqrt(jnp.mean(xv * xv, axis=1, keepdims=True) + EPS)
    ng = ng * gain[...]
    inner_norm = jnp.mean(ng * xv, axis=1, keepdims=True)
    grad_out[...] = (dlayer[...].astype(f32) + rms * ng - xv * (rms * rms * rms * inner_norm)).astype(bf16)


    @pl.when(i == pl.num_programs(0) - 1)
    def _():
        if len(outs) > 1:
            for out, total in zip(outs, (in_up_z, in_up_x, out_up, in_down_sum)):
                out[...] = total[...].astype(bf16)
            return
        (shares,) = outs
        cols = inner // parts
        for g in range(groups):
            for t in range(parts):
                own = g * parts + t
                at = g * 2 * cols // groups
                total = in_up_z if at < cols else in_up_x
                at = at % cols + t * cols
                wide = 2 * cols // groups
                shares[own, :, 0:wide] = total[:, at : at + wide].astype(bf16)
                other = shares.shape[2] - wide
                at = own * other
                for total in (out_down, out_up, in_down_sum):
                    if 0 <= at < total.shape[1]:
                        shares[own, :, wide:] = total[:, at : at + other].astype(bf16)
                    at = at - total.shape[1]


def shares_of(groups, parts, inner, width):
    ups, others = 2 * inner // (groups * parts), (inner + 2 * width) // (groups * parts)
    return None if ups % 128 or others % 128 or width % others or inner % others else ups + others


def call_back(rows_in, consts, groups, parts, heads):
    x = rows_in[0]
    length, width = x.shape
    inner = rows_in[4].shape[1]
    two_n = rows_in[7].shape[1]
    steps, subs = length // ROWS, ROWS // SCAN
    shares = shares_of(groups, parts, inner, width)
    if shares is None:
        sums = [(RANK, inner), (RANK, inner), (RANK, width), (RANK, width)]
    else:
        sums = [(groups * parts, RANK, shares)]

    def spec(a):
        if a.ndim == 3:
            return pl.BlockSpec((subs,) + a.shape[1:], lambda i: (steps - 1 - i, 0, 0))
        return pl.BlockSpec((ROWS, a.shape[1]), lambda i: (steps - 1 - i, 0))

    return pl.pallas_call(
        functools.partial(back_kernel, groups, parts, heads),
        grid=(steps,),
        in_specs=[spec(a) for a in rows_in] + [whole_block(a.shape) for a in consts],
        out_shape=[jax.ShapeDtypeStruct((length, width), bf16)] + [jax.ShapeDtypeStruct(s, bf16) for s in sums],
        out_specs=[spec(x)] + [whole_block(s) for s in sums],
        scratch_shapes=[
            pltpu.VMEM((RANK, inner), f32), pltpu.VMEM((RANK, width), f32), pltpu.VMEM((RANK, width), f32),
            pltpu.VMEM((two_n // 2, inner), f32),
            pltpu.VMEM((ROWS + 8, inner), f32), pltpu.VMEM((ROWS + 8, two_n), f32), pltpu.VMEM((ROWS, inner), bf16),
            pltpu.VMEM((8, 128), f32),
        ],
        compiler_params=pltpu.CompilerParams(vmem_limit_bytes=LIMIT, dimension_semantics=("arbitrary",)),
        cost_estimate=cost(50),
    )(*rows_in, *consts)


def turn_kernel(info, came, leave):
    groups, parts = came.shape[:2]
    for p in range(parts):
        for d in range(groups):
            leave[d, p, :, :] = came[lax.rem(d + groups - info[p], groups), p, :, :]


def call_turn(offsets, came):
    return pl.pallas_call(
        turn_kernel,
        in_specs=[SMEM, pl.BlockSpec(memory_space=pltpu.VMEM)],
        out_shape=jax.ShapeDtypeStruct(came.shape, came.dtype),
        out_specs=pl.BlockSpec(memory_space=pltpu.VMEM),
        compiler_params=pltpu.CompilerParams(vmem_limit_bytes=LIMIT),
        cost_estimate=cost(3),
    )(offsets, came)


def arrange_kernel(labels, far_labels, groups, parts, info, sums, *refs):
    far, (in_up, out_down, out_up, in_down) = refs[:-4], refs[-4:]
    cols = in_up.shape[1] // groups
    for i, label in enumerate(labels):
        g = info[1 + label["z"] * 2 + label["x"]]
        in_up[:, lanes(g, cols)] = sums[i, :, 0:cols].astype(f32)
    width = far[0].shape[2]
    first, second = out_down.shape[1] // width, out_up.shape[1] // width
    at = 0
    for part in far:
        for i in range(part.shape[0]):
            label = far_labels[at]
            at += 1
            own = info[1 + label["z"] * 2 + label["x"]] * parts + info[1 + groups + label["y"] * 2 + label["c"]]

            @pl.when(own < first)
            def _():
                out_down[:, lanes(own, width)] = part[i, :, :].astype(f32)

            @pl.when((own >= first) & (own < first + second))
            def _():
                out_up[:, lanes(own - first, width)] = part[i, :, :].astype(f32)

            @pl.when(own >= first + second)
            def _():
                in_down[lanes(own - first - second, width), :] = part[i, :, :].astype(f32).T


def call_arrange(info, sums, far_sums, labels, far_labels, groups, parts, inner, width, cols):
    rows = sums.shape[1]
    vmem = pl.BlockSpec(memory_space=pltpu.VMEM)
    shapes = [(rows, 2 * cols), (rows, inner), (rows, width), (width, rows)]
    return pl.pallas_call(
        functools.partial(arrange_kernel, labels, far_labels, groups, parts),
        in_specs=[SMEM, vmem] + [vmem] * len(far_sums),
        out_shape=[jax.ShapeDtypeStruct(s, f32) for s in shapes],
        out_specs=[vmem] * 4,
        compiler_params=pltpu.CompilerParams(vmem_limit_bytes=LIMIT),
        cost_estimate=cost(3),
    )(info, sums, *far_sums)


def moved(block, axis, route):
    size = lax.axis_size(axis)
    return lax.ppermute(block, axis, [(i, route(i, size)) for i in range(size)])


def hop(name, block):
    axis = "dp" if name in "zx" else "tensor"
    if name in "xc":
        return [moved(block, axis, lambda i, n: i ^ 1)]
    return [
        moved(block, axis, functools.partial(lambda k, i, n: (i + 2 * k) % n, k))
        for k in range(1, lax.axis_size(axis) // 2)
    ]


def widened(name, block, labels):
    got = hop(name, block)
    lists = labels + sum([[dict(label, **{name: k + 1}) for label in labels] for k in range(len(got))], [])
    return [block] + got, lists


HERE = dict(z=0, x=0, y=0, c=0)


def tie(first, *others):
    return lax.optimization_barrier((first,) + others)[0]


def index_table(length_of, groups, parts, group, rank):
    dp_from = [((group ^ kx) - 2 * kz) % groups for kz in range(groups // 2) for kx in range(2)]
    part_from = [((rank ^ kc) - 2 * ky) % parts for ky in range(parts // 2) for kc in range(2)]
    partner = [rank ^ k for k in range(parts)]
    return jnp.stack([length_of] + dp_from + part_from + partner).astype(jnp.int32)


def placed(arrays, labels, groups, take, place):
    moves, at = [], 0
    for which, array in enumerate(arrays):
        for index in range(array.shape[0]):
            label = labels[at]
            at += 1
            if label is None:
                continue
            g_at = 1 + label["z"] * 2 + label["x"]
            t_at = 1 + groups + label["y"] * 2 + label["c"]
            moves.append((which, index, take, functools.partial(
                lambda g_at, t_at, info, full: place(info[g_at], info[t_at], full), g_at, t_at)))
    return Pieces(list(arrays), moves)


def paired(arrays, groups, parts, index, place):
    moves = [
        (k, index, None, functools.partial(lambda at, info, full: place(info[at], full), 1 + groups + parts + k))
        for k in range(parts)
    ]
    return Pieces(list(arrays), moves)


def single(array):
    return Pieces([array], [(0, None, None, lambda info, full: full)])


def span(index, size, offset=0, step=None):
    return pl.ds(pl.multiple_of(index * (size if step is None else step) + offset, 16), size)


def lanes(index, size):
    return pl.ds(pl.multiple_of(index * size, size), size)


def exchanged(blocks):
    return [
        block if k == 0 else moved(block, "tensor", functools.partial(lambda k, i, n: i ^ k, k))
        for k, block in enumerate(blocks)
    ]


def on_device(
    tokens, cotangent, destination, lengths, adapter_of, norm_gain, w_zx, w_bc, w_dt, w_out,
    conv_x, conv_bc, dt_bias, a_log, d_skip, out_gain, in_down, in_up, out_down, out_up,
):
    groups, parts = lax.axis_size("dp"), lax.axis_size("tensor")
    group, rank = lax.axis_index("dp"), lax.axis_index("tensor")
    seq_grp, part_len, width = tokens.shape
    rows, _, cols = w_zx.shape
    own_heads = w_dt.shape[1]
    length, inner, heads = part_len * parts, cols * parts, own_heads * parts
    mine = group * seq_grp + rank
    offset = destination[rank] // seq_grp
    adapter = adapter_of[mine] * RANK
    info = index_table(lengths[mine], groups, parts, group, rank)

    def swapped(array, axes="tensor"):
        return lax.all_to_all(array, axes, split_axis=0, concat_axis=0, tiled=True)

    def col_place(t, full):
        return full.at[:, lanes(t, cols)]

    down_in = lax.dynamic_slice_in_dim(in_down, adapter, RANK, 1)
    down_out = lax.dynamic_slice_in_dim(out_down, adapter, RANK, 0)
    up_out = lax.dynamic_slice_in_dim(out_up, adapter, RANK, 0)
    gain = norm_gain.astype(f32)[None]
    convbc = jnp.pad(conv_bc.astype(f32), ((0, 3), (0, 0)))
    head_of = jnp.arange(inner) // (inner // heads)
    spread_heads = (jnp.arange(2 * heads)[:, None] % heads == head_of[None, :]).astype(bf16)
    small_inputs = (info, down_in, gain, convbc, spread_heads)

    head_rows = lax.dynamic_update_slice(jnp.zeros((2, cols), f32), jnp.stack([dt_bias, a_log]), (0, rank * own_heads))
    exact_rows = jnp.concatenate([jnp.repeat(d_skip, cols // own_heads)[None], head_rows])
    high = lax.reduce_precision(exact_rows, 8, 7)
    middle = lax.reduce_precision(exact_rows - high, 8, 7)
    thirds = jnp.stack([high, middle, exact_rows - high - middle], axis=1).astype(bf16).reshape(9, cols)
    own_vec = jnp.concatenate([
        conv_x, out_gain[None], thirds, jnp.zeros((1, cols), bf16)])

    half, share, two_n = rows // 2, rows // parts, w_bc.shape[1]
    packed = share % 32 == 0 and rows % 128 == 0 and cols == 2 * two_n
    w_x = w_zx[:, 1]
    if packed:
        own_bc = lax.dynamic_slice_in_dim(w_bc, rank * share, share, 0)
        own_bc = jnp.concatenate([own_bc[: share // 2], own_bc[share // 2 :]], axis=1)
        own_dt = jnp.zeros((16, cols), bf16).at[:own_heads, :rows].set(w_dt.T)
        block = jnp.concatenate([w_x[:half], own_bc, w_x[half:], own_dt])
    else:
        block = w_x
    extra = block.shape[0] // 2
    along_z, labels = widened("z", jnp.concatenate([block, w_out])[None], [HERE])
    wz, wz_labels = widened("y", w_zx[:, 0][None], [HERE])
    along_z, wz, token_rows = lax.optimization_barrier((along_z, wz, swapped(tokens)))

    own_vec, in_up = lax.optimization_barrier((own_vec, in_up, along_z))[:2]
    vecs = []
    for k in range(parts):
        theirs = lax.dynamic_slice_in_dim(in_up, adapter_of[group * seq_grp + k] * RANK, RANK, 0)
        vecs.append(jnp.concatenate([own_vec, theirs[:, 1], theirs[:, 0]]))

    first = jnp.concatenate([a[:, :extra] for a in along_z])
    second = jnp.concatenate([a[:, extra : 2 * extra] for a in along_z])
    first, second, wz = lax.optimization_barrier((first, second, jnp.concatenate(wz)))
    first, first_labels = widened("x", first, labels)
    second, second_labels = widened("y", second, labels)
    wo, wo_labels = jnp.concatenate([a[:, 2 * extra :] for a in along_z]), labels
    wz, wz_labels = widened("z", wz, wz_labels)
    first, second, wz[1], wz[-1], wo, vecs = lax.optimization_barrier((first, second, wz[1], wz[-1], wo, jnp.stack(vecs)))

    vec_rows = swapped(vecs)
    near = len(wz_labels) // len(wz)
    wz_near = jnp.concatenate([wz[0], wz[1], wz[-1]]) if len(wz) > 2 else jnp.concatenate(wz)
    near_labels = wz_labels[: 2 * near] + (wz_labels[-near:] if len(wz) > 2 else [])
    first = jnp.concatenate(first)
    second = jnp.concatenate(second)
    gathered = [first, second] + hop("c", first) + hop("c", second)
    first, far_first_labels = widened("y", first, first_labels)
    second, far_second_labels = widened("x", second, second_labels)
    wz_far, far_labels = wz[2:-1], wz_labels[2 * near : -near]
    first, second, wz_far, wz_near, vec_rows, gathered, small_inputs = lax.optimization_barrier(
        (first[1:], second[1:], wz_far, wz_near, vec_rows, gathered, small_inputs)
    )
    info, down_in, gain, convbc, spread_heads = small_inputs

    both_labels = [first_labels, second_labels]
    both_labels += [[dict(label, c=1) for label in labels] for labels in both_labels]
    halves_of = [0, 1, 0, 1]
    for which, arrays, labels, own in ((0, first, far_first_labels, first_labels), (1, second, far_second_labels, second_labels)):
        labels = labels[len(own) :]
        for at, array in enumerate(arrays):
            part = labels[at * len(own) : (at + 1) * len(own)]
            gathered += [array] + hop("c", array)
            both_labels += [part, [dict(label, c=1) for label in part]]
            halves_of += [which, which]
    x_pieces = single(token_rows.reshape(length, width))
    vec_pieces = Pieces([vec_rows], [
        (0, k, None, functools.partial(lambda k, info, full: full.at[:, pl.ds(k * cols, cols)], k)) for k in range(parts)])

    def of_half(which):
        return sum([labels if which == h else [None] * len(labels) for labels, h in zip(both_labels, halves_of)], [])

    x_weights = placed(
        gathered, of_half(0), groups, (pl.ds(0, half),),
        lambda g, t, full: full.at[span(g, half, 0, rows), lanes(t, cols)],
    )
    x_weights.moves += placed(
        gathered, of_half(1), groups, (pl.ds(0, half),),
        lambda g, t, full: full.at[span(g, half, half, rows), lanes(t, cols)],
    ).moves
    if packed:
        bc_weights = placed(
            gathered, of_half(0), groups, (pl.ds(half, 16), pl.ds(0, two_n)),
            lambda g, t, full: full.at[span(g * parts + t, 16, 0, share), :],
        )
        bc_weights.moves += placed(
            gathered, of_half(0), groups, (pl.ds(half, 16), pl.ds(two_n, two_n)),
            lambda g, t, full: full.at[span(g * parts + t, 16, 16, share), :],
        ).moves
        dt_weights = placed(
            gathered, of_half(1), groups, (pl.ds(half, 16), pl.ds(0, rows)),
            lambda g, t, full: full.at[span(t, 16), lanes(g, rows)],
        )
        bc_weights.arrays, dt_weights.arrays = [], []
    else:
        bc_weights = single(lax.all_gather(w_bc, "dp", axis=0, tiled=True))
        all_dt = lax.all_gather(lax.all_gather(w_dt, "dp", axis=0, tiled=True), "tensor", axis=0)
        all_dt = jnp.pad(all_dt.transpose(0, 2, 1), ((0, 0), (0, 16 - own_heads), (0, 0)))
        dt_weights = single(all_dt.reshape(parts * 16, width))

    wz, wz_labels = widened("x", wz_near, near_labels)
    for at, array in enumerate(wz_far):
        got, labels = widened("x", array, far_labels[at * near : (at + 1) * near])
        wz, wz_labels = wz + got, wz_labels + labels
    by_chip = [(wo, wo_labels), (hop("x", wo)[0], [dict(label, x=1) for label in wo_labels])]
    for k, got in enumerate(hop("y", wo)):
        by_chip.append((got, [dict(label, y=k + 1) for label in wo_labels]))
    for k in range(1, parts // 2):
        got = lax.ppermute(wo, ("dp", "tensor"), [
            (g * parts + t, (g ^ 1) * parts + (t + 2 * k) % parts) for g in range(groups) for t in range(parts)])
        by_chip.append((got, [dict(label, x=1, y=k) for label in wo_labels]))
    wo, wo_labels = [a for a, _ in by_chip], sum([lab for _, lab in by_chip], [])

    def block_place(g, t, full):
        return full.at[span(g, rows), lanes(t, cols)]

    def across_cores(arrays, labels):
        arrays = arrays + [hop("c", a)[0] for a in arrays]
        return placed(arrays, labels + [dict(label, c=1) for label in labels], groups, None, block_place)

    head_sum = (head_of[:, None] == jnp.arange(heads)[None, :]).astype(bf16)

    (x, w_full, bc_full, dt_full, vec, up, normed, low, slope, values, scanned, keys, prebc, scal, states) = call_scan(
        info, gain, down_in, convbc, spread_heads,
        dict(x=x_pieces, w=x_weights, bc=bc_weights, dt=dt_weights, vec=vec_pieces),
        parts, heads, length, width, inner,
    )

    cot_rows = swapped(tie(cotangent, gathered[0]))
    wz, wo, cot_rows, low = lax.optimization_barrier((wz, wo, cot_rows, low))
    cot_pieces = single(cot_rows.reshape(length, width))
    z_weights, o_weights = across_cores(wz, wz_labels), across_cores(wo, wo_labels)
    out = call_gate(
        info, normed, low, scanned, x, vec, down_out, up_out,
        dict(z=z_weights, o=o_weights, cot=cot_pieces), groups, parts,
    )
    mixed, dlayer, dy, side, z_grad, low_back, up_z_part, out_down_part, z_full = out

    if mixed.ndim == 2:
        mixed = mixed.reshape(parts, groups, -1, width).transpose(1, 0, 2, 3)
    chunk = mixed.shape[2]
    came = swapped(mixed.reshape(groups * parts, chunk, width), ("dp", "tensor"))

    out = call_back(
        (x, normed, low, dlayer, dy, values, slope, keys, prebc, scal, states, scanned, side, z_grad, low_back),
        (w_full, z_full, bc_full, dt_full, vec, up, gain, down_in, convbc, spread_heads, head_sum)
        + (up_z_part, out_down_part), groups, parts, heads,
    )
    came, out = lax.optimization_barrier((came, out))
    token_rows, sums = out[0], out[1:]

    offsets = destination[:seq_grp] // seq_grp
    leave = call_turn(offsets, came.reshape(groups, parts, chunk, width))

    def second_leg(leave):
        return swapped(leave, "dp").transpose(1, 0, 2, 3).reshape(parts, part_len, width)

    token_rows = token_rows.reshape(parts, part_len, width)
    token_grad = exchanged([lax.dynamic_index_in_dim(token_rows, rank ^ k, 0, keepdims=False) for k in range(parts)])

    def stacked(blocks):
        result = jnp.zeros((parts,) + blocks[0].shape, blocks[0].dtype)
        for k, block in enumerate(blocks):
            result = lax.dynamic_update_index_in_dim(result, block, rank ^ k, 0)
        return result

    own = groups * parts
    if len(sums) > 1:

        def at_adapter(part):
            zeros = jnp.zeros((in_down.shape[1], part.shape[1]), bf16)
            return lax.dynamic_update_slice_in_dim(zeros, part.astype(bf16), adapter, 0)

        in_up_grad = [lax.psum_scatter(at_adapter(a), "tensor", scatter_dimension=1, tiled=True) for a in sums[:2]]
        in_up_grad = lax.psum(jnp.stack(in_up_grad, axis=1), "dp").astype(f32)
        others = [at_adapter(a) for a in (out_down_part, sums[2], sums[3])]
        out_down_grad, out_up_grad, in_down_grad = (a.astype(f32) for a in lax.psum(others, ("dp", "tensor")))
        return second_leg(leave), stacked(token_grad), in_down_grad.T, in_up_grad, out_down_grad, out_up_grad

    pooled = swapped(sums[0], ("dp", "tensor"))
    row_of = adapter_of[:, None] * RANK + jnp.arange(RANK)[None, :]
    select = (row_of.reshape(1, -1) == jnp.arange(in_down.shape[1])[:, None]).astype(bf16)
    sums = nn(select, pooled.reshape(own * RANK, -1)).astype(bf16)[None]
    sums, labels = widened("z", sums, [HERE])
    sums, leave = lax.optimization_barrier((sums, leave))
    mixed = second_leg(leave)
    sums, labels = widened("x", jnp.concatenate(sums), labels)
    sums = jnp.concatenate(sums)
    far_sums, far_labels = widened("y", sums[:, :, 2 * cols // groups :], labels)
    far_sums, token_grad = lax.optimization_barrier((jnp.concatenate(far_sums), token_grad))
    far_sums, far_labels = widened("c", far_sums, far_labels)
    in_up_grad, out_down_grad, out_up_grad, in_down_grad = call_arrange(
        info, sums, far_sums, labels, far_labels, groups, parts, inner, width, cols
    )
    in_up_grad = jnp.stack([in_up_grad[:, :cols], in_up_grad[:, cols:]], axis=1)
    return (mixed, stacked(token_grad), in_down_grad, in_up_grad, out_down_grad, out_up_grad)


def solution(mesh):
    return jax.shard_map(
        on_device,
        mesh=mesh,
        in_specs=(
            P("dp", "tensor", None), P("dp", "tensor", None), P(), P(), P(), P(),
            P("dp", None, "tensor"), P("dp", None), P("dp", "tensor"), P("dp", "tensor"),
            P(None, "tensor"), P(), P("tensor"), P("tensor"), P("tensor"), P("tensor"),
            P(), P(None, None, "tensor"), P(), P(),
        ),
        out_specs=(
            P("dp", "tensor", None), P("dp", "tensor", None), P(), P(None, None, "tensor"), P(), P(),
        ),
        check_vma=False,
    )
```

```python
import functools

import jax
import jax.numpy as jnp
from jax import lax
from jax.experimental import pallas as pl
from jax.experimental.pallas import tpu as pltpu
from jax.sharding import PartitionSpec as P

RANK = 16
SCAN = 128
ROWS = 256
TILE = 512
HEAD = 64
EPS = 1e-05
LIMIT = 58 * 1024 * 1024

f32 = jnp.float32
bf16 = jnp.bfloat16
ANY = pl.BlockSpec(memory_space=pl.ANY)
SMEM = pl.BlockSpec(memory_space=pltpu.SMEM)


def nn(a, b):
    return lax.dot_general(a, b, (((1,), (0,)), ((), ())), preferred_element_type=f32)


def nt(a, b):
    return lax.dot_general(a, b, (((1,), (1,)), ((), ())), preferred_element_type=f32)


def tn(a, b):
    return lax.dot_general(a, b, (((0,), (0,)), ((), ())), preferred_element_type=f32)


def exact(a, b):
    return lax.dot_general(
        a, b, (((1,), (0,)), ((), ())), preferred_element_type=f32, precision=lax.Precision.HIGHEST
    )


def halves(v, axis):
    high = v.astype(bf16)
    low = (v - high.astype(f32)).astype(bf16)
    return jnp.concatenate([high, low], axis=axis)


def sigmoid(v):
    return 1.0 / (1.0 + jnp.exp(-v))


def softplus(v):
    return jnp.maximum(v, 0.0) + jnp.log1p(jnp.exp(-jnp.abs(v)))


def triangle(n, lower):
    row = lax.broadcasted_iota(jnp.int32, (n, n), 0)
    col = lax.broadcasted_iota(jnp.int32, (n, n), 1)
    return row >= col if lower else row <= col


def head_vectors(vec, parts):
    width = vec.shape[1] // parts
    total = vec[8:16, 0:128]
    for t in range(1, parts):
        total = total + vec[8:16, t * width : t * width + 128]
    return total


def split_lanes(v):
    low_lanes = lax.broadcasted_iota(jnp.int32, v.shape, 1) < HEAD
    return jnp.where(low_lanes, v, 0.0).astype(bf16), jnp.where(low_lanes, 0.0, v).astype(bf16)


class Pieces:
    def __init__(self, arrays, moves):
        self.arrays, self.moves = arrays, moves


def copy_in(info, groups, sems):
    copies = []
    for refs, moves, full in groups:
        for which, index, take, place in moves:
            src = refs[which]
            if index is not None:
                src = src.at[index]
            if take is not None:
                src = src.at[take]
            copies.append(pltpu.make_async_copy(src, place(info, full), sems.at[len(copies)]))
    for copy in copies:
        copy.start()
    for copy in copies:
        copy.wait()


def whole_block(shape):
    return pl.BlockSpec(shape, lambda c: (0,) * len(shape))


def row_block(width, rows=ROWS):
    return pl.BlockSpec((rows, width), lambda c: (c, 0))


def take_refs(refs, counts):
    taken, at = [], 0
    for count in counts:
        taken.append(refs[at : at + count])
        at += count
    return taken, refs[at:]


def gathered_operands(names, pieces):
    owners, lists, arrays, counts = [], [], [], []
    for i, name in enumerate(names):
        owners.append(i if pieces[name].arrays else owners[-1])
        lists.append(pieces[name].moves)
        arrays += pieces[name].arrays
        counts.append(len(pieces[name].arrays))
    return (owners, lists), arrays, counts, sum(len(m) for m in lists)


def cost(micros):
    return pl.CostEstimate(flops=int(micros * 1.1e9), bytes_accessed=1 << 20, transcendentals=0)


def scan_kernel(names, moves, counts, parts, heads, *refs):
    info, gain, in_down, convbc, spread_heads = refs[:5]
    groups, rest = take_refs(refs[5:], counts)
    (x_out, w_full, bc_full, dt_full, vec, up, normed_out, low_out, slope_out, values_out, scanned_out) = rest[:11]
    (keys_out, prebc_out, scal_out, states_out, vec_low, xs, dt_wide, xbuf, bcbuf, state, sems) = rest[11:]
    fulls = dict(x=xs, w=w_full, bc=bc_full, dt=dt_wide, vec=vec_low)
    c = pl.program_id(0)
    inner = w_full.shape[1]
    subs = ROWS // SCAN

    @pl.when(c == 0)
    def _():
        copy_in(info, [(groups[g], m, fulls[name]) for name, g, m in zip(names, moves[0], moves[1])], sems)
        state[...] = jnp.zeros_like(state)
        xbuf[0:8, :] = jnp.zeros((8, inner), f32)
        bcbuf[0:8, :] = jnp.zeros((8, bcbuf.shape[1]), f32)
        vec[16:, :] = vec_low[16:, :].astype(f32)
        top = vec_low[0:16, :].astype(f32)
        skip, bias, decay = (top[n : n + 1] + top[n + 1 : n + 2] + top[n + 2 : n + 3] for n in (6, 9, 12))
        vec[0:16, :] = jnp.concatenate([top[0:6], skip, jnp.zeros_like(skip), bias, decay, jnp.zeros((6, inner), f32)], axis=0)
        up[...] = vec_low[16 : 16 + RANK, :]
        own = heads // parts
        dt_full[...] = jnp.concatenate(
            [dt_wide[16 * t : 16 * t + 16, :].astype(f32)[:own] for t in range(parts)], axis=0
        ).astype(bf16)

    x_low = xs[pl.ds(pl.multiple_of(c * ROWS, ROWS), ROWS), :]
    x_out[...] = x_low
    x = x_low.astype(f32)
    rms = lax.rsqrt(jnp.mean(x * x, axis=1, keepdims=True) + EPS)
    normed_out[...] = (x * rms * gain[...]).astype(bf16)
    low_out[...] = nn(normed_out[...], in_down[...]).astype(bf16)
    hv = head_vectors(vec, parts)
    bias, rate = hv[0:1, 0:heads], -jnp.exp(hv[1:2, 0:heads])

    bcbuf[8:, :] = nn(normed_out[...], bc_full[...])
    pre = convbc[4:5, :] + sum(convbc[k : k + 1, :] * bcbuf[5 + k : 5 + k + ROWS, :] for k in range(4))
    bcbuf[0:8, :] = bcbuf[ROWS : ROWS + 8, :]
    prebc_out[...] = pre
    keys_out[...] = (pre * sigmoid(pre)).astype(bf16)
    nstate = keys_out.shape[1] // 2

    raw = nt(normed_out[...], dt_full[...]) + bias
    steps = softplus(raw)
    lower = triangle(SCAN, True)
    lower_f = lower.astype(f32)
    cums, cum_rows, grown, scores, key_cols = [], [], [], [], []
    for s in range(subs):
        rows = slice(s * SCAN, (s + 1) * SCAN)
        dt_s = steps[rows]
        cum = exact(lower_f, dt_s * rate)
        cums.append(cum)
        cum_rows.append(cum.T)
        b_part, c_part = keys_out[rows, 0:nstate], keys_out[rows, nstate:]
        scores.append(jnp.where(lower, nt(c_part, b_part), 0.0))
        key_cols.append(b_part.astype(f32).T.astype(bf16))
        tail = jnp.exp(cum[SCAN - 1 : SCAN, :] - cum)
        grown.append((halves(dt_s, 1), halves(jnp.exp(cum), 1), halves(dt_s * tail, 1)))
    scal_out[...] = jnp.concatenate(
        [steps, jnp.concatenate(cums, axis=0), sigmoid(raw), jnp.zeros((ROWS, 128 - 3 * heads), f32)], axis=1
    )

    for j in range(inner // TILE):
        cols = slice(j * TILE, (j + 1) * TILE)
        xbuf[8:, cols] = nn(normed_out[...], w_full[:, cols]) + nn(low_out[...], up[:, cols])
        halo = xbuf[:, cols]
        pre = vec[4:5, cols] + vec[3:4, cols] * halo[8:]
        pre = pre + sum(vec[k : k + 1, cols] * pltpu.roll(halo, 3 - k, 0)[8:] for k in range(3))
        xbuf[0:8, cols] = xbuf[ROWS : ROWS + 8, cols]
        sig = sigmoid(pre)
        values_out[:, cols] = (pre * sig).astype(bf16)
        slope_out[:, cols] = (sig * (1.0 + pre * (1.0 - sig))).astype(bf16)
        for s in range(subs):
            rows = slice(s * SCAN, (s + 1) * SCAN)
            dtx, ecx, tlx = (nn(v, spread_heads[:, cols]) for v in grown[s])
            state_low = state[:, cols].astype(bf16)
            states_out[s, :, cols] = state_low
            v = values_out[rows, cols].astype(f32)
            y = ecx * nn(keys_out[rows, nstate:], state_low) + vec[6:7, cols] * v
            vw = v * dtx
            within = []
            for p in range(TILE // 128):
                lhs = []
                for a in range(2):
                    h = (j * TILE + p * 128) // HEAD + a
                    gap = cums[s][:, h : h + 1] - cum_rows[s][h : h + 1, :]
                    lhs.append((jnp.exp(jnp.minimum(gap, 0.0)) * scores[s]).astype(bf16))
                rhs = jnp.concatenate(split_lanes(vw[:, p * 128 : (p + 1) * 128]), axis=0)
                within.append(nn(jnp.concatenate(lhs, axis=1), rhs))
            scanned_out[rows, cols] = y + jnp.concatenate(within, axis=1)
            state[:, cols] = ecx[SCAN - 1 : SCAN, :] * state[:, cols] + nn(key_cols[s], (v * tlx).astype(bf16))


def call_scan(info, gain, in_down, convbc, spread_heads, pieces, parts, heads, length, width, inner):
    names = ("x", "w", "bc", "dt", "vec")
    moves, arrays, counts, total = gathered_operands(names, pieces)
    two_n = convbc.shape[1]
    steps, subs = length // ROWS, ROWS // SCAN
    shapes = [
        ((length, width), bf16), ((width, inner), bf16), ((width, two_n), bf16), ((heads, width), bf16),
        ((16 + 2 * RANK, inner), f32), ((RANK, inner), bf16), ((length, width), bf16), ((length, RANK), bf16),
        ((length, inner), bf16), ((length, inner), bf16), ((length, inner), f32), ((length, two_n), bf16),
        ((length, two_n), f32), ((length, 128), f32), ((length // SCAN, two_n // 2, inner), bf16),
    ]
    specs = [
        row_block(width), whole_block((width, inner)), whole_block((width, two_n)), whole_block((heads, width)),
        whole_block((16 + 2 * RANK, inner)), whole_block((RANK, inner)), row_block(width), row_block(RANK),
        row_block(inner), row_block(inner), row_block(inner), row_block(two_n),
        row_block(two_n), row_block(128), pl.BlockSpec((subs, two_n // 2, inner), lambda c: (c, 0, 0)),
    ]
    return pl.pallas_call(
        functools.partial(scan_kernel, names, moves, counts, parts, heads),
        grid=(steps,),
        in_specs=[SMEM, whole_block(gain.shape), whole_block(in_down.shape), whole_block(convbc.shape)]
        + [whole_block(spread_heads.shape)] + [ANY] * len(arrays),
        out_shape=[jax.ShapeDtypeStruct(s, d) for s, d in shapes],
        out_specs=specs,
        scratch_shapes=[
            pltpu.VMEM((16 + 2 * RANK, inner), bf16),
            pltpu.VMEM((length, width), bf16), pltpu.VMEM((parts * 16, width), bf16),
            pltpu.VMEM((ROWS + 8, inner), f32), pltpu.VMEM((ROWS + 8, two_n), f32),
            pltpu.VMEM((two_n // 2, inner), f32), pltpu.SemaphoreType.DMA((total,)),
        ],
        compiler_params=pltpu.CompilerParams(vmem_limit_bytes=LIMIT, dimension_semantics=("arbitrary",)),
        cost_estimate=cost(44),
    )(info, gain, in_down, convbc, spread_heads, *arrays)


def gate_kernel(names, moves, counts, *refs):
    info, normed, low, scanned, x, vec, out_down, out_up = refs[:8]
    groups, rest = take_refs(refs[8:], counts)
    (mixed_out, dlayer_out, dy_out, side_out, zg, low_back_out, in_up_out, out_down_out, wz) = rest[:9]
    (wo, upz, cots, z, gi, gated, gg, sems) = rest[9:]
    fulls = dict(z=wz, o=wo, cot=cots)
    c = pl.program_id(0)
    inner = wz.shape[1]
    tiles = [slice(j * TILE, (j + 1) * TILE) for j in range(inner // TILE)]

    @pl.when(c == 0)
    def _():
        copy_in(info, [(groups[g], m, fulls[name]) for name, g, m in zip(names, moves[0], moves[1])], sems)
        upz[...] = vec[16 + RANK : 16 + 2 * RANK, :].astype(bf16)
        in_up_out[...] = jnp.zeros_like(in_up_out)
        out_down_out[...] = jnp.zeros_like(out_down_out)

    squares = jnp.zeros((ROWS, 128), f32)
    for cols in tiles:
        zj = nn(normed[...], wz[:, cols]) + nn(low[...], upz[:, cols])
        z[:, cols] = zj
        g = scanned[:, cols] * (zj * sigmoid(zj))
        gi[:, cols] = g
        g = g * g
        squares = squares + sum(g[:, k : k + 128] for k in range(0, TILE, 128))
    scale = lax.rsqrt(jnp.sum(squares, axis=1, keepdims=True) / inner + EPS)
    for cols in tiles:
        gated[:, cols] = (gi[:, cols] * scale * vec[5:6, cols]).astype(bf16)
    side = nt(gated[...], out_down[...]).astype(bf16)
    side_out[...] = side
    terms = nt(gated[...], wo[...]) + nn(side, out_up[...])
    live = lax.broadcasted_iota(jnp.int32, (ROWS, 1), 0) + c * ROWS < info[0]
    mixed = jnp.where(live, x[...].astype(f32) + terms, 0.0).astype(bf16)
    if len(mixed_out.shape) == 2:
        mixed_out[...] = mixed
    else:
        chunk = mixed_out.shape[2]
        for j in range(mixed_out.shape[0]):
            mixed_out[j, 0, :, :] = mixed[j * chunk : (j + 1) * chunk, :]
    cot = cots[pl.ds(pl.multiple_of(c * ROWS, ROWS), ROWS), :]
    dlayer_out[...] = jnp.where(live, cot.astype(f32), 0.0).astype(bf16)
    side_grad = nt(dlayer_out[...], out_up[...]).astype(bf16)
    products = jnp.zeros((ROWS, 128), f32)
    for cols in tiles:
        grad = (nn(dlayer_out[...], wo[:, cols]) + nn(side_grad, out_down[:, cols])).astype(bf16)
        gg[:, cols] = grad
        g = grad.astype(f32) * vec[5:6, cols] * gi[:, cols]
        products = products + sum(g[:, k : k + 128] for k in range(0, TILE, 128))
    factor = scale * scale * scale * (jnp.sum(products, axis=1, keepdims=True) / inner)
    for cols in tiles:
        grad = scale * (gg[:, cols].astype(f32) * vec[5:6, cols]) - gi[:, cols] * factor
        zj = z[:, cols]
        sig = sigmoid(zj)
        sc = scanned[:, cols].astype(f32)
        dy = (grad * (zj * sig)).astype(bf16)
        dy_out[:, cols] = dy
        zg[:, cols] = (grad * sc * (sig * (1.0 + zj * (1.0 - sig)))).astype(bf16)
    low_back_out[...] = nt(zg[...], upz[...])
    in_up_out[...] += tn(low[...], zg[...])
    out_down_out[...] += tn(side_grad, gated[...])


def call_gate(info, normed, low, scanned, x, vec, out_down, out_up, pieces, groups, parts):
    names = ("z", "o", "cot")
    moves, arrays, counts, total = gathered_operands(names, pieces)
    length, width = x.shape
    inner = scanned.shape[1]
    chunk = length // (groups * parts)
    if chunk % 16 == 0 and length // parts == ROWS:
        leaving = ((groups, parts, chunk, width), pl.BlockSpec((groups, 1, chunk, width), lambda c: (0, c, 0, 0)))
    else:
        leaving = ((length, width), row_block(width))
    shapes = [
        (leaving[0], bf16), ((length, width), bf16), ((length, inner), bf16), ((length, RANK), bf16),
        ((length, inner), bf16), ((length, RANK), f32), ((RANK, inner), f32), ((RANK, inner), f32),
        ((width, inner), bf16),
    ]
    specs = [
        leaving[1], row_block(width), row_block(inner), row_block(RANK), row_block(inner), row_block(RANK),
        whole_block((RANK, inner)), whole_block((RANK, inner)), whole_block((width, inner)),
    ]
    return pl.pallas_call(
        functools.partial(gate_kernel, names, moves, counts),
        grid=(length // ROWS,),
        in_specs=[SMEM, row_block(width), row_block(RANK), row_block(inner), row_block(width), whole_block(vec.shape)]
        + [whole_block(out_down.shape), whole_block(out_up.shape)] + [ANY] * len(arrays),
        out_shape=[jax.ShapeDtypeStruct(s, d) for s, d in shapes],
        out_specs=specs,
        scratch_shapes=[
            pltpu.VMEM((width, inner), bf16), pltpu.VMEM((RANK, inner), bf16), pltpu.VMEM((length, width), bf16),
            pltpu.VMEM((ROWS, inner), f32), pltpu.VMEM((ROWS, inner), f32), pltpu.VMEM((ROWS, inner), bf16),
            pltpu.VMEM((ROWS, inner), bf16), pltpu.SemaphoreType.DMA((total,)),
        ],
        compiler_params=pltpu.CompilerParams(vmem_limit_bytes=LIMIT, dimension_semantics=("arbitrary",)),
        cost_estimate=cost(43),
    )(info, normed, low, scanned, x, vec, out_down, out_up, *arrays)


def back_kernel(groups, parts, heads, *refs):
    (x, normed, low, dlayer, dy, values, slope, keys, prebc, scal, states, scanned, side, zg, low_back) = refs[:15]
    (w_full, wz, bc_full, dt_full, vec, up, gain, in_down, convbc, spread_heads, head_sum) = refs[15:26]
    (in_up_z, out_down, grad_out) = refs[26:29]
    outs, (in_up_x, out_up, in_down_sum, dstate, xbuf, bcbuf, xg, summed) = refs[29:-8], refs[-8:]
    i = pl.program_id(0)
    inner = w_full.shape[1]
    subs = ROWS // SCAN
    nstate = keys.shape[1] // 2
    tiles = [slice(j * 1024, (j + 1) * 1024) for j in range(inner // 1024)]

    @pl.when(i == 0)
    def _():
        dstate[...] = jnp.zeros_like(dstate)
        xbuf[ROWS:, :] = jnp.zeros((8, inner), f32)
        bcbuf[ROWS:, :] = jnp.zeros((8, bcbuf.shape[1]), f32)
        summed[...] = jnp.zeros_like(summed)
        for total in (in_up_x, out_up, in_down_sum):
            total[...] = jnp.zeros_like(total)

    hv = head_vectors(vec, parts)
    rate = -jnp.exp(hv[1:2, 0:heads])
    upper = triangle(SCAN, False)
    upper_f = upper.astype(f32)
    raw_parts = [None] * subs
    for s in reversed(range(subs)):
        rows = slice(s * SCAN, (s + 1) * SCAN)
        steps, cum = scal[rows, 0:heads], scal[rows, heads : 2 * heads]
        cum_row = cum.T
        last = cum[SCAN - 1 : SCAN, :]
        dt2, ecum2, tail2 = halves(steps, 1), halves(jnp.exp(cum), 1), halves(jnp.exp(last - cum), 1)
        b_part, c_part = keys[rows, 0:nstate], keys[rows, nstate:]
        c_cols = c_part.astype(f32).T.astype(bf16)
        scores = jnp.where(upper, nt(b_part, c_part), 0.0)
        pulled = jnp.zeros((SCAN, SCAN), f32)
        c_grad = jnp.zeros((SCAN, nstate), f32)
        b_grad = jnp.zeros((SCAN, nstate), f32)
        direct = jnp.zeros((SCAN, heads), f32)
        change = jnp.zeros((SCAN, heads), f32)
        for j, cols in enumerate(tiles):
            dtx, ecx, tlx = (nn(v, spread_heads[:, cols]) for v in (dt2, ecum2, tail2))
            g_low = dy[rows, cols]
            g = g_low.astype(f32)
            v = values[rows, cols].astype(f32)
            vw = v * dtx
            dstate_low = dstate[:, cols].astype(bf16)
            within = []
            for p in range(1024 // 128):
                part = slice(p * 128, (p + 1) * 128)
                vw_split = split_lanes(vw[:, part])
                lhs = []
                for a in range(2):
                    h = (j * 1024 + p * 128) // HEAD + a
                    gap = cum_row[h : h + 1, :] - cum[:, h : h + 1]
                    decay = jnp.exp(jnp.minimum(gap, 0.0))
                    pulled = pulled + decay * nt(vw_split[a], g_low[:, part])
                    lhs.append((decay * scores).astype(bf16))
                rhs = jnp.concatenate(split_lanes(g[:, part]), axis=0)
                within.append(nn(jnp.concatenate(lhs, axis=1), rhs))
            dvw = jnp.concatenate(within, axis=1) + tlx * nn(b_part, dstate_low)
            vg = dtx * dvw + vec[6:7, cols] * g
            summer = head_sum[cols, :]
            direct = direct + nn((v * dvw).astype(bf16), summer)
            summer = jnp.concatenate([summer, summer], axis=0)
            change = change + nn(halves(g * scanned[rows, cols] - v * vg, 1), summer)
            ge = (ecx * g).astype(bf16)
            c_grad = c_grad + nt(ge, states[s, :, cols])
            b_grad = b_grad + nt((tlx * vw).astype(bf16), dstate_low)
            dstate[:, cols] = ecx[SCAN - 1 : SCAN, :] * dstate[:, cols] + nn(c_cols, ge)
            xbuf[rows, cols] = vg * slope[rows, cols].astype(f32)
        pulled = jnp.where(upper, pulled, 0.0)
        b_grad = b_grad + nn(pulled.astype(bf16), c_part)
        c_grad = c_grad + nn(pulled.T.astype(bf16), b_part)
        pb = prebc[rows, :]
        sig = sigmoid(pb)
        bcbuf[rows, :] = jnp.concatenate([b_grad, c_grad], axis=1) * (sig * (1.0 + pb * (1.0 - sig)))
        later = exact(upper_f, change) + summed[0:1, 0:heads]
        summed[0:1, 0:heads] = later[0:1, :]
        raw_parts[s] = (direct + rate * later) * scal[rows, 2 * heads : 3 * heads]
    raw_grad = jnp.concatenate(raw_parts, axis=0).astype(bf16)

    for cols in tiles:
        halo = xbuf[:, cols]
        total = vec[3:4, cols] * halo[:ROWS]
        total = total + sum(vec[k : k + 1, cols] * pltpu.roll(halo, ROWS + 5 + k, 0)[:ROWS] for k in range(3))
        xg[:, cols] = total.astype(bf16)
    xbuf[ROWS:, :] = xbuf[0:8, :]
    bc_grad = sum(convbc[k : k + 1, :] * bcbuf[3 - k : 3 - k + ROWS, :] for k in range(4)).astype(bf16)
    bcbuf[ROWS:, :] = bcbuf[0:8, :]
    low_grad = (low_back[...] + nt(xg[...], up[...])).astype(bf16)
    in_up_x[...] += tn(low[...], xg[...])
    out_up[...] += tn(side[...], dlayer[...])
    in_down_sum[...] += tn(low_grad, normed[...])
    ng = nt(zg[...], wz[...]) + nt(xg[...], w_full[...]) + nt(bc_grad, bc_full[...])
    ng = ng + nn(raw_grad, dt_full[...]) + nt(low_grad, in_down[...])
    xv = x[...].astype(f32)
    rms = lax.rsqrt(jnp.mean(xv * xv, axis=1, keepdims=True) + EPS)
    ng = ng * gain[...]
    inner_norm = jnp.mean(ng * xv, axis=1, keepdims=True)
    grad_out[...] = (dlayer[...].astype(f32) + rms * ng - xv * (rms * rms * rms * inner_norm)).astype(bf16)


    @pl.when(i == pl.num_programs(0) - 1)
    def _():
        if len(outs) > 1:
            for out, total in zip(outs, (in_up_z, in_up_x, out_up, in_down_sum)):
                out[...] = total[...].astype(bf16)
            return
        (shares,) = outs
        cols = inner // parts
        for g in range(groups):
            for t in range(parts):
                own = g * parts + t
                at = g * 2 * cols // groups
                total = in_up_z if at < cols else in_up_x
                at = at % cols + t * cols
                wide = 2 * cols // groups
                shares[own, :, 0:wide] = total[:, at : at + wide].astype(bf16)
                other = shares.shape[2] - wide
                at = own * other
                for total in (out_down, out_up, in_down_sum):
                    if 0 <= at < total.shape[1]:
                        shares[own, :, wide:] = total[:, at : at + other].astype(bf16)
                    at = at - total.shape[1]


def shares_of(groups, parts, inner, width):
    ups, others = 2 * inner // (groups * parts), (inner + 2 * width) // (groups * parts)
    return None if ups % 128 or others % 128 or width % others or inner % others else ups + others


def call_back(rows_in, consts, groups, parts, heads):
    x = rows_in[0]
    length, width = x.shape
    inner = rows_in[4].shape[1]
    two_n = rows_in[7].shape[1]
    steps, subs = length // ROWS, ROWS // SCAN
    shares = shares_of(groups, parts, inner, width)
    if shares is None:
        sums = [(RANK, inner), (RANK, inner), (RANK, width), (RANK, width)]
    else:
        sums = [(groups * parts, RANK, shares)]

    def spec(a):
        if a.ndim == 3:
            return pl.BlockSpec((subs,) + a.shape[1:], lambda i: (steps - 1 - i, 0, 0))
        return pl.BlockSpec((ROWS, a.shape[1]), lambda i: (steps - 1 - i, 0))

    return pl.pallas_call(
        functools.partial(back_kernel, groups, parts, heads),
        grid=(steps,),
        in_specs=[spec(a) for a in rows_in] + [whole_block(a.shape) for a in consts],
        out_shape=[jax.ShapeDtypeStruct((length, width), bf16)] + [jax.ShapeDtypeStruct(s, bf16) for s in sums],
        out_specs=[spec(x)] + [whole_block(s) for s in sums],
        scratch_shapes=[
            pltpu.VMEM((RANK, inner), f32), pltpu.VMEM((RANK, width), f32), pltpu.VMEM((RANK, width), f32),
            pltpu.VMEM((two_n // 2, inner), f32),
            pltpu.VMEM((ROWS + 8, inner), f32), pltpu.VMEM((ROWS + 8, two_n), f32), pltpu.VMEM((ROWS, inner), bf16),
            pltpu.VMEM((8, 128), f32),
        ],
        compiler_params=pltpu.CompilerParams(vmem_limit_bytes=LIMIT, dimension_semantics=("arbitrary",)),
        cost_estimate=cost(50),
    )(*rows_in, *consts)


def turn_kernel(info, came, leave):
    groups, parts = came.shape[:2]
    for p in range(parts):
        for d in range(groups):
            leave[d, p, :, :] = came[lax.rem(d + groups - info[p], groups), p, :, :]


def call_turn(offsets, came):
    return pl.pallas_call(
        turn_kernel,
        in_specs=[SMEM, pl.BlockSpec(memory_space=pltpu.VMEM)],
        out_shape=jax.ShapeDtypeStruct(came.shape, came.dtype),
        out_specs=pl.BlockSpec(memory_space=pltpu.VMEM),
        compiler_params=pltpu.CompilerParams(vmem_limit_bytes=LIMIT),
        cost_estimate=cost(3),
    )(offsets, came)


def arrange_kernel(labels, far_labels, groups, parts, info, sums, *refs):
    far, (in_up, out_down, out_up, in_down) = refs[:-4], refs[-4:]
    cols = in_up.shape[1] // groups
    for i, label in enumerate(labels):
        g = info[1 + label["z"] * 2 + label["x"]]
        in_up[:, lanes(g, cols)] = sums[i, :, 0:cols].astype(f32)
    width = far[0].shape[2]
    first, second = out_down.shape[1] // width, out_up.shape[1] // width
    at = 0
    for part in far:
        for i in range(part.shape[0]):
            label = far_labels[at]
            at += 1
            own = info[1 + label["z"] * 2 + label["x"]] * parts + info[1 + groups + label["y"] * 2 + label["c"]]

            @pl.when(own < first)
            def _():
                out_down[:, lanes(own, width)] = part[i, :, :].astype(f32)

            @pl.when((own >= first) & (own < first + second))
            def _():
                out_up[:, lanes(own - first, width)] = part[i, :, :].astype(f32)

            @pl.when(own >= first + second)
            def _():
                in_down[lanes(own - first - second, width), :] = part[i, :, :].astype(f32).T


def call_arrange(info, sums, far_sums, labels, far_labels, groups, parts, inner, width, cols):
    rows = sums.shape[1]
    vmem = pl.BlockSpec(memory_space=pltpu.VMEM)
    shapes = [(rows, 2 * cols), (rows, inner), (rows, width), (width, rows)]
    return pl.pallas_call(
        functools.partial(arrange_kernel, labels, far_labels, groups, parts),
        in_specs=[SMEM, vmem] + [vmem] * len(far_sums),
        out_shape=[jax.ShapeDtypeStruct(s, f32) for s in shapes],
        out_specs=[vmem] * 4,
        compiler_params=pltpu.CompilerParams(vmem_limit_bytes=LIMIT),
        cost_estimate=cost(3),
    )(info, sums, *far_sums)


def moved(block, axis, route):
    size = lax.axis_size(axis)
    return lax.ppermute(block, axis, [(i, route(i, size)) for i in range(size)])


def hop(name, block):
    axis = "dp" if name in "zx" else "tensor"
    if name in "xc":
        return [moved(block, axis, lambda i, n: i ^ 1)]
    return [
        moved(block, axis, functools.partial(lambda k, i, n: (i + 2 * k) % n, k))
        for k in range(1, lax.axis_size(axis) // 2)
    ]


def widened(name, block, labels):
    got = hop(name, block)
    lists = labels + sum([[dict(label, **{name: k + 1}) for label in labels] for k in range(len(got))], [])
    return [block] + got, lists


HERE = dict(z=0, x=0, y=0, c=0)


def tie(first, *others):
    return lax.optimization_barrier((first,) + others)[0]


def index_table(length_of, groups, parts, group, rank):
    dp_from = [((group ^ kx) - 2 * kz) % groups for kz in range(groups // 2) for kx in range(2)]
    part_from = [((rank ^ kc) - 2 * ky) % parts for ky in range(parts // 2) for kc in range(2)]
    partner = [rank ^ k for k in range(parts)]
    return jnp.stack([length_of] + dp_from + part_from + partner).astype(jnp.int32)


def placed(arrays, labels, groups, take, place):
    moves, at = [], 0
    for which, array in enumerate(arrays):
        for index in range(array.shape[0]):
            label = labels[at]
            at += 1
            if label is None:
                continue
            g_at = 1 + label["z"] * 2 + label["x"]
            t_at = 1 + groups + label["y"] * 2 + label["c"]
            moves.append((which, index, take, functools.partial(
                lambda g_at, t_at, info, full: place(info[g_at], info[t_at], full), g_at, t_at)))
    return Pieces(list(arrays), moves)


def paired(arrays, groups, parts, index, place):
    moves = [
        (k, index, None, functools.partial(lambda at, info, full: place(info[at], full), 1 + groups + parts + k))
        for k in range(parts)
    ]
    return Pieces(list(arrays), moves)


def single(array):
    return Pieces([array], [(0, None, None, lambda info, full: full)])


def span(index, size, offset=0, step=None):
    return pl.ds(pl.multiple_of(index * (size if step is None else step) + offset, 16), size)


def lanes(index, size):
    return pl.ds(pl.multiple_of(index * size, size), size)


def exchanged(blocks):
    return [
        block if k == 0 else moved(block, "tensor", functools.partial(lambda k, i, n: i ^ k, k))
        for k, block in enumerate(blocks)
    ]


def on_device(
    tokens, cotangent, destination, lengths, adapter_of, norm_gain, w_zx, w_bc, w_dt, w_out,
    conv_x, conv_bc, dt_bias, a_log, d_skip, out_gain, in_down, in_up, out_down, out_up,
):
    groups, parts = lax.axis_size("dp"), lax.axis_size("tensor")
    group, rank = lax.axis_index("dp"), lax.axis_index("tensor")
    seq_grp, part_len, width = tokens.shape
    rows, _, cols = w_zx.shape
    own_heads = w_dt.shape[1]
    length, inner, heads = part_len * parts, cols * parts, own_heads * parts
    mine = group * seq_grp + rank
    offset = destination[rank] // seq_grp
    adapter = adapter_of[mine] * RANK
    info = index_table(lengths[mine], groups, parts, group, rank)

    def swapped(array, axes="tensor"):
        return lax.all_to_all(array, axes, split_axis=0, concat_axis=0, tiled=True)

    def col_place(t, full):
        return full.at[:, lanes(t, cols)]

    down_in = lax.dynamic_slice_in_dim(in_down, adapter, RANK, 1)
    down_out = lax.dynamic_slice_in_dim(out_down, adapter, RANK, 0)
    up_out = lax.dynamic_slice_in_dim(out_up, adapter, RANK, 0)
    gain = norm_gain.astype(f32)[None]
    convbc = jnp.pad(conv_bc.astype(f32), ((0, 3), (0, 0)))
    head_of = jnp.arange(inner) // (inner // heads)
    spread_heads = (jnp.arange(2 * heads)[:, None] % heads == head_of[None, :]).astype(bf16)
    small_inputs = (info, down_in, gain, convbc, spread_heads)

    head_rows = lax.dynamic_update_slice(jnp.zeros((2, cols), f32), jnp.stack([dt_bias, a_log]), (0, rank * own_heads))
    exact_rows = jnp.concatenate([jnp.repeat(d_skip, cols // own_heads)[None], head_rows])
    high = lax.reduce_precision(exact_rows, 8, 7)
    middle = lax.reduce_precision(exact_rows - high, 8, 7)
    thirds = jnp.stack([high, middle, exact_rows - high - middle], axis=1).astype(bf16).reshape(9, cols)
    own_vec = jnp.concatenate([
        conv_x, out_gain[None], thirds, jnp.zeros((1, cols), bf16)])

    half, share, two_n = rows // 2, rows // parts, w_bc.shape[1]
    packed = share % 32 == 0 and rows % 128 == 0 and cols == 2 * two_n
    w_x = w_zx[:, 1]
    if packed:
        own_bc = lax.dynamic_slice_in_dim(w_bc, rank * share, share, 0)
        own_bc = jnp.concatenate([own_bc[: share // 2], own_bc[share // 2 :]], axis=1)
        own_dt = jnp.zeros((16, cols), bf16).at[:own_heads, :rows].set(w_dt.T)
        block = jnp.concatenate([w_x[:half], own_bc, w_x[half:], own_dt])
    else:
        block = w_x
    extra = block.shape[0] // 2
    along_z, labels = widened("z", jnp.concatenate([block, w_out])[None], [HERE])
    wz, wz_labels = widened("y", w_zx[:, 0][None], [HERE])
    along_z, wz, token_rows = lax.optimization_barrier((along_z, wz, swapped(tokens)))

    own_vec, in_up = lax.optimization_barrier((own_vec, in_up, along_z))[:2]
    vecs = []
    for k in range(parts):
        theirs = lax.dynamic_slice_in_dim(in_up, adapter_of[group * seq_grp + k] * RANK, RANK, 0)
        vecs.append(jnp.concatenate([own_vec, theirs[:, 1], theirs[:, 0]]))

    first = jnp.concatenate([a[:, :extra] for a in along_z])
    second = jnp.concatenate([a[:, extra : 2 * extra] for a in along_z])
    first, second, wz = lax.optimization_barrier((first, second, jnp.concatenate(wz)))
    first, first_labels = widened("x", first, labels)
    second, second_labels = widened("y", second, labels)
    wo, wo_labels = jnp.concatenate([a[:, 2 * extra :] for a in along_z]), labels
    wz, wz_labels = widened("z", wz, wz_labels)
    first, second, wz[1], wz[-1], wo, vecs = lax.optimization_barrier((first, second, wz[1], wz[-1], wo, jnp.stack(vecs)))

    vec_rows = swapped(vecs)
    near = len(wz_labels) // len(wz)
    wz_near = jnp.concatenate([wz[0], wz[1], wz[-1]]) if len(wz) > 2 else jnp.concatenate(wz)
    near_labels = wz_labels[: 2 * near] + (wz_labels[-near:] if len(wz) > 2 else [])
    first = jnp.concatenate(first)
    second = jnp.concatenate(second)
    gathered = [first, second] + hop("c", first) + hop("c", second)
    first, far_first_labels = widened("y", first, first_labels)
    second, far_second_labels = widened("x", second, second_labels)
    wz_far, far_labels = wz[2:-1], wz_labels[2 * near : -near]
    first, second, wz_far, wz_near, vec_rows, gathered, small_inputs = lax.optimization_barrier(
        (first[1:], second[1:], wz_far, wz_near, vec_rows, gathered, small_inputs)
    )
    info, down_in, gain, convbc, spread_heads = small_inputs

    both_labels = [first_labels, second_labels]
    both_labels += [[dict(label, c=1) for label in labels] for labels in both_labels]
    halves_of = [0, 1, 0, 1]
    for which, arrays, labels, own in ((0, first, far_first_labels, first_labels), (1, second, far_second_labels, second_labels)):
        labels = labels[len(own) :]
        for at, array in enumerate(arrays):
            part = labels[at * len(own) : (at + 1) * len(own)]
            gathered += [array] + hop("c", array)
            both_labels += [part, [dict(label, c=1) for label in part]]
            halves_of += [which, which]
    own_cores = hop("c", wo)
    token_rows, own_cores = lax.optimization_barrier((token_rows, own_cores))
    x_pieces = single(token_rows.reshape(length, width))
    vec_pieces = Pieces([vec_rows], [
        (0, k, None, functools.partial(lambda k, info, full: full.at[:, pl.ds(k * cols, cols)], k)) for k in range(parts)])

    def of_half(which):
        return sum([labels if which == h else [None] * len(labels) for labels, h in zip(both_labels, halves_of)], [])

    x_weights = placed(
        gathered, of_half(0), groups, (pl.ds(0, half),),
        lambda g, t, full: full.at[span(g, half, 0, rows), lanes(t, cols)],
    )
    x_weights.moves += placed(
        gathered, of_half(1), groups, (pl.ds(0, half),),
        lambda g, t, full: full.at[span(g, half, half, rows), lanes(t, cols)],
    ).moves
    if packed:
        bc_weights = placed(
            gathered, of_half(0), groups, (pl.ds(half, 16), pl.ds(0, two_n)),
            lambda g, t, full: full.at[span(g * parts + t, 16, 0, share), :],
        )
        bc_weights.moves += placed(
            gathered, of_half(0), groups, (pl.ds(half, 16), pl.ds(two_n, two_n)),
            lambda g, t, full: full.at[span(g * parts + t, 16, 16, share), :],
        ).moves
        dt_weights = placed(
            gathered, of_half(1), groups, (pl.ds(half, 16), pl.ds(0, rows)),
            lambda g, t, full: full.at[span(t, 16), lanes(g, rows)],
        )
        bc_weights.arrays, dt_weights.arrays = [], []
    else:
        bc_weights = single(lax.all_gather(w_bc, "dp", axis=0, tiled=True))
        all_dt = lax.all_gather(lax.all_gather(w_dt, "dp", axis=0, tiled=True), "tensor", axis=0)
        all_dt = jnp.pad(all_dt.transpose(0, 2, 1), ((0, 0), (0, 16 - own_heads), (0, 0)))
        dt_weights = single(all_dt.reshape(parts * 16, width))

    wz, wz_labels = widened("x", wz_near, near_labels)
    for at, array in enumerate(wz_far):
        got, labels = widened("x", array, far_labels[at * near : (at + 1) * near])
        wz, wz_labels = wz + got, wz_labels + labels
    by_chip = [(wo, wo_labels), (hop("x", wo)[0], [dict(label, x=1) for label in wo_labels])]
    for k, got in enumerate(hop("y", wo)):
        by_chip.append((got, [dict(label, y=k + 1) for label in wo_labels]))
    for k in range(1, parts // 2):
        got = lax.ppermute(wo, ("dp", "tensor"), [
            (g * parts + t, (g ^ 1) * parts + (t + 2 * k) % parts) for g in range(groups) for t in range(parts)])
        by_chip.append((got, [dict(label, x=1, y=k) for label in wo_labels]))
    wo, wo_labels = [a for a, _ in by_chip], sum([lab for _, lab in by_chip], [])

    def block_place(g, t, full):
        return full.at[span(g, rows), lanes(t, cols)]

    def across_cores(arrays, labels, own_core=()):
        arrays = arrays + list(own_core) + [hop("c", a)[0] for a in arrays[len(own_core) :]]
        return placed(arrays, labels + [dict(label, c=1) for label in labels], groups, None, block_place)

    head_sum = (head_of[:, None] == jnp.arange(heads)[None, :]).astype(bf16)

    (x, w_full, bc_full, dt_full, vec, up, normed, low, slope, values, scanned, keys, prebc, scal, states) = call_scan(
        info, gain, down_in, convbc, spread_heads,
        dict(x=x_pieces, w=x_weights, bc=bc_weights, dt=dt_weights, vec=vec_pieces),
        parts, heads, length, width, inner,
    )

    cot_rows = swapped(tie(cotangent, gathered[0]))
    wz, wo, cot_rows, low = lax.optimization_barrier((wz, wo, cot_rows, low))
    cot_pieces = single(cot_rows.reshape(length, width))
    z_weights, o_weights = across_cores(wz, wz_labels), across_cores(wo, wo_labels, own_cores)
    out = call_gate(
        info, normed, low, scanned, x, vec, down_out, up_out,
        dict(z=z_weights, o=o_weights, cot=cot_pieces), groups, parts,
    )
    mixed, dlayer, dy, side, z_grad, low_back, up_z_part, out_down_part, z_full = out

    if mixed.ndim == 2:
        mixed = mixed.reshape(parts, groups, -1, width).transpose(1, 0, 2, 3)
    chunk = mixed.shape[2]
    came = swapped(mixed.reshape(groups * parts, chunk, width), ("dp", "tensor"))

    out = call_back(
        (x, normed, low, dlayer, dy, values, slope, keys, prebc, scal, states, scanned, side, z_grad, low_back),
        (w_full, z_full, bc_full, dt_full, vec, up, gain, down_in, convbc, spread_heads, head_sum)
        + (up_z_part, out_down_part), groups, parts, heads,
    )
    came, out = lax.optimization_barrier((came, out))
    token_rows, sums = out[0], out[1:]

    offsets = destination[:seq_grp] // seq_grp
    leave = call_turn(offsets, came.reshape(groups, parts, chunk, width))

    def second_leg(leave):
        return swapped(leave, "dp").transpose(1, 0, 2, 3).reshape(parts, part_len, width)

    token_rows = token_rows.reshape(parts, part_len, width)
    token_grad = exchanged([lax.dynamic_index_in_dim(token_rows, rank ^ k, 0, keepdims=False) for k in range(parts)])

    def stacked(blocks):
        result = jnp.zeros((parts,) + blocks[0].shape, blocks[0].dtype)
        for k, block in enumerate(blocks):
            result = lax.dynamic_update_index_in_dim(result, block, rank ^ k, 0)
        return result

    own = groups * parts
    if len(sums) > 1:

        def at_adapter(part):
            zeros = jnp.zeros((in_down.shape[1], part.shape[1]), bf16)
            return lax.dynamic_update_slice_in_dim(zeros, part.astype(bf16), adapter, 0)

        in_up_grad = [lax.psum_scatter(at_adapter(a), "tensor", scatter_dimension=1, tiled=True) for a in sums[:2]]
        in_up_grad = lax.psum(jnp.stack(in_up_grad, axis=1), "dp").astype(f32)
        others = [at_adapter(a) for a in (out_down_part, sums[2], sums[3])]
        out_down_grad, out_up_grad, in_down_grad = (a.astype(f32) for a in lax.psum(others, ("dp", "tensor")))
        return second_leg(leave), stacked(token_grad), in_down_grad.T, in_up_grad, out_down_grad, out_up_grad

    pooled = swapped(sums[0], ("dp", "tensor"))
    row_of = adapter_of[:, None] * RANK + jnp.arange(RANK)[None, :]
    select = (row_of.reshape(1, -1) == jnp.arange(in_down.shape[1])[:, None]).astype(bf16)
    sums = nn(select, pooled.reshape(own * RANK, -1)).astype(bf16)[None]
    sums, labels = widened("z", sums, [HERE])
    sums, leave = lax.optimization_barrier((sums, leave))
    mixed = second_leg(leave)
    sums, labels = widened("x", jnp.concatenate(sums), labels)
    sums = jnp.concatenate(sums)
    far_sums, far_labels = widened("y", sums[:, :, 2 * cols // groups :], labels)
    far_sums, token_grad = lax.optimization_barrier((jnp.concatenate(far_sums), token_grad))
    far_sums, far_labels = widened("c", far_sums, far_labels)
    in_up_grad, out_down_grad, out_up_grad, in_down_grad = call_arrange(
        info, sums, far_sums, labels, far_labels, groups, parts, inner, width, cols
    )
    in_up_grad = jnp.stack([in_up_grad[:, :cols], in_up_grad[:, cols:]], axis=1)
    return (mixed, stacked(token_grad), in_down_grad, in_up_grad, out_down_grad, out_up_grad)


def solution(mesh):
    return jax.shard_map(
        on_device,
        mesh=mesh,
        in_specs=(
            P("dp", "tensor", None), P("dp", "tensor", None), P(), P(), P(), P(),
            P("dp", None, "tensor"), P("dp", None), P("dp", "tensor"), P("dp", "tensor"),
            P(None, "tensor"), P(), P("tensor"), P("tensor"), P("tensor"), P("tensor"),
            P(), P(None, None, "tensor"), P(), P(),
        ),
        out_specs=(
            P("dp", "tensor", None), P("dp", "tensor", None), P(), P(None, None, "tensor"), P(), P(),
        ),
        check_vma=False,
    )
```
